256 devices in a mesh: store: 8 (over z), mp: 32 (over x, y, core).
Axes of the slice: x: 4, y: 4, z: 8, core: 2. Of those that a mesh axis runs over, the one named last changes fastest.
Arguments:
- kv_store: bfloat16 [128, 512, 2048], P('store', 'mp'), may hold values from -6 to 6
- retrieval: int32 [32, 8], replicated, may hold values from 0 to 127, as said below
- positions: int32 [32, 8], P('store'), may hold values from 0 to 7, each once within a row
- lengths: int32 [32], P('store'), may hold values from 1 to 128, 2048 in all
- queries: bfloat16 [32, 128, 8192], P('store', 'mp'), may hold values from -8 to 8
- new_kv: bfloat16 [32, 128, 2048], P('store', 'mp'), may hold values from -8 to 8
- hidden: bfloat16 [32, 128, 8192], P('store', 'mp'), may hold values from -4 to 4
- out_weight: bfloat16 [8192, 8192], P('mp'), may hold values from -0.0625 to 0.0625
- norm_gain: bfloat16 [8192], replicated, may hold values from 0.25 to 1.75
Outputs:
- residual_sum: bfloat16 [32, 128, 8192], P('store', 'mp')
- normed_out: bfloat16 [32, 128, 8192], P('store', 'mp')
The draws below stay inside these ranges and needn't reach their ends.
Inputs may be any that keep to these rules, and one draw needn't show every extreme that they name: `retrieval`: store group of stretch c is c // 16. Taking the rows in consecutive blocks of 4 requests, the 32 ids of a block are all distinct and lie in exactly 4 store groups, 8 ids in each. `positions`: each row is a permutation of 0 to 7. `lengths`: they sum to 2048, and the largest is 128.
All inputs are finite; a program needn't handle non-finite values. No bound on the sum of `lengths` on one device may be relied on, other than what follows from the above.
Results may differ from the reference program's by a relative error of at most 0.015.
The reference program's roundings to bfloat16 on the way count: a program that leaves them out, or rounds other values in their place, can miss the bound.
Values may be sent and summed in bfloat16 or wider, within the bound.
A program may use at most 128 MiB of HBM per device.

```python
import math
import jax
import jax.numpy as jnp
import numpy as np
from jax import lax

D = 8192
NH = 64
KVH = 8
HD = 128
CTOK = 512
R = 8
QMAX = 128
CH_DEV = 16
SLOTS = 32
CAP = 8
REQUESTS = 32
STRETCHES = 128
N_STORE = 8
N_MP = 32


def draw_retrieval(key, part):
    key = jax.random.fold_in(key, 17)
    start_key, order_key, local_key = jax.random.split(key, 3)
    starts = jax.random.randint(start_key, (N_STORE,), 0, N_STORE)
    orders = jax.vmap(lambda k: jax.random.permutation(k, SLOTS))(jax.random.split(order_key, N_STORE))
    local_table = jax.vmap(lambda k: jax.random.permutation(k, CH_DEV))(jax.random.split(local_key, N_STORE * N_STORE))
    local_table = local_table.reshape(N_STORE, N_STORE, CH_DEV)
    sources = (starts[:, None] + orders // CAP) % N_STORE
    slot_rank = orders % CAP
    dest_rows = jnp.arange(N_STORE, dtype=jnp.int32)[:, None] * jnp.ones_like(sources)
    chosen = local_table[dest_rows, sources, slot_rank]
    return (sources * CH_DEV + chosen).reshape(REQUESTS, R).astype(jnp.int32)


def draw_queries(key, part):
    key = jax.random.fold_in(key, 29)
    base = jnp.clip(jax.random.normal(key, (REQUESTS, QMAX, NH, HD), jnp.float32), -6.0, 6.0)
    return base.reshape(REQUESTS, QMAX, NH * HD).astype(jnp.bfloat16)


def draw_new_kv(key, part):
    key = jax.random.fold_in(key, 31)
    base = jnp.clip(jax.random.normal(key, (REQUESTS, QMAX, KVH, 2, HD), jnp.float32), -6.0, 6.0)
    return base.reshape(REQUESTS, QMAX, KVH * 2 * HD).astype(jnp.bfloat16)


def steps_of(key, extent, cuts, smallest, high):
    loudness, own = 1.0, jax.random.fold_in(key, 6)
    for dim, shards_of in cuts:
        heights = jnp.exp(jax.random.uniform(jax.random.fold_in(own, dim), (shards_of,), jnp.float32, smallest / len(cuts), high / len(cuts)))
        loudness = loudness * jnp.repeat(heights, extent[dim] // shards_of).reshape([-1 if axis == dim else 1 for axis in range(len(extent))])
    return loudness


def profile(amount, total, reach, lean):
    loads = [(1 << 20) // math.isqrt(grade ** lean) + 1 for grade in range(2, amount + 1)]
    rest, given = total - reach - (amount - 1), [1] * (amount - 1)
    while rest > 0:
        movable = [i for i in range(amount - 1) if given[i] < reach]
        pool, budget = sum([loads[i] for i in movable]), rest
        for i in movable:
            addition = min(reach - given[i], max(1, budget * loads[i] // pool), rest)
            given[i] = given[i] + addition
            rest = rest - addition
    return np.array([reach] + given)


def uneven_parts(stream_key, number_of, total, reach, skew):
    if number_of == 2:
        one = jax.random.randint(stream_key, (), max(1, total - reach), min(reach, total - 1) + 1)
        return jnp.stack([one, total - one])
    tallies = jnp.asarray(profile(number_of, total, reach, skew), jnp.int32)
    pairs = (number_of - 1) // 2
    source_of, receiver = tallies[1:1 + 2 * pairs:2], tallies[2:2 + 2 * pairs:2]
    margin = jnp.minimum(source_of - 1, reach - receiver)
    shifted = jax.random.randint(jax.random.fold_in(stream_key, 1), (pairs,), 0, 1 << 20) % (margin + 1)
    tallies = tallies.at[1:1 + 2 * pairs:2].set(source_of - shifted).at[2:2 + 2 * pairs:2].set(receiver + shifted)
    return tallies[jax.random.permutation(jax.random.fold_in(stream_key, 2), number_of)]


def noise(key, dims, spread, reach, shards=(), held_as=jnp.bfloat16):
    values = jax.random.normal(key, dims, jnp.float32) * spread
    if len(shards) > 0:
        values = steps_of(key, dims, shards, -0.22, 0.18) * values
    return jnp.clip(values, min=-reach, max=reach).astype(held_as)


def setup_inputs(seed: int = 0) -> dict:
    streams_of = jax.random.split(jax.random.key(seed), 10)
    return {
        "kv_store": noise(streams_of[0], (STRETCHES, CTOK, KVH * 2 * HD), 1.0, 6.0, ((0, 8), (1, 32))),
        "retrieval": draw_retrieval(jax.random.fold_in(streams_of[9], 71), 0),
        "positions": jax.vmap(lambda own: jax.random.permutation(own, R))(jax.random.split(streams_of[2], REQUESTS)).reshape((REQUESTS, R)).astype(jnp.int32),
        "lengths": uneven_parts(streams_of[3], REQUESTS, REQUESTS * QMAX // 2, QMAX, 2).astype(jnp.int32),
        "queries": draw_queries(jax.random.fold_in(streams_of[9], 71), 0),
        "new_kv": draw_new_kv(jax.random.fold_in(streams_of[9], 71), 0),
        "hidden": noise(streams_of[6], (REQUESTS, QMAX, D), 0.3, 4.0, ((0, 8), (1, 32))),
        "out_weight": noise(streams_of[7], (NH * HD, D), (NH * HD) ** -0.5, 0.0625, ((0, 32),)),
        "norm_gain": jnp.clip(1.0 + 0.15 * jax.random.normal(streams_of[8], (D,), jnp.float32), 0.25, 1.75).astype(jnp.bfloat16),
    }


theta_base = 1000000.0
eps_norm = 1e-06

def rotate(field_in, angles_at):
    half_dim = field_in.shape[-1] // 2
    inv_freq = theta_base ** (-(jnp.arange(half_dim, dtype=jnp.float32) * 2.0) / field_in.shape[-1])
    angles = angles_at[..., None] * inv_freq
    cosines = jnp.cos(angles)
    sine_val = jnp.sin(angles)
    lower_half = field_in[..., :half_dim]
    upper_half = field_in[..., half_dim:]
    return jnp.concatenate([lower_half * cosines - upper_half * sine_val, upper_half * cosines + lower_half * sine_val], axis=-1)

def reference(kv_store, retrieval, positions, lengths, queries, new_kv, hidden, out_weight, norm_gain):
    per_group = NH // KVH
    score_scale = HD ** (-0.5)
    context = R * CTOK
    token_index = jnp.arange(QMAX, dtype=jnp.int32)
    key_index = jnp.arange(context + QMAX, dtype=jnp.int32)
    allowed = (key_index[None, :] < context) | (key_index[None, :] - context <= token_index[:, None])
    places = (context + token_index).astype(jnp.float32)

    def one_request(request):
        stretch_ids, slot_pos, length, query_rows, fresh_kv = request
        stretches = kv_store[stretch_ids.astype(jnp.int32)].reshape(R, CTOK, KVH, 2, HD)
        offsets = (slot_pos * CTOK).astype(jnp.float32)
        stretch_keys = rotate(stretches[:, :, :, 0].astype(jnp.float32), offsets[:, None, None]).astype(jnp.bfloat16)
        stretch_keys = stretch_keys.reshape(context, KVH, HD)
        stretch_values = stretches[:, :, :, 1].reshape(context, KVH, HD)
        fresh_kv = fresh_kv.reshape(QMAX, KVH, 2, HD)
        own_keys = rotate(fresh_kv[:, :, 0].astype(jnp.float32), places[:, None]).astype(jnp.bfloat16)
        all_keys = jnp.concatenate([stretch_keys, own_keys], axis=0)
        values = jnp.concatenate([stretch_values, fresh_kv[:, :, 1]], axis=0)
        rotated = rotate(query_rows.reshape(QMAX, NH, HD).astype(jnp.float32), places[:, None]).astype(jnp.bfloat16)
        rotated = rotated.reshape(QMAX, KVH, per_group, HD)
        scores = jnp.einsum('tkgd,skd->kgts', rotated.astype(jnp.float32), all_keys.astype(jnp.float32)) * score_scale
        scores = jnp.where(allowed[None, None], scores, -1e+30)
        highest = lax.optimization_barrier(jnp.max(scores, axis=-1, keepdims=True))
        exponent = jnp.where(allowed[None, None], jnp.exp(scores - highest), 0.0)
        row_total = lax.optimization_barrier(jnp.sum(exponent, axis=-1, keepdims=True))
        weights = exponent.astype(jnp.bfloat16)
        blended = jnp.einsum('kgts,skd->kgtd', weights.astype(jnp.float32), values.astype(jnp.float32)) / row_total
        blended = jnp.transpose(blended, (2, 0, 1, 3)).reshape(QMAX, NH * HD)
        blended = jnp.where((token_index < length)[:, None], blended, 0.0)
        return blended.astype(jnp.bfloat16)
    attended = lax.map(one_request, (retrieval, positions, lengths, queries, new_kv))
    width = NH * HD // N_MP
    flat_attn = jnp.transpose(attended.reshape(REQUESTS * QMAX, N_MP, width), (1, 0, 2))
    weight_groups = out_weight.reshape(N_MP, width, D)

    def add_group(running, pair):
        partial_value = jnp.dot(pair[0], pair[1], preferred_element_type=jnp.float32).astype(jnp.bfloat16)
        return (running + partial_value.astype(jnp.float32), None)
    running, unused = lax.scan(add_group, jnp.zeros((REQUESTS * QMAX, D), jnp.float32), (flat_attn, weight_groups))
    mixed = hidden.reshape(REQUESTS * QMAX, D).astype(jnp.float32) + running
    residual_sum = mixed.astype(jnp.bfloat16)
    normed = mixed * lax.rsqrt(lax.optimization_barrier(jnp.mean(mixed * mixed, axis=-1, keepdims=True)) + eps_norm) * norm_gain.astype(jnp.float32)
    return (residual_sum.reshape(REQUESTS, QMAX, D), normed.astype(jnp.bfloat16).reshape(REQUESTS, QMAX, D))
```

```python
import jax
import jax.numpy as jnp
import numpy as np
from jax import lax
from jax.experimental import pallas as pl
from jax.experimental.pallas import tpu as pltpu
from jax.sharding import PartitionSpec as P

MESH = pl.DeviceIdType.MESH
ANY = pl.BlockSpec(memory_space=pl.ANY)
VMEM = pl.BlockSpec(memory_space=pltpu.VMEM)
SMEM = pl.BlockSpec(memory_space=pltpu.SMEM)

STORES = 8
SHARDS = 32
HEADS = 64
KVH = 8
GROUP = 8
HD = 128
D = 8192
QUARTERS = 4
CTOK = 512
R = 8
REQ = 4
QMAX = 128
HELD = 16
CHUNKS = 4
PER = HELD // CHUNKS
WIDTH = D // QUARTERS
ROWS = QMAX * GROUP
LANES = 256

theta_base = 1000000.0
eps_norm = 1e-06


def turns(places):
    inv_freq = theta_base ** (-(jnp.arange(HD // 2, dtype=jnp.float32) * 2.0) / HD)
    angles = places[..., None] * inv_freq
    cosines, sines = jnp.cos(angles), jnp.sin(angles)
    return (
        jnp.concatenate([cosines, cosines], axis=-1),
        jnp.concatenate([-sines, sines], axis=-1),
    )


def rotate(field_in, cosines, sines):
    half = HD // 2
    other = jnp.concatenate([field_in[..., half:], field_in[..., :half]], axis=-1)
    return field_in * cosines + other * sines


def ahead(a, b, n):
    return lax.rem(a + b, n)


def spread_kernel(
    kv, q, fresh, w, kv_all, q_all, fresh_all, w_all,
    own_sem, kv_send, kv_recv, q_send, q_recv, f_send, f_recv, w_send, w_recv, z_send, z_recv,
):
    m = lax.axis_index("mp")
    z = lax.axis_index("store")
    k = m // QUARTERS
    j = lax.rem(m, QUARTERS)
    right, left = ahead(z, 1, STORES), ahead(z, STORES - 1, STORES)

    barrier = pltpu.get_barrier_semaphore()

    def greet(i, carry):
        pl.semaphore_signal(barrier, 1, device_id={"mp": ahead(m, i, SHARDS)}, device_id_type=MESH)
        return carry

    lax.fori_loop(1, SHARDS, greet, 0)
    for near in (left, right):
        pl.semaphore_signal(barrier, 1, device_id={"store": near}, device_id_type=MESH)
    pl.semaphore_wait(barrier, SHARDS + 1)

    def remote(src, dst, send, recv, **where):
        return pltpu.make_async_remote_copy(
            src_ref=src, dst_ref=dst, send_sem=send, recv_sem=recv, device_id=where, device_id_type=MESH
        )

    def kv_rows(c, head):
        return kv_all.at[z, pl.ds(PER * c, PER), pl.ds(pl.multiple_of(16 * head, 16), 16), :]

    def kv_part(c, head):
        return kv.at[pl.ds(PER * c, PER), :, pl.ds(pl.multiple_of(2 * HD * head, 2 * HD), 2 * HD)]

    def kv_copy(c, i):
        to = ahead(k, i, KVH)
        return remote(
            kv_part(c, to), kv_rows(c, k), kv_send.at[c, i], kv_recv.at[c, k], mp=QUARTERS * to + j
        )

    def kv_arrival(c, i):
        come = ahead(k, i, KVH)
        return remote(
            kv_part(c, come), kv_rows(c, come), kv_send.at[c, i], kv_recv.at[c, come], mp=QUARTERS * come + j
        )

    def own_kv(c):
        return pltpu.make_async_copy(kv_part(c, k), kv_rows(c, k), own_sem.at[c])

    for c in range(CHUNKS):
        own_kv(c).start()

        def send_kv(i, carry):
            kv_copy(c, i).start()
            return carry

        lax.fori_loop(1, KVH, send_kv, 0)

    def z_copy(way, s, c):
        owner = ahead(z, (STORES - s) if way == 0 else s, STORES)
        slab = kv_all.at[owner, pl.ds(PER * c, PER)]
        return remote(
            slab, slab, z_send.at[way, s, c], z_recv.at[way, s, c], store=right if way == 0 else left
        )

    def z_arrival(way, s, c):
        owner = ahead(z, (STORES - 1 - s) if way == 0 else (s + 1), STORES)
        slab = kv_all.at[owner, pl.ds(PER * c, PER)]
        return remote(
            slab, slab, z_send.at[way, s, c], z_recv.at[way, s, c], store=right if way == 0 else left
        )

    for c in range(CHUNKS):
        own_kv(c).wait()

        def take_kv(i, carry):
            kv_arrival(c, i).wait_recv()
            return carry

        lax.fori_loop(1, KVH, take_kv, 0)
        for way in range(2):
            z_copy(way, 0, c).start()

    def fresh_part(head):
        return fresh.at[:, pl.ds(pl.multiple_of(2 * HD * head, 2 * HD), 2 * HD)]

    def f_copy(i):
        to = ahead(k, i, KVH)
        return remote(fresh_part(to), fresh_all.at[k], f_send.at[i], f_recv.at[k], mp=QUARTERS * to + j)

    def f_arrival(i):
        come = ahead(k, i, KVH)
        return remote(fresh_part(come), fresh_all.at[come], f_send.at[i], f_recv.at[come], mp=QUARTERS * come + j)

    def q_copy(i):
        to = ahead(m, i, SHARDS)
        return remote(q.at[to // QUARTERS], q_all.at[:, m], q_send.at[i], q_recv.at[m], mp=to)

    def q_arrival(i):
        come = ahead(m, i, SHARDS)
        return remote(q.at[k], q_all.at[:, come], q_send.at[i], q_recv.at[come], mp=come)

    def w_part(block):
        return w.at[:, pl.ds(pl.multiple_of(WIDTH * block, WIDTH), WIDTH)]

    def w_copy(i):
        to = ahead(j, i, QUARTERS)
        return remote(w_part(to), w_all.at[j], w_send.at[i], w_recv.at[j], mp=QUARTERS * k + to)

    def w_arrival(i):
        come = ahead(j, i, QUARTERS)
        return remote(w_part(come), w_all.at[come], w_send.at[i], w_recv.at[come], mp=QUARTERS * k + come)

    own = [
        pltpu.make_async_copy(fresh_part(k), fresh_all.at[k], own_sem.at[CHUNKS]),
        pltpu.make_async_copy(q.at[k], q_all.at[:, m], own_sem.at[CHUNKS + 1]),
        pltpu.make_async_copy(w_part(j), w_all.at[j], own_sem.at[CHUNKS + 2]),
    ]

    def loop(low, high, act):
        def body(i, carry):
            act(i)
            return carry

        lax.fori_loop(low, high, body, 0)

    for copy in own:
        copy.start()
    loop(1, QUARTERS, lambda i: w_copy(i).start())
    loop(1, KVH, lambda i: f_copy(i).start())
    loop(1, SHARDS, lambda i: q_copy(i).start())

    last = STORES // 2 - 1
    halves = (range(CHUNKS // 2), range(CHUNKS // 2, CHUNKS))
    for s in range(1, last + 1):
        for c in range(CHUNKS):
            for way in range(2):
                if s < last or c in halves[way]:
                    z_arrival(way, s - 1, c).wait_recv()
                    z_copy(way, s, c).start()
    for way in range(2):
        for c in range(CHUNKS):
            if c in halves[way]:
                z_arrival(way, last, c).wait_recv()
            else:
                z_arrival(way, last - 1, c).wait_recv()

    for copy in own:
        copy.wait()
    loop(1, QUARTERS, lambda i: w_arrival(i).wait_recv())
    loop(1, KVH, lambda i: f_arrival(i).wait_recv())
    loop(1, SHARDS, lambda i: q_arrival(i).wait_recv())
    loop(1, QUARTERS, lambda i: w_copy(i).wait_send())
    loop(1, KVH, lambda i: f_copy(i).wait_send())
    loop(1, SHARDS, lambda i: q_copy(i).wait_send())
    for c in range(CHUNKS):
        loop(1, KVH, lambda i: kv_copy(c, i).wait_send())
    for way in range(2):
        for s in range(last + 1):
            for c in range(CHUNKS):
                if s < last or c in halves[way]:
                    z_copy(way, s, c).wait_send()


def spread(kv, q, fresh, w):
    bf = jnp.bfloat16
    dma = pltpu.SemaphoreType.DMA
    return pl.pallas_call(
        spread_kernel,
        out_shape=(
            jax.ShapeDtypeStruct((STORES, HELD, CTOK // QUARTERS, 2 * HD), bf),
            jax.ShapeDtypeStruct((REQ, SHARDS, QMAX // SHARDS * GROUP, HD), bf),
            jax.ShapeDtypeStruct((KVH, 16, 2 * HD), bf),
            jax.ShapeDtypeStruct((QUARTERS, D // SHARDS, WIDTH), bf),
        ),
        in_specs=[ANY] * 4,
        out_specs=(ANY,) * 4,
        scratch_shapes=[
            dma((CHUNKS + 3,)),
            dma((CHUNKS, KVH)), dma((CHUNKS, KVH)),
            dma((SHARDS,)), dma((SHARDS,)),
            dma((KVH,)), dma((KVH,)),
            dma((QUARTERS,)), dma((QUARTERS,)),
            dma((2, STORES // 2, CHUNKS)), dma((2, STORES // 2, CHUNKS)),
        ],
        compiler_params=pltpu.CompilerParams(collective_id=0, has_side_effects=True),
        name="spread",
    )(kv, q, fresh, w)


def attend_kernel(
    ids, places, lengths, q, fresh, cosines, sines, kv_all, out, lse, slots, keys, values, sem
):
    quarter = CTOK // QUARTERS
    j = lax.rem(lax.axis_index("mp"), QUARTERS)

    def fetch(n):
        return pltpu.make_async_copy(kv_all.at[ids[n]], slots.at[n], sem.at[n])

    for n in range(REQ * R):
        fetch(n).start()
    keys[R * quarter :, :] = fresh[:, :HD]
    values[:, R * quarter :] = fresh[:, HD:].astype(jnp.float32).T.astype(jnp.bfloat16)
    row = lax.broadcasted_iota(jnp.int32, (quarter, LANES), 0)
    lane = lax.broadcasted_iota(jnp.int32, (quarter, LANES), 1)
    fresh_token = 4 * (QUARTERS * (row >> 4) + j) + (row & 3)
    fresh_request = (row >> 2) & 3
    for b in range(REQ):
        for r in range(R):
            n = b * R + r
            fetch(n).wait()
            key = slots[n, :, :HD].astype(jnp.float32)
            at = places[n]
            key = key * cosines[pl.ds(at, 1), :] + pltpu.roll(key, HD // 2, 1) * sines[pl.ds(at, 1), :]
            keys[r * quarter : (r + 1) * quarter, :] = key.astype(jnp.bfloat16)
            values[:, r * quarter : (r + 1) * quarter] = (
                slots[n, :, HD:].astype(jnp.float32).T.astype(jnp.bfloat16)
            )
        length = lengths[b]

        def block(i, carry):
            span = pl.ds(pl.multiple_of(i * LANES, LANES), LANES)

            @pl.when(i * LANES < length * GROUP)
            def _():
                scores = lax.dot_general(
                    keys[...], q[b, span, :], (((1,), (1,)), ((), ())), preferred_element_type=jnp.float32
                ) * (HD**-0.5)
                token = (i * LANES + lane) >> 3
                allowed = (fresh_request == b) & (fresh_token <= token)
                scores = jnp.concatenate(
                    [scores[: R * quarter], jnp.where(allowed, scores[R * quarter :], -1e30)], axis=0
                )
                top = jnp.max(scores, axis=0, keepdims=True)
                expo = jnp.exp(scores - top)
                total = jnp.sum(expo, axis=0, keepdims=True)
                sums = jnp.dot(
                    values[...], expo.astype(jnp.bfloat16), preferred_element_type=jnp.float32
                )
                used = (i * LANES + lane) < length * GROUP
                out[b, :, span] = jnp.where(used, sums / total, 0.0).astype(jnp.bfloat16)
                lse[b, :, span] = jnp.broadcast_to(top + jnp.log(total), (8, LANES))

            @pl.when(i * LANES >= length * GROUP)
            def _():
                out[b, :, span] = jnp.zeros((HD, LANES), jnp.bfloat16)
                lse[b, :, span] = jnp.zeros((8, LANES), jnp.float32)

            return carry

        lax.fori_loop(0, ROWS // LANES, block, 0)


def attend(ids, places, lengths, q, fresh, cosines, sines, kv_all):
    quarter = CTOK // QUARTERS
    return pl.pallas_call(
        attend_kernel,
        out_shape=(
            jax.ShapeDtypeStruct((REQ, HD, ROWS), jnp.bfloat16),
            jax.ShapeDtypeStruct((REQ, 8, ROWS), jnp.float32),
        ),
        in_specs=[SMEM] * 3 + [VMEM] * 4 + [ANY],
        out_specs=(VMEM, VMEM),
        scratch_shapes=[
            pltpu.VMEM((REQ * R, quarter, 2 * HD), jnp.bfloat16),
            pltpu.VMEM(((R + 1) * quarter, HD), jnp.bfloat16),
            pltpu.VMEM((HD, (R + 1) * quarter), jnp.bfloat16),
            pltpu.SemaphoreType.DMA((REQ * R,)),
        ],
        compiler_params=pltpu.CompilerParams(vmem_limit_bytes=32 << 20),
        name="attend",
    )(ids, places, lengths, q, fresh, cosines, sines, kv_all)


def merge_kernel(
    part, lse, w_hbm, hidden, gain, residual, normed,
    w, got_part, got_lse, rows, attended, sent, got, mixed,
    w_sem, own_sem, c_send, c_recv, l_send, l_recv, g_send, g_recv, p_send, p_recv,
):
    m = lax.axis_index("mp")
    k = m // QUARTERS
    j = lax.rem(m, QUARTERS)
    w_load = pltpu.make_async_copy(w_hbm, w, w_sem)
    w_load.start()

    barrier = pltpu.get_barrier_semaphore()

    def loop(low, high, act):
        def body(i, carry):
            act(i)
            return carry

        lax.fori_loop(low, high, body, 0)

    loop(
        1,
        SHARDS,
        lambda i: pl.semaphore_signal(
            barrier, 1, device_id={"mp": ahead(m, i, SHARDS)}, device_id_type=MESH
        ),
    )
    pl.semaphore_wait(barrier, SHARDS - 1)

    def remote(src, dst, send, recv, to):
        return pltpu.make_async_remote_copy(
            src_ref=src, dst_ref=dst, send_sem=send, recv_sem=recv, device_id={"mp": to}, device_id_type=MESH
        )

    def part_copy(i):
        to = ahead(j, i, QUARTERS)
        return remote(part.at[to], got_part.at[i], c_send.at[i], c_recv.at[i], QUARTERS * k + to)

    def lse_copy(i):
        to = ahead(j, i, QUARTERS)
        return remote(lse.at[to], got_lse.at[i], l_send.at[i], l_recv.at[i], QUARTERS * k + to)

    for i in range(1, QUARTERS):
        lse_copy(i).start()
        part_copy(i).start()
    for i in range(1, QUARTERS):
        lse_copy(i).wait_recv()
    logs = [lse[j, :1, :]] + [got_lse[i, :1, :] for i in range(1, QUARTERS)]
    top = jnp.maximum(jnp.maximum(logs[0], logs[1]), jnp.maximum(logs[2], logs[3]))
    shares = [jnp.exp(one - top) for one in logs]
    scale = 1.0 / (shares[0] + shares[1] + shares[2] + shares[3])
    total = part[j].astype(jnp.float32) * (shares[0] * scale)
    for i in range(1, QUARTERS):
        part_copy(i).wait_recv()
        total = total + got_part[i].astype(jnp.float32) * (shares[i] * scale)
    rows[...] = total.T
    for h in range(GROUP):
        attended[j, :, h * HD : (h + 1) * HD] = rows[pl.ds(h, QMAX, stride=GROUP), :].astype(jnp.bfloat16)

    def g_copy(i):
        to = ahead(j, i, QUARTERS)
        return remote(attended.at[j], attended.at[j], g_send.at[i], g_recv.at[j], QUARTERS * k + to)

    def g_arrival(i):
        come = ahead(j, i, QUARTERS)
        return remote(attended.at[come], attended.at[come], g_send.at[i], g_recv.at[come], QUARTERS * k + come)

    for i in range(1, QUARTERS):
        g_copy(i).start()
    w_load.wait()
    for i in range(1, QUARTERS):
        g_arrival(i).wait_recv()

    tokens = QMAX // SHARDS
    owned = REQ * tokens
    span = REQ * QMAX // 4
    per = span // owned

    def p_copy(to):
        return remote(
            sent.at[pl.ds(pl.multiple_of(owned * to, owned), owned), :], got.at[m], p_send.at[to], p_recv.at[m], to
        )

    def p_own():
        return pltpu.make_async_copy(
            sent.at[pl.ds(pl.multiple_of(owned * m, owned), owned), :], got.at[m], own_sem
        )

    def p_arrival(come):
        return remote(
            sent.at[pl.ds(pl.multiple_of(owned * come, owned), owned), :], got.at[come], p_send.at[come], p_recv.at[come], come
        )

    def project(i):
        block = ahead(m // per, i, 4)
        at = block * span + lax.broadcasted_iota(jnp.int32, (span, REQ * QMAX), 0)
        source = QMAX * ((at >> 2) & 3) + 4 * (at >> 4) + (at & 3)
        pick = (source == lax.broadcasted_iota(jnp.int32, (span, REQ * QMAX), 1)).astype(jnp.bfloat16)
        chosen = jnp.dot(
            pick, attended[...].reshape(REQ * QMAX, GROUP * HD), preferred_element_type=jnp.float32
        ).astype(jnp.bfloat16)
        sent[pl.ds(pl.multiple_of(block * span, span), span), :] = jnp.dot(
            chosen, w[...].reshape(GROUP * HD, WIDTH), preferred_element_type=jnp.float32
        ).astype(jnp.bfloat16)

        def ship(t):
            to = block * per + ahead(m, t, per)

            @pl.when(to != m)
            def _():
                p_copy(to).start()

            @pl.when(to == m)
            def _():
                p_own().start()

        loop(0, per, ship)

    loop(0, 4, project)
    p_own().wait()
    loop(1, SHARDS, lambda i: p_arrival(ahead(m, i, SHARDS)).wait_recv())

    square = jnp.zeros((owned, 1), jnp.float32)
    for c in range(QUARTERS):
        cols = slice(c * WIDTH, (c + 1) * WIDTH)
        value = hidden[:, cols].astype(jnp.float32)
        for head in range(KVH):
            value = value + got[QUARTERS * head + c].astype(jnp.float32)
        mixed[:, cols] = value
        residual[:, cols] = value.astype(jnp.bfloat16)
        square = square + jnp.sum(value * value, axis=-1, keepdims=True)
    factor = lax.rsqrt(square / D + eps_norm)
    normed[...] = (mixed[...] * factor * gain[...].astype(jnp.float32)).astype(jnp.bfloat16)

    for i in range(1, QUARTERS):
        part_copy(i).wait_send()
        lse_copy(i).wait_send()
        g_copy(i).wait_send()
    loop(1, SHARDS, lambda i: p_copy(ahead(m, i, SHARDS)).wait_send())


def merge(part, lse, w, hidden, gain):
    bf, f32 = jnp.bfloat16, jnp.float32
    dma = pltpu.SemaphoreType.DMA
    owned = REQ * QMAX // SHARDS
    return pl.pallas_call(
        merge_kernel,
        out_shape=(jax.ShapeDtypeStruct((owned, D), bf), jax.ShapeDtypeStruct((owned, D), bf)),
        in_specs=[VMEM, VMEM, ANY, VMEM, VMEM],
        out_specs=(VMEM, VMEM),
        scratch_shapes=[
            pltpu.VMEM((QUARTERS, D // SHARDS, WIDTH), bf),
            pltpu.VMEM((QUARTERS, HD, ROWS), bf),
            pltpu.VMEM((QUARTERS, 8, ROWS), f32),
            pltpu.VMEM((ROWS, HD), f32),
            pltpu.VMEM((REQ, QMAX, GROUP * HD), bf),
            pltpu.VMEM((REQ * QMAX, WIDTH), bf),
            pltpu.VMEM((SHARDS, owned, WIDTH), bf),
            pltpu.VMEM((owned, D), f32),
            dma, dma,
            dma((QUARTERS,)), dma((QUARTERS,)),
            dma((QUARTERS,)), dma((QUARTERS,)),
            dma((QUARTERS,)), dma((QUARTERS,)),
            dma((SHARDS,)), dma((SHARDS,)),
        ],
        compiler_params=pltpu.CompilerParams(
            collective_id=1, has_side_effects=True, vmem_limit_bytes=48 << 20
        ),
        name="merge",
    )(part, lse, w, hidden, gain)


def on_device(
    kv_store, retrieval, positions, lengths, queries, new_kv, hidden, out_weight, norm_gain
):
    z = lax.axis_index("store")
    m = lax.axis_index("mp")
    tokens = queries.shape[1]
    context = R * CTOK
    own_places = (context + m * tokens + jnp.arange(tokens, dtype=jnp.int32)).astype(jnp.float32)
    cos_own, sin_own = turns(own_places)
    q = rotate(
        queries.reshape(REQ, tokens, HEADS, HD).astype(jnp.float32),
        cos_own[None, :, None], sin_own[None, :, None],
    ).astype(jnp.bfloat16)
    q = jnp.transpose(q.reshape(REQ, tokens, KVH, GROUP, HD), (2, 0, 1, 3, 4))
    q = q.reshape(KVH, REQ, tokens * GROUP, HD)
    pair = new_kv.reshape(REQ, tokens, KVH, 2, HD)
    own_keys = rotate(
        pair[:, :, :, 0].astype(jnp.float32), cos_own[None, :, None], sin_own[None, :, None]
    ).astype(jnp.bfloat16)
    fresh = jnp.stack([own_keys, pair[:, :, :, 1]], axis=3).reshape(REQ * tokens, KVH * 2 * HD)

    kv_all, q_all, fresh_all, w_all = spread(kv_store, q, fresh, out_weight)

    ids = lax.dynamic_slice_in_dim(retrieval, z * REQ, REQ, 0).reshape(-1)
    cos_at, sin_at = turns((jnp.arange(R, dtype=jnp.int32) * CTOK).astype(jnp.float32))
    part, lse = attend(
        ids, positions.reshape(-1), lengths, q_all.reshape(REQ, ROWS, HD),
        fresh_all.reshape(KVH * 16, 2 * HD), cos_at, sin_at,
        kv_all.reshape(STORES * HELD, CTOK // QUARTERS, 2 * HD),
    )
    residual, normed = merge(part, lse, w_all, hidden.reshape(REQ * tokens, D), norm_gain.reshape(1, D))
    return residual.reshape(REQ, tokens, D), normed.reshape(REQ, tokens, D)


def solution(mesh):
    return jax.shard_map(
        on_device,
        mesh=mesh,
        in_specs=(
            P("store", "mp", None),
            P(),
            P("store", None),
            P("store"),
            P("store", "mp", None),
            P("store", "mp", None),
            P("store", "mp", None),
            P("mp", None),
            P(),
        ),
        out_specs=(P("store", "mp", None), P("store", "mp", None)),
        check_vma=False,
    )
```

```python
import jax
import jax.numpy as jnp
import numpy as np
from jax import lax
from jax.experimental import pallas as pl
from jax.experimental.pallas import tpu as pltpu
from jax.sharding import PartitionSpec as P

MESH = pl.DeviceIdType.MESH
HBM = pl.BlockSpec(memory_space=pltpu.HBM)
VMEM = pl.BlockSpec(memory_space=pltpu.VMEM)
SMEM = pl.BlockSpec(memory_space=pltpu.SMEM)

STORES = 8
SHARDS = 32
HEADS = 64
KVH = 8
GROUP = 8
HD = 128
D = 8192
QUARTERS = 4
CTOK = 512
R = 8
REQ = 4
QMAX = 128
HELD = 16
CHUNKS = 4
PER = HELD // CHUNKS
RING = 8
WIDTH = D // RING
ROWS = QMAX * GROUP
BLOCK = 512
TOKENS = QMAX // SHARDS
OWNED = REQ * TOKENS
LOG2E = 1.4426950408889634

theta_base = 1000000.0
eps_norm = 1e-06


def turns(places):
    inv_freq = np.float32(theta_base) ** (-(np.arange(HD // 2, dtype=np.float32) * np.float32(2.0)) / np.float32(HD))
    angles = np.asarray(places, np.float32)[..., None] * inv_freq
    cosines, sines = np.cos(angles), np.sin(angles)
    return (
        jnp.asarray(np.concatenate([cosines, cosines], axis=-1)),
        jnp.asarray(np.concatenate([-sines, sines], axis=-1)),
    )


def rotate(field_in, cosines, sines):
    return field_in * cosines + pltpu.roll(field_in, HD // 2, 1) * sines


def ahead(a, b, n):
    return lax.rem(a + b, n)


def spread_kernel(
    kv, queries, new_kv, cosines, sines, w, kv_all, q_all, fresh_all, w_all,
    q_wide, q, fresh_wide, fresh, own_sem, kv_send, kv_recv, q_send, q_recv, f_send, f_recv, w_send, w_recv, z_send, z_recv,
):
    m = lax.axis_index("mp")
    z = lax.axis_index("store")
    k = m // QUARTERS
    j = lax.rem(m, QUARTERS)
    right, left = ahead(z, 1, STORES), ahead(z, STORES - 1, STORES)

    barrier = pltpu.get_barrier_semaphore()

    def greet(i, carry):
        pl.semaphore_signal(barrier, 1, device_id={"mp": ahead(m, i, SHARDS)}, device_id_type=MESH)
        return carry

    lax.fori_loop(1, SHARDS, greet, 0)
    for near in (left, right):
        pl.semaphore_signal(barrier, 1, device_id={"store": near}, device_id_type=MESH)
    pl.semaphore_wait(barrier, SHARDS + 1)

    def remote(src, dst, send, recv, **where):
        return pltpu.make_async_remote_copy(
            src_ref=src, dst_ref=dst, send_sem=send, recv_sem=recv, device_id=where, device_id_type=MESH
        )

    def kv_rows(c, head):
        return kv_all.at[z, pl.ds(PER * c, PER), pl.ds(pl.multiple_of(16 * head, 16), 16), :]

    def kv_part(c, head):
        return kv.at[pl.ds(PER * c, PER), :, pl.ds(pl.multiple_of(2 * HD * head, 2 * HD), 2 * HD)]

    def kv_copy(c, i):
        to = ahead(k, i, KVH)
        return remote(
            kv_part(c, to), kv_rows(c, k), kv_send.at[c, i], kv_recv.at[c, k], mp=QUARTERS * to + j
        )

    def kv_arrival(c, i):
        come = ahead(k, i, KVH)
        return remote(
            kv_part(c, come), kv_rows(c, come), kv_send.at[c, i], kv_recv.at[c, come], mp=QUARTERS * come + j
        )

    def own_kv(c):
        return pltpu.make_async_copy(kv_part(c, k), kv_rows(c, k), own_sem.at[c])

    for c in range(CHUNKS):
        own_kv(c).start()

        def send_kv(i, carry):
            kv_copy(c, i).start()
            return carry

        lax.fori_loop(1, KVH, send_kv, 0)

    def z_copy(way, s, c):
        owner = ahead(z, (STORES - s) if way == 0 else s, STORES)
        slab = kv_all.at[owner, pl.ds(PER * c, PER)]
        return remote(
            slab, slab, z_send.at[way, s, c], z_recv.at[way, s, c], store=right if way == 0 else left
        )

    def z_arrival(way, s, c):
        owner = ahead(z, (STORES - 1 - s) if way == 0 else (s + 1), STORES)
        slab = kv_all.at[owner, pl.ds(PER * c, PER)]
        return remote(
            slab, slab, z_send.at[way, s, c], z_recv.at[way, s, c], store=right if way == 0 else left
        )

    for c in range(CHUNKS):
        own_kv(c).wait()

        def take_kv(i, carry):
            kv_arrival(c, i).wait_recv()
            return carry

        lax.fori_loop(1, KVH, take_kv, 0)
        for way in range(2):
            z_copy(way, 0, c).start()

    def fresh_part(head):
        return fresh.at[:, pl.ds(pl.multiple_of(2 * HD * head, 2 * HD), 2 * HD)]

    def f_copy(i):
        to = ahead(k, i, KVH)
        return remote(fresh_part(to), fresh_all.at[k], f_send.at[i], f_recv.at[k], mp=QUARTERS * to + j)

    def f_arrival(i):
        come = ahead(k, i, KVH)
        return remote(fresh_part(come), fresh_all.at[come], f_send.at[i], f_recv.at[come], mp=QUARTERS * come + j)

    def q_copy(i):
        to = ahead(m, i, SHARDS)
        return remote(q.at[to // QUARTERS], q_all.at[:, m], q_send.at[i], q_recv.at[m], mp=to)

    def q_arrival(i):
        come = ahead(m, i, SHARDS)
        return remote(q.at[k], q_all.at[:, come], q_send.at[i], q_recv.at[come], mp=come)

    ring = RING * (m // RING)
    place = lax.rem(m, RING)

    def w_part(block):
        return w.at[:, pl.ds(pl.multiple_of(WIDTH * block, WIDTH), WIDTH)]

    def w_copy(i):
        to = ahead(place, i, RING)
        return remote(w_part(to), w_all.at[place], w_send.at[i], w_recv.at[place], mp=ring + to)

    def w_arrival(i):
        come = ahead(place, i, RING)
        return remote(w_part(come), w_all.at[come], w_send.at[i], w_recv.at[come], mp=ring + come)

    own = [
        pltpu.make_async_copy(fresh_part(k), fresh_all.at[k], own_sem.at[CHUNKS]),
        pltpu.make_async_copy(q.at[k], q_all.at[:, m], own_sem.at[CHUNKS + 1]),
    ]

    def loop(low, high, act):
        def body(i, carry):
            act(i)
            return carry

        lax.fori_loop(low, high, body, 0)

    loop(1, RING, lambda i: w_copy(i).start())

    cos, sin = cosines[m], sines[m]

    def turn(head):
        for b in range(REQ):
            for g in range(GROUP):
                at = pl.ds(pl.multiple_of((head * GROUP + g) * HD, HD), HD)
                value = rotate(queries[b, :, at].astype(jnp.float32), cos, sin)
                q_wide[head, b, pl.ds(g, TOKENS, stride=GROUP), :] = value
            at = pl.multiple_of(2 * HD * head, 2 * HD)
            key = rotate(new_kv[b, :, pl.ds(at, HD)].astype(jnp.float32), cos, sin)
            fresh_wide[b * TOKENS : (b + 1) * TOKENS, pl.ds(at, HD)] = key
            at = pl.multiple_of(at + HD, HD)
            fresh_wide[b * TOKENS : (b + 1) * TOKENS, pl.ds(at, HD)] = new_kv[b, :, pl.ds(at, HD)].astype(jnp.float32)
        q[head] = q_wide[head].astype(jnp.bfloat16)

    loop(0, KVH, turn)
    fresh[...] = fresh_wide[...].astype(jnp.bfloat16)
    for copy in own:
        copy.start()
    loop(1, KVH, lambda i: f_copy(i).start())
    loop(1, SHARDS, lambda i: q_copy(i).start())

    last = STORES // 2 - 1
    halves = (range(CHUNKS // 2), range(CHUNKS // 2, CHUNKS))
    for s in range(1, last + 1):
        for c in range(CHUNKS):
            for way in range(2):
                if s < last or c in halves[way]:
                    z_arrival(way, s - 1, c).wait_recv()
                    z_copy(way, s, c).start()
    for way in range(2):
        for c in range(CHUNKS):
            if c in halves[way]:
                z_arrival(way, last, c).wait_recv()
            else:
                z_arrival(way, last - 1, c).wait_recv()

    for copy in own:
        copy.wait()
    loop(1, RING, lambda i: w_arrival(i).wait_recv())
    loop(1, KVH, lambda i: f_arrival(i).wait_recv())
    loop(1, SHARDS, lambda i: q_arrival(i).wait_recv())
    loop(1, RING, lambda i: w_copy(i).wait_send())
    loop(1, KVH, lambda i: f_copy(i).wait_send())
    loop(1, SHARDS, lambda i: q_copy(i).wait_send())
    for c in range(CHUNKS):
        loop(1, KVH, lambda i: kv_copy(c, i).wait_send())
    for way in range(2):
        for s in range(last + 1):
            for c in range(CHUNKS):
                if s < last or c in halves[way]:
                    z_copy(way, s, c).wait_send()


def spread(kv, queries, new_kv, cosines, sines, w):
    bf, f32 = jnp.bfloat16, jnp.float32
    dma = pltpu.SemaphoreType.DMA
    return pl.pallas_call(
        spread_kernel,
        out_shape=(
            jax.ShapeDtypeStruct((STORES, HELD, CTOK // QUARTERS, 2 * HD), bf),
            jax.ShapeDtypeStruct((REQ, SHARDS, QMAX // SHARDS * GROUP, HD), bf),
            jax.ShapeDtypeStruct((KVH, 16, 2 * HD), bf),
            jax.ShapeDtypeStruct((RING, D // SHARDS, WIDTH), bf),
        ),
        in_specs=[HBM] + [VMEM] * 4 + [HBM],
        out_specs=(HBM,) * 4,
        scratch_shapes=[
            pltpu.VMEM((KVH, REQ, TOKENS * GROUP, HD), f32),
            pltpu.VMEM((KVH, REQ, TOKENS * GROUP, HD), bf),
            pltpu.VMEM((OWNED, KVH * 2 * HD), f32),
            pltpu.VMEM((OWNED, KVH * 2 * HD), bf),
            dma((CHUNKS + 2,)),
            dma((CHUNKS, KVH)), dma((CHUNKS, KVH)),
            dma((SHARDS,)), dma((SHARDS,)),
            dma((KVH,)), dma((KVH,)),
            dma((RING,)), dma((RING,)),
            dma((2, STORES // 2, CHUNKS)), dma((2, STORES // 2, CHUNKS)),
        ],
        compiler_params=pltpu.CompilerParams(
            collective_id=0, has_side_effects=True, vmem_limit_bytes=60 << 20
        ),
        name="spread",
    )(kv, queries, new_kv, cosines, sines, w)


def attend_kernel(
    retrieval, places, lengths, cosines, sines, q_all, fresh_all, kv_all, out, lse,
    slots, keys, q, fresh, sem, q_sem, fresh_sem,
):
    quarter = CTOK // QUARTERS
    held = R * quarter
    j = lax.rem(lax.axis_index("mp"), QUARTERS)
    z = lax.axis_index("store")

    def fetch(b, r):
        return pltpu.make_async_copy(
            kv_all.at[retrieval[z * REQ + b, r]], slots.at[b, pl.ds(r * quarter, quarter)], sem.at[b, r]
        )

    def fetch_q(b):
        return pltpu.make_async_copy(q_all.at[b], q.at[b], q_sem.at[b])

    fetch_fresh = pltpu.make_async_copy(fresh_all, fresh, fresh_sem)
    for b in range(REQ):
        for r in range(R):
            fetch(b, r).start()
        fetch_q(b).start()
        if b == 0:
            fetch_fresh.start()
    fetch_fresh.wait()
    for b in range(REQ):
        slots[b, held:, :] = fresh[...]
    keys[held:, :] = fresh[:, :HD]
    col = lax.broadcasted_iota(jnp.int32, (BLOCK, quarter), 1)
    fresh_token = TOKENS * (QUARTERS * (col >> 4) + j) + (col & 3)
    fresh_request = (col >> 2) & 3
    row = lax.broadcasted_iota(jnp.int32, (BLOCK, quarter), 0)
    for b in range(REQ):
        for r in range(R):
            fetch(b, r).wait()
        for r in range(R):
            at = places[b, r]
            key = slots[b, r * quarter : (r + 1) * quarter, :HD].astype(jnp.float32)
            key = rotate(key, cosines[pl.ds(at, 1), :], sines[pl.ds(at, 1), :])
            keys[r * quarter : (r + 1) * quarter, :] = key.astype(jnp.bfloat16)
        fetch_q(b).wait()
        length = lengths[b]

        def block(i, carry):
            span = pl.ds(pl.multiple_of(i * BLOCK, BLOCK), BLOCK)
            scores = lax.dot_general(
                q[b, span, :], keys[...], (((1,), (1,)), ((), ())), preferred_element_type=jnp.float32
            ) * (HD**-0.5 * LOG2E)
            allowed = (fresh_request == b) & (fresh_token <= ((i * BLOCK + row) >> 3))
            fresh_scores = jnp.where(allowed, scores[:, held:], -1e30)
            scores = scores[:, :held]
            top = jnp.maximum(
                jnp.max(scores, axis=1, keepdims=True), jnp.max(fresh_scores, axis=1, keepdims=True)
            )
            expo, fresh_expo = jnp.exp2(scores - top), jnp.exp2(fresh_scores - top)
            total = jnp.sum(expo, axis=1, keepdims=True) + jnp.sum(fresh_expo, axis=1, keepdims=True)
            sums = jnp.dot(
                expo.astype(jnp.bfloat16), slots[b, :held, HD:], preferred_element_type=jnp.float32
            ) + jnp.dot(
                fresh_expo.astype(jnp.bfloat16), slots[b, held:, HD:], preferred_element_type=jnp.float32
            )
            out[b, span, :] = jnp.where(i * BLOCK + row < length * GROUP, sums / total, 0.0).astype(jnp.bfloat16)
            logs = top + jnp.log(total) * LOG2E
            lse[b, :, span] = jnp.broadcast_to(logs, (BLOCK, HD)).T[:8]
            return carry

        def blank(i, carry):
            span = pl.ds(pl.multiple_of(i * BLOCK, BLOCK), BLOCK)
            out[b, span, :] = jnp.zeros((BLOCK, HD), jnp.bfloat16)
            lse[b, :, span] = jnp.zeros((8, BLOCK), jnp.float32)
            return carry

        used = (length * GROUP + BLOCK - 1) // BLOCK
        lax.fori_loop(0, used, block, 0)
        lax.fori_loop(used, ROWS // BLOCK, blank, 0)


def attend(retrieval, places, lengths, cosines, sines, q_all, fresh_all, kv_all):
    quarter = CTOK // QUARTERS
    bf = jnp.bfloat16
    dma = pltpu.SemaphoreType.DMA
    return pl.pallas_call(
        attend_kernel,
        out_shape=(
            jax.ShapeDtypeStruct((REQ, ROWS, HD), bf),
            jax.ShapeDtypeStruct((REQ, 8, ROWS), jnp.float32),
        ),
        in_specs=[SMEM] * 3 + [VMEM] * 2 + [HBM] * 3,
        out_specs=(VMEM, VMEM),
        scratch_shapes=[
            pltpu.VMEM((REQ, (R + 1) * quarter, 2 * HD), bf),
            pltpu.VMEM(((R + 1) * quarter, HD), bf),
            pltpu.VMEM((REQ, ROWS, HD), bf),
            pltpu.VMEM((quarter, 2 * HD), bf),
            dma((REQ, R)), dma((REQ,)), dma,
        ],
        compiler_params=pltpu.CompilerParams(vmem_limit_bytes=60 << 20),
        name="attend",
    )(retrieval, places, lengths, cosines, sines, q_all, fresh_all, kv_all)


def merge_kernel(
    part, lse, w_own, w_all, hidden, gain, residual, normed,
    w, from_mate, from_mate_lse, pair, pair_lse, from_chip, from_chip_lse, rows, attended, sent, got, mixed,
    w_sem, own_sem, c_send, c_recv, l_send, l_recv, g_send, g_recv, p_send, p_recv,
):
    m = lax.axis_index("mp")
    k = m // QUARTERS
    j = lax.rem(m, QUARTERS)
    core, half = lax.rem(j, 2), j // 2
    mate, chip = m + 1 - 2 * core, QUARTERS * k + ahead(j, 2, QUARTERS)
    ring = RING * (m // RING)
    place = lax.rem(m, RING)
    w_loads = [
        pltpu.make_async_copy(
            w_own.at[:, pl.ds(pl.multiple_of(WIDTH * place, WIDTH), WIDTH)], w.at[place], w_sem.at[0]
        )
    ]
    for i in range(1, RING):
        come = ahead(place, i, RING)
        w_loads.append(pltpu.make_async_copy(w_all.at[come], w.at[come], w_sem.at[i]))
    for load in w_loads:
        load.start()

    barrier = pltpu.get_barrier_semaphore()

    def loop(low, high, act):
        def body(i, carry):
            act(i)
            return carry

        lax.fori_loop(low, high, body, 0)

    loop(
        1,
        SHARDS,
        lambda i: pl.semaphore_signal(
            barrier, 1, device_id={"mp": ahead(m, i, SHARDS)}, device_id_type=MESH
        ),
    )
    pl.semaphore_wait(barrier, SHARDS - 1)

    def remote(src, dst, send, recv, to):
        return pltpu.make_async_remote_copy(
            src_ref=src, dst_ref=dst, send_sem=send, recv_sem=recv, device_id={"mp": to}, device_id_type=MESH
        )

    def mate_copies(at, n):
        give = 1 - core + 2 * at
        return (
            remote(lse.at[give], from_mate_lse.at[at], l_send.at[n], l_recv.at[n], mate),
            remote(part.at[give], from_mate.at[at], c_send.at[n], c_recv.at[n], mate),
        )

    def combine(one, one_log, two, two_log):
        top = jnp.maximum(one_log, two_log)
        one_share, two_share = jnp.exp2(one_log - top), jnp.exp2(two_log - top)
        total = one_share + two_share
        share = jnp.broadcast_to(one_share / total, (HD, ROWS)).T
        return two + (one - two) * share, top + jnp.log(total) * LOG2E

    def wide(ref, at):
        return ref[at].astype(jnp.float32)

    pair_copies = (
        remote(pair_lse, from_chip_lse, l_send.at[2], l_recv.at[2], chip),
        remote(pair, from_chip, c_send.at[2], c_recv.at[2], chip),
    )
    other = 1 - half
    order = ((other, 0), (half, 1))
    for at, n in order:
        for copy in mate_copies(at, n):
            copy.start()
    for copy in mate_copies(other, 0):
        copy.wait_recv()
    give = core + 2 * other
    value, logs = combine(
        wide(part, give), lse[give, :1, :], wide(from_mate, other), from_mate_lse[other, :1, :]
    )
    pair[...] = value.astype(jnp.bfloat16)
    pair_lse[...] = jnp.broadcast_to(logs, (8, ROWS))
    for copy in pair_copies:
        copy.start()
    for copy in mate_copies(half, 1):
        copy.wait_recv()
    value, logs = combine(
        wide(part, j), lse[j, :1, :], wide(from_mate, half), from_mate_lse[half, :1, :]
    )
    rows[...] = value
    for copy in pair_copies:
        copy.wait_recv()
    value, logs = combine(rows[...], logs, from_chip[...].astype(jnp.float32), from_chip_lse[:1, :])
    rows[...] = value
    for h in range(GROUP):
        attended[place, :, h * HD : (h + 1) * HD] = rows[pl.ds(h, QMAX, stride=GROUP), :].astype(jnp.bfloat16)

    def g_copy(at, n, to):
        return remote(attended.at[at], attended.at[at], g_send.at[n], g_recv.at[n], to)

    hops = (2, 6, 4)
    mate_place = place + 1 - 2 * core
    g_copy(place, 0, mate).start()
    for n, hop in enumerate(hops):
        g_copy(place, 1 + n, ring + ahead(place, hop, RING)).start()
    for load in w_loads:
        load.wait()
    for n, hop in enumerate(hops):
        come = ahead(place, RING - hop, RING)
        g_copy(come, 1 + n, mate).wait_recv()
        g_copy(come, 4 + n, mate).start()
    g_copy(mate_place, 0, mate).wait_recv()
    for n, hop in enumerate(hops):
        g_copy(ahead(mate_place, RING - hop, RING), 4 + n, mate).wait_recv()

    owned = OWNED
    span = REQ * QMAX // 4
    per = span // owned

    def p_copy(to):
        return remote(
            sent.at[pl.ds(pl.multiple_of(owned * to, owned), owned), :], got.at[m], p_send.at[to], p_recv.at[m], to
        )

    def p_own():
        return pltpu.make_async_copy(
            sent.at[pl.ds(pl.multiple_of(owned * m, owned), owned), :], got.at[m], own_sem
        )

    def p_arrival(come):
        return remote(
            sent.at[pl.ds(pl.multiple_of(owned * come, owned), owned), :], got.at[come], p_send.at[come], p_recv.at[come], come
        )

    def project(i):
        block = ahead(m // per, i, 4)
        at = block * span + lax.broadcasted_iota(jnp.int32, (span, REQ * QMAX), 0)
        source = QMAX * ((at >> 2) & 3) + 4 * (at >> 4) + (at & 3)
        pick = (source == lax.broadcasted_iota(jnp.int32, (span, REQ * QMAX), 1)).astype(jnp.bfloat16)
        total = None
        for g in range(RING // REQ):
            chosen = jnp.dot(
                pick,
                attended[REQ * g : REQ * (g + 1)].reshape(REQ * QMAX, GROUP * HD),
                preferred_element_type=jnp.float32,
            ).astype(jnp.bfloat16)
            term = jnp.dot(
                chosen,
                w[REQ * g : REQ * (g + 1)].reshape(GROUP * HD, WIDTH),
                preferred_element_type=jnp.float32,
            )
            total = term if total is None else total + term
        sent[pl.ds(pl.multiple_of(block * span, span), span), :] = total.astype(jnp.bfloat16)

        def ship(t):
            to = block * per + ahead(m, t, per)

            @pl.when(to != m)
            def _():
                p_copy(to).start()

            @pl.when(to == m)
            def _():
                p_own().start()

        loop(0, per, ship)

    loop(0, 4, project)
    p_own().wait()
    loop(1, SHARDS, lambda i: p_arrival(ahead(m, i, SHARDS)).wait_recv())

    square = jnp.zeros((owned, 1), jnp.float32)
    for c in range(RING):
        cols = slice(c * WIDTH, (c + 1) * WIDTH)
        value = jnp.concatenate([hidden[b, :, cols].astype(jnp.float32) for b in range(REQ)], axis=0)
        for group in range(SHARDS // RING):
            value = value + got[RING * group + c].astype(jnp.float32)
        mixed[:, cols] = value
        square = square + jnp.sum(value * value, axis=-1, keepdims=True)
    factor = lax.rsqrt(square / D + eps_norm)
    for b in range(REQ):
        mine = slice(b * TOKENS, (b + 1) * TOKENS)
        residual[b] = mixed[mine, :].astype(jnp.bfloat16)
        normed[b] = (mixed[mine, :] * factor[mine] * gain[...].astype(jnp.float32)).astype(jnp.bfloat16)

    for at, n in order:
        for copy in mate_copies(at, n):
            copy.wait_send()
    for copy in pair_copies:
        copy.wait_send()
    g_copy(place, 0, mate).wait_send()
    for n, hop in enumerate(hops):
        g_copy(place, 1 + n, mate).wait_send()
        g_copy(ahead(place, RING - hop, RING), 4 + n, mate).wait_send()
    loop(1, SHARDS, lambda i: p_copy(ahead(m, i, SHARDS)).wait_send())


def merge(part, lse, w_own, w_all, hidden, gain):
    bf, f32 = jnp.bfloat16, jnp.float32
    dma = pltpu.SemaphoreType.DMA
    owned = OWNED
    return pl.pallas_call(
        merge_kernel,
        out_shape=(jax.ShapeDtypeStruct((REQ, TOKENS, D), bf),) * 2,
        in_specs=[VMEM, VMEM, HBM, HBM, VMEM, VMEM],
        out_specs=(VMEM, VMEM),
        scratch_shapes=[
            pltpu.VMEM((RING, D // SHARDS, WIDTH), bf),
            pltpu.VMEM((2, ROWS, HD), bf),
            pltpu.VMEM((2, 8, ROWS), f32),
            pltpu.VMEM((ROWS, HD), bf),
            pltpu.VMEM((8, ROWS), f32),
            pltpu.VMEM((ROWS, HD), bf),
            pltpu.VMEM((8, ROWS), f32),
            pltpu.VMEM((ROWS, HD), f32),
            pltpu.VMEM((RING, QMAX, GROUP * HD), bf),
            pltpu.VMEM((REQ * QMAX, WIDTH), bf),
            pltpu.VMEM((SHARDS, owned, WIDTH), bf),
            pltpu.VMEM((owned, D), f32),
            dma((RING,)), dma,
            dma((3,)), dma((3,)),
            dma((3,)), dma((3,)),
            dma((7,)), dma((7,)),
            dma((SHARDS,)), dma((SHARDS,)),
        ],
        compiler_params=pltpu.CompilerParams(
            collective_id=1, has_side_effects=True, vmem_limit_bytes=60 << 20
        ),
        name="merge",
    )(part, lse, w_own, w_all, hidden, gain)


def on_device(
    kv_store, retrieval, positions, lengths, queries, new_kv, hidden, out_weight, norm_gain
):
    context = R * CTOK
    cos_own, sin_own = turns(np.arange(context, context + QMAX))
    shape = (SHARDS, TOKENS, HD)
    kv_all, q_all, fresh_all, w_all = spread(
        kv_store, queries, new_kv, cos_own.reshape(shape), sin_own.reshape(shape), out_weight
    )
    cos_at, sin_at = turns(np.arange(R) * CTOK)
    part, lse = attend(
        retrieval, positions, lengths, cos_at, sin_at, q_all.reshape(REQ, ROWS, HD),
        fresh_all.reshape(KVH * 16, 2 * HD),
        kv_all.reshape(STORES * HELD, CTOK // QUARTERS, 2 * HD),
    )
    return merge(part, lse, out_weight, w_all, hidden, norm_gain.reshape(1, D))


def solution(mesh):
    return jax.shard_map(
        on_device,
        mesh=mesh,
        in_specs=(
            P("store", "mp", None),
            P(),
            P("store", None),
            P("store"),
            P("store", "mp", None),
            P("store", "mp", None),
            P("store", "mp", None),
            P("mp", None),
            P(),
        ),
        out_specs=(P("store", "mp", None), P("store", "mp", None)),
        check_vma=False,
    )
```

```python
import jax
import jax.numpy as jnp
import numpy as np
from jax import lax
from jax.experimental import pallas as pl
from jax.experimental.pallas import tpu as pltpu
from jax.sharding import PartitionSpec as P

MESH = pl.DeviceIdType.MESH
HBM = pl.BlockSpec(memory_space=pltpu.HBM)
VMEM = pl.BlockSpec(memory_space=pltpu.VMEM)
SMEM = pl.BlockSpec(memory_space=pltpu.SMEM)

STORES = 8
SHARDS = 32
HEADS = 64
KVH = 8
GROUP = 8
HD = 128
D = 8192
QUARTERS = 4
CTOK = 512
R = 8
REQ = 4
QMAX = 128
HELD = 16
CHUNKS = 4
PART = CTOK // 4 // CHUNKS
CAP = 8
PLACES = 5 * HELD + 3 * CAP
RING = 8
WIDTH = D // RING
ROWS = QMAX * GROUP
BLOCK = 512
TOKENS = QMAX // SHARDS
OWNED = REQ * TOKENS
LOG2E = 1.4426950408889634

theta_base = 1000000.0
eps_norm = 1e-06


def turns(places):
    inv_freq = np.float32(theta_base) ** (-(np.arange(HD // 2, dtype=np.float32) * np.float32(2.0)) / np.float32(HD))
    angles = np.asarray(places, np.float32)[..., None] * inv_freq
    cosines, sines = np.cos(angles), np.sin(angles)
    return (
        jnp.asarray(np.concatenate([cosines, cosines], axis=-1)),
        jnp.asarray(np.concatenate([-sines, sines], axis=-1)),
    )


def rotate(field_in, cosines, sines):
    return field_in * cosines + pltpu.roll(field_in, HD // 2, 1) * sines


def ahead(a, b, n):
    return lax.rem(a + b, n)


def spread_kernel(
    retrieval, kv, queries, new_kv, cosines, sines, w, kv_all, q_all, fresh_all, w_all,
    q_wide, q, fresh_wide, fresh, near, packed, packed_far, relay, near_sem, own_sem, kv_send, kv_recv, q_send, q_recv, f_send, f_recv, w_send, w_recv, z_send, z_recv,
):
    m = lax.axis_index("mp")
    z = lax.axis_index("store")
    k = m // QUARTERS
    j = lax.rem(m, QUARTERS)
    right, left = ahead(z, 1, STORES), ahead(z, STORES - 1, STORES)

    barrier = pltpu.get_barrier_semaphore()

    def greet(i, carry):
        pl.semaphore_signal(barrier, 1, device_id={"mp": ahead(m, i, SHARDS)}, device_id_type=MESH)
        return carry

    lax.fori_loop(1, SHARDS, greet, 0)
    for beside in (left, right):
        pl.semaphore_signal(barrier, 1, device_id={"store": beside}, device_id_type=MESH)
    pl.semaphore_wait(barrier, SHARDS + 1)

    def remote(src, dst, send, recv, **where):
        return pltpu.make_async_remote_copy(
            src_ref=src, dst_ref=dst, send_sem=send, recv_sem=recv, device_id=where, device_id_type=MESH
        )

    def kv_rows(i):
        return kv_all.at[pl.ds(0, HELD), pl.ds(16 * i, 16), :]

    def kv_part(head):
        return kv.at[:, :, pl.ds(pl.multiple_of(2 * HD * head, 2 * HD), 2 * HD)]

    def kv_copy(i):
        to = ahead(k, KVH - i, KVH)
        return remote(kv_part(to), kv_rows(i), kv_send.at[i], kv_recv.at[i], mp=QUARTERS * to + j)

    own_kv = pltpu.make_async_copy(kv_part(k), kv_rows(0), own_sem.at[2])
    own_kv.start()
    for i in range(1, KVH):
        kv_copy(i).start()

    target = (right, left)

    def rows_of(c):
        return pl.ds(PART * c, PART)

    def held(base, count, c):
        return kv_all.at[pl.ds(base, count), rows_of(c)]

    def z_copy(way, s, c):
        if s == 0:
            src, dst = held(0, HELD, c), held(HELD * (1 + way), HELD, c)
        elif s == 1:
            src, dst = held(HELD * (1 + way), HELD, c), near[way * CHUNKS + c]
        elif s == 2:
            src, dst = packed.at[way, c], held(5 * HELD + CAP * way, CAP, c)
        elif s == 3:
            src, dst = packed_far.at[way, c % 2], relay.at[way, c % 2]
        else:
            src, dst = relay.at[way, c % 2], held(5 * HELD + 2 * CAP, CAP, c)
        return remote(src, dst, z_send.at[way, s, c], z_recv.at[way, s, c], store=target[way])

    for c in range(CHUNKS):
        if c == 0:
            own_kv.wait()
        else:
            kv_copy(2 * c).wait_recv()
        kv_copy(2 * c + 1).wait_recv()
        for way in range(2):
            z_copy(way, 0, c).start()

    def fresh_part(head):
        return fresh.at[:, pl.ds(pl.multiple_of(2 * HD * head, 2 * HD), 2 * HD)]

    def f_copy(i):
        to = ahead(k, i, KVH)
        return remote(fresh_part(to), fresh_all.at[k], f_send.at[i], f_recv.at[k], mp=QUARTERS * to + j)

    def f_arrival(i):
        come = ahead(k, i, KVH)
        return remote(fresh_part(come), fresh_all.at[come], f_send.at[i], f_recv.at[come], mp=QUARTERS * come + j)

    def q_copy(i):
        to = ahead(m, i, SHARDS)
        return remote(q.at[to // QUARTERS], q_all.at[:, m], q_send.at[i], q_recv.at[m], mp=to)

    def q_arrival(i):
        come = ahead(m, i, SHARDS)
        return remote(q.at[k], q_all.at[:, come], q_send.at[i], q_recv.at[come], mp=come)

    ring = RING * (m // RING)
    place = lax.rem(m, RING)

    def w_part(block):
        return w.at[:, pl.ds(pl.multiple_of(WIDTH * block, WIDTH), WIDTH)]

    def w_copy(i):
        to = ahead(place, i, RING)
        return remote(w_part(to), w_all.at[place], w_send.at[i], w_recv.at[place], mp=ring + to)

    def w_arrival(i):
        come = ahead(place, i, RING)
        return remote(w_part(come), w_all.at[come], w_send.at[i], w_recv.at[come], mp=ring + come)

    own = [
        pltpu.make_async_copy(fresh_part(k), fresh_all.at[k], own_sem.at[0]),
        pltpu.make_async_copy(q.at[k], q_all.at[:, m], own_sem.at[1]),
    ]

    def loop(low, high, act):
        def body(i, carry):
            act(i)
            return carry

        lax.fori_loop(low, high, body, 0)

    loop(1, RING, lambda i: w_copy(i).start())

    cos, sin = cosines[m], sines[m]

    def turn(head):
        for b in range(REQ):
            for g in range(GROUP):
                at = pl.ds(pl.multiple_of((head * GROUP + g) * HD, HD), HD)
                value = rotate(queries[b, :, at].astype(jnp.float32), cos, sin)
                q_wide[head, b, pl.ds(g, TOKENS, stride=GROUP), :] = value
            at = pl.multiple_of(2 * HD * head, 2 * HD)
            key = rotate(new_kv[b, :, pl.ds(at, HD)].astype(jnp.float32), cos, sin)
            fresh_wide[b * TOKENS : (b + 1) * TOKENS, pl.ds(at, HD)] = key
            at = pl.multiple_of(at + HD, HD)
            fresh_wide[b * TOKENS : (b + 1) * TOKENS, pl.ds(at, HD)] = new_kv[b, :, pl.ds(at, HD)].astype(jnp.float32)
        q[head] = q_wide[head].astype(jnp.bfloat16)

    loop(0, KVH, turn)
    fresh[...] = fresh_wide[...].astype(jnp.bfloat16)
    for copy in own:
        copy.start()
    loop(1, KVH, lambda i: f_copy(i).start())
    loop(1, SHARDS, lambda i: q_copy(i).start())

    def wanted(dest, source):
        def look(n, carry):
            count, picks = carry
            found = retrieval[lax.rem(n, R), dest * REQ + n // R]
            hit = (found >> 4) == source
            picks = tuple(
                jnp.where(hit & (count == at), found & (HELD - 1), pick) for at, pick in enumerate(picks)
            )
            return jnp.where(hit, count + 1, count), picks

        zero = jnp.int32(0)
        return lax.fori_loop(0, REQ * R, look, (zero, (zero,) * CAP))[1]

    picks = [wanted(ahead(z, 1, STORES), ahead(z, 6, STORES)), wanted(ahead(z, 7, STORES), ahead(z, 2, STORES))]
    far_picks = [wanted(ahead(z, 2, STORES), ahead(z, 6, STORES)), wanted(ahead(z, 6, STORES), ahead(z, 2, STORES))]

    halves = (range(CHUNKS // 2), range(CHUNKS // 2, CHUNKS))
    for c in range(CHUNKS):
        for way in range(2):
            z_copy(way, 0, c).wait_recv()
            z_copy(way, 1, c).start()

    def keep(way, c):
        return pltpu.make_async_copy(
            near[way * CHUNKS + c], held(HELD * (3 + way), HELD, c), near_sem.at[way, c]
        )

    for c in range(CHUNKS):
        for way in range(2):
            z_copy(way, 1, c).wait_recv()
            source = near[way * CHUNKS + c]
            for at in range(CAP):
                packed[way, c, at] = source[picks[way][at]]
            z_copy(way, 2, c).start()
            if c in halves[way]:
                for at in range(CAP):
                    packed_far[way, c % 2, at] = source[far_picks[way][at]]
                z_copy(way, 3, c).start()
            keep(way, c).start()
    for n in range(CHUNKS // 2):
        for way in range(2):
            z_copy(way, 3, halves[way][n]).wait_recv()
            z_copy(way, 4, halves[way][n]).start()
    for c in range(CHUNKS):
        for way in range(2):
            keep(way, c).wait()
            z_copy(way, 2, c).wait_recv()
            if c in halves[way]:
                z_copy(way, 4, c).wait_recv()

    for copy in own:
        copy.wait()
    loop(1, RING, lambda i: w_arrival(i).wait_recv())
    loop(1, KVH, lambda i: f_arrival(i).wait_recv())
    loop(1, SHARDS, lambda i: q_arrival(i).wait_recv())
    loop(1, RING, lambda i: w_copy(i).wait_send())
    loop(1, KVH, lambda i: f_copy(i).wait_send())
    loop(1, SHARDS, lambda i: q_copy(i).wait_send())
    for i in range(1, KVH):
        kv_copy(i).wait_send()
    for way in range(2):
        for c in range(CHUNKS):
            for s in (0, 1, 2):
                z_copy(way, s, c).wait_send()
            if c in halves[way]:
                for s in (3, 4):
                    z_copy(way, s, c).wait_send()


def spread(retrieval, kv, queries, new_kv, cosines, sines, w):
    bf, f32 = jnp.bfloat16, jnp.float32
    dma = pltpu.SemaphoreType.DMA
    return pl.pallas_call(
        spread_kernel,
        out_shape=(
            jax.ShapeDtypeStruct((PLACES, CTOK // QUARTERS, 2 * HD), bf),
            jax.ShapeDtypeStruct((REQ, SHARDS, QMAX // SHARDS * GROUP, HD), bf),
            jax.ShapeDtypeStruct((KVH, 16, 2 * HD), bf),
            jax.ShapeDtypeStruct((RING, D // SHARDS, WIDTH), bf),
        ),
        in_specs=[SMEM, HBM] + [VMEM] * 4 + [HBM],
        out_specs=(HBM,) * 4,
        scratch_shapes=[
            pltpu.VMEM((KVH, REQ, TOKENS * GROUP, HD), f32),
            pltpu.VMEM((KVH, REQ, TOKENS * GROUP, HD), bf),
            pltpu.VMEM((OWNED, KVH * 2 * HD), f32),
            pltpu.VMEM((OWNED, KVH * 2 * HD), bf),
            [pltpu.VMEM((HELD, PART, 2 * HD), bf)] * (2 * CHUNKS),
            pltpu.VMEM((2, CHUNKS, CAP, PART, 2 * HD), bf),
            pltpu.VMEM((2, CHUNKS // 2, CAP, PART, 2 * HD), bf),
            pltpu.VMEM((2, CHUNKS // 2, CAP, PART, 2 * HD), bf),
            dma((2, CHUNKS)),
            dma((3,)),
            dma((KVH,)), dma((KVH,)),
            dma((SHARDS,)), dma((SHARDS,)),
            dma((KVH,)), dma((KVH,)),
            dma((RING,)), dma((RING,)),
            dma((2, 5, CHUNKS)), dma((2, 5, CHUNKS)),
        ],
        compiler_params=pltpu.CompilerParams(
            collective_id=0, has_side_effects=True, vmem_limit_bytes=60 << 20
        ),
        name="spread",
    )(retrieval, kv, queries, new_kv, cosines, sines, w)


def attend_kernel(
    retrieval, places, lengths, cosines, sines, q_all, fresh_all, kv_all, out, lse,
    slots, keys, q, fresh, counts, sem, q_sem, fresh_sem,
):
    quarter = CTOK // QUARTERS
    held = R * quarter
    j = lax.rem(lax.axis_index("mp"), QUARTERS)
    z = lax.axis_index("store")

    def fetch(b, r, place=0):
        return pltpu.make_async_copy(
            kv_all.at[place], slots.at[b, pl.ds(r * quarter, quarter)], sem.at[b, r]
        )

    for s in range(STORES):
        counts[s] = 0

    def locate(b, r):
        found = retrieval[r, z * REQ + b]
        apart = ((found >> 4) - z) & (STORES - 1)
        rank = counts[apart]
        counts[apart] = rank + 1
        near = HELD * jnp.where(apart <= 2, 2 * apart, 2 * (STORES - apart) - 1) + (found & (HELD - 1))
        far = 5 * HELD + CAP * jnp.where(apart == 5, 0, jnp.where(apart == 3, 1, 2)) + rank
        return jnp.where((apart <= 2) | (apart >= 6), near, far)

    def fetch_q(b):
        return pltpu.make_async_copy(q_all.at[b], q.at[b], q_sem.at[b])

    fetch_fresh = pltpu.make_async_copy(fresh_all, fresh, fresh_sem)
    for b in range(REQ):
        for r in range(R):
            fetch(b, r, locate(b, r)).start()
        fetch_q(b).start()
        if b == 0:
            fetch_fresh.start()
    fetch_fresh.wait()
    for b in range(REQ):
        slots[b, held:, :] = fresh[...]
    keys[held:, :] = fresh[:, :HD]
    col = lax.broadcasted_iota(jnp.int32, (BLOCK, quarter), 1)
    fresh_token = TOKENS * (QUARTERS * (col >> 4) + j) + (col & 3)
    fresh_request = (col >> 2) & 3
    row = lax.broadcasted_iota(jnp.int32, (BLOCK, quarter), 0)
    for b in range(REQ):
        for r in range(R):
            fetch(b, r).wait()
        for r in range(R):
            at = places[b, r]
            key = slots[b, r * quarter : (r + 1) * quarter, :HD].astype(jnp.float32)
            key = rotate(key, cosines[pl.ds(at, 1), :], sines[pl.ds(at, 1), :])
            keys[r * quarter : (r + 1) * quarter, :] = key.astype(jnp.bfloat16)
        fetch_q(b).wait()
        length = lengths[b]

        def block(i, carry):
            span = pl.ds(pl.multiple_of(i * BLOCK, BLOCK), BLOCK)
            scores = lax.dot_general(
                q[b, span, :], keys[...], (((1,), (1,)), ((), ())), preferred_element_type=jnp.float32
            ) * (HD**-0.5 * LOG2E)
            allowed = (fresh_request == b) & (fresh_token <= ((i * BLOCK + row) >> 3))
            fresh_scores = jnp.where(allowed, scores[:, held:], -1e30)
            scores = scores[:, :held]
            top = jnp.maximum(
                jnp.max(scores, axis=1, keepdims=True), jnp.max(fresh_scores, axis=1, keepdims=True)
            )
            expo, fresh_expo = jnp.exp2(scores - top), jnp.exp2(fresh_scores - top)
            total = jnp.sum(expo, axis=1, keepdims=True) + jnp.sum(fresh_expo, axis=1, keepdims=True)
            sums = jnp.dot(
                expo.astype(jnp.bfloat16), slots[b, :held, HD:], preferred_element_type=jnp.float32
            ) + jnp.dot(
                fresh_expo.astype(jnp.bfloat16), slots[b, held:, HD:], preferred_element_type=jnp.float32
            )
            out[b, span, :] = jnp.where(i * BLOCK + row < length * GROUP, sums / total, 0.0).astype(jnp.bfloat16)
            logs = top + jnp.log(total) * LOG2E
            lse[b, :, span] = jnp.broadcast_to(logs, (BLOCK, HD)).T[:8]
            return carry

        def blank(i, carry):
            span = pl.ds(pl.multiple_of(i * BLOCK, BLOCK), BLOCK)
            out[b, span, :] = jnp.zeros((BLOCK, HD), jnp.bfloat16)
            lse[b, :, span] = jnp.zeros((8, BLOCK), jnp.float32)
            return carry

        used = (length * GROUP + BLOCK - 1) // BLOCK
        lax.fori_loop(0, used, block, 0)
        lax.fori_loop(used, ROWS // BLOCK, blank, 0)


def attend(retrieval, places, lengths, cosines, sines, q_all, fresh_all, kv_all):
    quarter = CTOK // QUARTERS
    bf = jnp.bfloat16
    dma = pltpu.SemaphoreType.DMA
    return pl.pallas_call(
        attend_kernel,
        out_shape=(
            jax.ShapeDtypeStruct((REQ, ROWS, HD), bf),
            jax.ShapeDtypeStruct((REQ, 8, ROWS), jnp.float32),
        ),
        in_specs=[SMEM] * 3 + [VMEM] * 2 + [HBM] * 3,
        out_specs=(VMEM, VMEM),
        scratch_shapes=[
            pltpu.VMEM((REQ, (R + 1) * quarter, 2 * HD), bf),
            pltpu.VMEM(((R + 1) * quarter, HD), bf),
            pltpu.VMEM((REQ, ROWS, HD), bf),
            pltpu.VMEM((quarter, 2 * HD), bf),
            pltpu.SMEM((STORES,), jnp.int32),
            dma((REQ, R)), dma((REQ,)), dma,
        ],
        compiler_params=pltpu.CompilerParams(vmem_limit_bytes=60 << 20),
        name="attend",
    )(retrieval, places, lengths, cosines, sines, q_all, fresh_all, kv_all)


def merge_kernel(
    part, lse, w_own, w_all, hidden, gain, residual, normed,
    w, from_mate, from_mate_lse, pair, pair_lse, from_chip, from_chip_lse, rows, attended, sent, got, mixed,
    w_sem, own_sem, c_send, c_recv, l_send, l_recv, g_send, g_recv, p_send, p_recv,
):
    m = lax.axis_index("mp")
    k = m // QUARTERS
    j = lax.rem(m, QUARTERS)
    core, half = lax.rem(j, 2), j // 2
    mate, chip = m + 1 - 2 * core, QUARTERS * k + ahead(j, 2, QUARTERS)
    ring = RING * (m // RING)
    place = lax.rem(m, RING)
    w_loads = [
        pltpu.make_async_copy(
            w_own.at[:, pl.ds(pl.multiple_of(WIDTH * place, WIDTH), WIDTH)], w.at[place], w_sem.at[0]
        )
    ]
    for i in range(1, RING):
        come = ahead(place, i, RING)
        w_loads.append(pltpu.make_async_copy(w_all.at[come], w.at[come], w_sem.at[i]))
    for load in w_loads:
        load.start()

    barrier = pltpu.get_barrier_semaphore()

    def loop(low, high, act):
        def body(i, carry):
            act(i)
            return carry

        lax.fori_loop(low, high, body, 0)

    loop(
        1,
        SHARDS,
        lambda i: pl.semaphore_signal(
            barrier, 1, device_id={"mp": ahead(m, i, SHARDS)}, device_id_type=MESH
        ),
    )
    pl.semaphore_wait(barrier, SHARDS - 1)

    def remote(src, dst, send, recv, to):
        return pltpu.make_async_remote_copy(
            src_ref=src, dst_ref=dst, send_sem=send, recv_sem=recv, device_id={"mp": to}, device_id_type=MESH
        )

    def mate_copies(at, n):
        give = 1 - core + 2 * at
        return (
            remote(lse.at[give], from_mate_lse.at[at], l_send.at[n], l_recv.at[n], mate),
            remote(part.at[give], from_mate.at[at], c_send.at[n], c_recv.at[n], mate),
        )

    def combine(one, one_log, two, two_log):
        top = jnp.maximum(one_log, two_log)
        one_share, two_share = jnp.exp2(one_log - top), jnp.exp2(two_log - top)
        total = one_share + two_share
        share = jnp.broadcast_to(one_share / total, (HD, ROWS)).T
        return two + (one - two) * share, top + jnp.log(total) * LOG2E

    def wide(ref, at):
        return ref[at].astype(jnp.float32)

    pair_copies = (
        remote(pair_lse, from_chip_lse, l_send.at[2], l_recv.at[2], chip),
        remote(pair, from_chip, c_send.at[2], c_recv.at[2], chip),
    )
    other = 1 - half
    order = ((other, 0), (half, 1))
    for at, n in order:
        for copy in mate_copies(at, n):
            copy.start()
    for copy in mate_copies(other, 0):
        copy.wait_recv()
    give = core + 2 * other
    value, logs = combine(
        wide(part, give), lse[give, :1, :], wide(from_mate, other), from_mate_lse[other, :1, :]
    )
    pair[...] = value.astype(jnp.bfloat16)
    pair_lse[...] = jnp.broadcast_to(logs, (8, ROWS))
    for copy in pair_copies:
        copy.start()
    for copy in mate_copies(half, 1):
        copy.wait_recv()
    value, logs = combine(
        wide(part, j), lse[j, :1, :], wide(from_mate, half), from_mate_lse[half, :1, :]
    )
    rows[...] = value
    for copy in pair_copies:
        copy.wait_recv()
    value, logs = combine(rows[...], logs, from_chip[...].astype(jnp.float32), from_chip_lse[:1, :])
    rows[...] = value
    for h in range(GROUP):
        attended[place, :, h * HD : (h + 1) * HD] = rows[pl.ds(h, QMAX, stride=GROUP), :].astype(jnp.bfloat16)

    def g_copy(at, n, to):
        return remote(attended.at[at], attended.at[at], g_send.at[n], g_recv.at[n], to)

    hops = (2, 6, 4)
    mate_place = place + 1 - 2 * core
    g_copy(place, 0, mate).start()
    for n, hop in enumerate(hops):
        g_copy(place, 1 + n, ring + ahead(place, hop, RING)).start()
    for load in w_loads:
        load.wait()
    for n, hop in enumerate(hops):
        come = ahead(place, RING - hop, RING)
        g_copy(come, 1 + n, mate).wait_recv()
        g_copy(come, 4 + n, mate).start()
    g_copy(mate_place, 0, mate).wait_recv()
    for n, hop in enumerate(hops):
        g_copy(ahead(mate_place, RING - hop, RING), 4 + n, mate).wait_recv()

    owned = OWNED
    span = REQ * QMAX // 4
    per = span // owned

    def p_copy(to):
        return remote(
            sent.at[pl.ds(pl.multiple_of(owned * to, owned), owned), :], got.at[m], p_send.at[to], p_recv.at[m], to
        )

    def p_own():
        return pltpu.make_async_copy(
            sent.at[pl.ds(pl.multiple_of(owned * m, owned), owned), :], got.at[m], own_sem
        )

    def p_arrival(come):
        return remote(
            sent.at[pl.ds(pl.multiple_of(owned * come, owned), owned), :], got.at[come], p_send.at[come], p_recv.at[come], come
        )

    def project(i):
        block = ahead(m // per, i, 4)
        at = block * span + lax.broadcasted_iota(jnp.int32, (span, REQ * QMAX), 0)
        source = QMAX * ((at >> 2) & 3) + 4 * (at >> 4) + (at & 3)
        pick = (source == lax.broadcasted_iota(jnp.int32, (span, REQ * QMAX), 1)).astype(jnp.bfloat16)
        total = None
        for g in range(RING // REQ):
            chosen = jnp.dot(
                pick,
                attended[REQ * g : REQ * (g + 1)].reshape(REQ * QMAX, GROUP * HD),
                preferred_element_type=jnp.float32,
            ).astype(jnp.bfloat16)
            term = jnp.dot(
                chosen,
                w[REQ * g : REQ * (g + 1)].reshape(GROUP * HD, WIDTH),
                preferred_element_type=jnp.float32,
            )
            total = term if total is None else total + term
        sent[pl.ds(pl.multiple_of(block * span, span), span), :] = total.astype(jnp.bfloat16)

        def ship(t):
            to = block * per + ahead(m, t, per)

            @pl.when(to != m)
            def _():
                p_copy(to).start()

            @pl.when(to == m)
            def _():
                p_own().start()

        loop(0, per, ship)

    loop(0, 4, project)
    p_own().wait()
    loop(1, SHARDS, lambda i: p_arrival(ahead(m, i, SHARDS)).wait_recv())

    square = jnp.zeros((owned, 1), jnp.float32)
    for c in range(RING):
        cols = slice(c * WIDTH, (c + 1) * WIDTH)
        value = jnp.concatenate([hidden[b, :, cols].astype(jnp.float32) for b in range(REQ)], axis=0)
        for group in range(SHARDS // RING):
            value = value + got[RING * group + c].astype(jnp.float32)
        mixed[:, cols] = value
        square = square + jnp.sum(value * value, axis=-1, keepdims=True)
    factor = lax.rsqrt(square / D + eps_norm)
    for b in range(REQ):
        mine = slice(b * TOKENS, (b + 1) * TOKENS)
        residual[b] = mixed[mine, :].astype(jnp.bfloat16)
        normed[b] = (mixed[mine, :] * factor[mine] * gain[...].astype(jnp.float32)).astype(jnp.bfloat16)

    for at, n in order:
        for copy in mate_copies(at, n):
            copy.wait_send()
    for copy in pair_copies:
        copy.wait_send()
    g_copy(place, 0, mate).wait_send()
    for n, hop in enumerate(hops):
        g_copy(place, 1 + n, mate).wait_send()
        g_copy(ahead(place, RING - hop, RING), 4 + n, mate).wait_send()
    loop(1, SHARDS, lambda i: p_copy(ahead(m, i, SHARDS)).wait_send())


def merge(part, lse, w_own, w_all, hidden, gain):
    bf, f32 = jnp.bfloat16, jnp.float32
    dma = pltpu.SemaphoreType.DMA
    owned = OWNED
    return pl.pallas_call(
        merge_kernel,
        out_shape=(jax.ShapeDtypeStruct((REQ, TOKENS, D), bf),) * 2,
        in_specs=[VMEM, VMEM, HBM, HBM, VMEM, VMEM],
        out_specs=(VMEM, VMEM),
        scratch_shapes=[
            pltpu.VMEM((RING, D // SHARDS, WIDTH), bf),
            pltpu.VMEM((2, ROWS, HD), bf),
            pltpu.VMEM((2, 8, ROWS), f32),
            pltpu.VMEM((ROWS, HD), bf),
            pltpu.VMEM((8, ROWS), f32),
            pltpu.VMEM((ROWS, HD), bf),
            pltpu.VMEM((8, ROWS), f32),
            pltpu.VMEM((ROWS, HD), f32),
            pltpu.VMEM((RING, QMAX, GROUP * HD), bf),
            pltpu.VMEM((REQ * QMAX, WIDTH), bf),
            pltpu.VMEM((SHARDS, owned, WIDTH), bf),
            pltpu.VMEM((owned, D), f32),
            dma((RING,)), dma,
            dma((3,)), dma((3,)),
            dma((3,)), dma((3,)),
            dma((7,)), dma((7,)),
            dma((SHARDS,)), dma((SHARDS,)),
        ],
        compiler_params=pltpu.CompilerParams(
            collective_id=1, has_side_effects=True, vmem_limit_bytes=60 << 20
        ),
        name="merge",
    )(part, lse, w_own, w_all, hidden, gain)


def on_device(
    kv_store, retrieval, positions, lengths, queries, new_kv, hidden, out_weight, norm_gain
):
    context = R * CTOK
    cos_own, sin_own = turns(np.arange(context, context + QMAX))
    shape = (SHARDS, TOKENS, HD)
    wanted = jnp.transpose(retrieval)
    kv_all, q_all, fresh_all, w_all = spread(
        wanted, kv_store, queries, new_kv, cos_own.reshape(shape), sin_own.reshape(shape), out_weight
    )
    cos_at, sin_at = turns(np.arange(R) * CTOK)
    part, lse = attend(
        wanted, positions, lengths, cos_at, sin_at, q_all.reshape(REQ, ROWS, HD),
        fresh_all.reshape(KVH * 16, 2 * HD),
        kv_all,
    )
    return merge(part, lse, out_weight, w_all, hidden, norm_gain.reshape(1, D))


def solution(mesh):
    return jax.shard_map(
        on_device,
        mesh=mesh,
        in_specs=(
            P("store", "mp", None),
            P(),
            P("store", None),
            P("store"),
            P("store", "mp", None),
            P("store", "mp", None),
            P("store", "mp", None),
            P("mp", None),
            P(),
        ),
        out_specs=(P("store", "mp", None), P("store", "mp", None)),
        check_vma=False,
    )
```

```python
import jax
import jax.numpy as jnp
import numpy as np
from jax import lax
from jax.experimental import pallas as pl
from jax.experimental.pallas import tpu as pltpu
from jax.sharding import PartitionSpec as P

MESH = pl.DeviceIdType.MESH
HBM = pl.BlockSpec(memory_space=pltpu.HBM)
VMEM = pl.BlockSpec(memory_space=pltpu.VMEM)
SMEM = pl.BlockSpec(memory_space=pltpu.SMEM)

STORES = 8
SHARDS = 32
HEADS = 64
KVH = 8
GROUP = 8
HD = 128
D = 8192
QUARTERS = 4
CTOK = 512
R = 8
REQ = 4
QMAX = 128
HELD = 16
CHUNKS = 4
PART = CTOK // 4 // CHUNKS
CAP = 8
WINDOW = 4
EARLY = 3
PLACES = 5 * HELD + 3 * CAP
RING = 8
WIDTH = D // RING
ROWS = QMAX * GROUP
BLOCK = 512
SUB = 256
TOKENS = QMAX // SHARDS
OWNED = REQ * TOKENS
LOG2E = 1.4426950408889634

theta_base = 1000000.0
eps_norm = 1e-06


def turns(places):
    inv_freq = np.float32(theta_base) ** (-(np.arange(HD // 2, dtype=np.float32) * np.float32(2.0)) / np.float32(HD))
    angles = np.asarray(places, np.float32)[..., None] * inv_freq
    cosines, sines = np.cos(angles), np.sin(angles)
    return (
        jnp.asarray(np.concatenate([cosines, cosines], axis=-1)),
        jnp.asarray(np.concatenate([-sines, sines], axis=-1)),
    )


def rotate(field_in, cosines, sines):
    return field_in * cosines + pltpu.roll(field_in, HD // 2, 1) * sines


def ahead(a, b, n):
    return lax.rem(a + b, n)


def spread_kernel(
    retrieval, kv, queries, new_kv, cosines, sines, w, kv_all, q_all, fresh_all, w_all,
    q_wide, q, fresh_wide, fresh, near, packed, packed_far, relay, near_sem, own_sem, kv_send, kv_recv, q_send, q_recv, f_send, f_recv, w_send, w_recv, o_send, o_recv, z_send, z_recv,
):
    m = lax.axis_index("mp")
    z = lax.axis_index("store")
    k = m // QUARTERS
    j = lax.rem(m, QUARTERS)
    right, left = ahead(z, 1, STORES), ahead(z, STORES - 1, STORES)

    barrier = pltpu.get_barrier_semaphore()

    def greet(i, carry):
        pl.semaphore_signal(barrier, 1, device_id={"mp": ahead(m, i, SHARDS)}, device_id_type=MESH)
        return carry

    lax.fori_loop(1, SHARDS, greet, 0)
    for beside in (left, right):
        pl.semaphore_signal(barrier, 1, device_id={"store": beside}, device_id_type=MESH)
    pl.semaphore_wait(barrier, SHARDS + 1)

    def remote(src, dst, send, recv, **where):
        return pltpu.make_async_remote_copy(
            src_ref=src, dst_ref=dst, send_sem=send, recv_sem=recv, device_id=where, device_id_type=MESH
        )

    def kv_rows(i):
        return kv_all.at[pl.ds(0, HELD), pl.ds(16 * i, 16), :]

    def kv_part(head):
        return kv.at[:, :, pl.ds(pl.multiple_of(2 * HD * head, 2 * HD), 2 * HD)]

    def kv_copy(i):
        to = ahead(k, KVH - i, KVH)
        return remote(kv_part(to), kv_rows(i), kv_send.at[i], kv_recv.at[i], mp=QUARTERS * to + j)

    own_kv = pltpu.make_async_copy(kv_part(k), kv_rows(0), own_sem.at[2])
    for i in range(1, KVH):
        kv_copy(i).start()
    own_kv.start()

    target = (right, left)

    def rows_of(c):
        return pl.ds(PART * c, PART)

    def held(base, count, c):
        return kv_all.at[pl.ds(base, count), rows_of(c)]

    def z_own(way, i):
        src = kv_part(k) if i == 0 else kv_rows(i)
        dst = kv_all.at[pl.ds(HELD * (1 + way), HELD), pl.ds(16 * i, 16), :]
        return remote(src, dst, o_send.at[way, i], o_recv.at[way, i], store=target[way])

    def z_copy(way, s, c):
        if s == 1:
            src, dst = held(HELD * (1 + way), HELD, c), near[way * CHUNKS + c]
        elif s == 2:
            src, dst = packed.at[way, c], held(5 * HELD + CAP * way, CAP, c)
        elif s == 3:
            src, dst = packed_far.at[way, c % 2], relay.at[way, c % 2]
        else:
            src, dst = relay.at[way, c % 2], held(5 * HELD + 2 * CAP, CAP, c)
        return remote(src, dst, z_send.at[way, s, c], z_recv.at[way, s, c], store=target[way])

    def fresh_part(head):
        return fresh.at[:, pl.ds(pl.multiple_of(2 * HD * head, 2 * HD), 2 * HD)]

    def f_copy(i):
        to = ahead(k, i, KVH)
        return remote(fresh_part(to), fresh_all.at[k], f_send.at[i], f_recv.at[k], mp=QUARTERS * to + j)

    def f_arrival(i):
        come = ahead(k, i, KVH)
        return remote(fresh_part(come), fresh_all.at[come], f_send.at[i], f_recv.at[come], mp=QUARTERS * come + j)

    def q_copy(i):
        to = ahead(m, i, SHARDS)
        return remote(q.at[to // QUARTERS], q_all.at[:, m], q_send.at[i], q_recv.at[m], mp=to)

    def q_arrival(i):
        come = ahead(m, i, SHARDS)
        return remote(q.at[k], q_all.at[:, come], q_send.at[i], q_recv.at[come], mp=come)

    ring = RING * (m // RING)
    place = lax.rem(m, RING)

    def w_part(block):
        return w.at[:, pl.ds(pl.multiple_of(WIDTH * block, WIDTH), WIDTH)]

    def w_copy(i):
        to = ahead(place, i, RING)
        return remote(w_part(to), w_all.at[place], w_send.at[i], w_recv.at[place], mp=ring + to)

    def w_arrival(i):
        come = ahead(place, i, RING)
        return remote(w_part(come), w_all.at[come], w_send.at[i], w_recv.at[come], mp=ring + come)

    own = [
        pltpu.make_async_copy(fresh_part(k), fresh_all.at[k], own_sem.at[0]),
        pltpu.make_async_copy(q.at[k], q_all.at[:, m], own_sem.at[1]),
    ]

    def loop(low, high, act):
        def body(i, carry):
            act(i)
            return carry

        lax.fori_loop(low, high, body, 0)

    sent = ([], [])

    def push(way, copy):
        if len(sent[way]) >= WINDOW:
            sent[way][-WINDOW].wait_send()
        copy.start()
        sent[way].append(copy)

    def push_own(i):
        if i > 0:
            kv_copy(i).wait_recv()
        for way in range(2):
            push(way, z_own(way, i))

    for i in range(EARLY):
        push_own(i)
    loop(1, RING, lambda i: w_copy(i).start())

    cos, sin = cosines[m], sines[m]

    def turn(head):
        for b in range(REQ):
            for g in range(GROUP):
                at = pl.ds(pl.multiple_of((head * GROUP + g) * HD, HD), HD)
                value = rotate(queries[b, :, at].astype(jnp.float32), cos, sin)
                q_wide[head, b, pl.ds(g, TOKENS, stride=GROUP), :] = value * (HD**-0.5 * LOG2E)
            at = pl.multiple_of(2 * HD * head, 2 * HD)
            key = rotate(new_kv[b, :, pl.ds(at, HD)].astype(jnp.float32), cos, sin)
            fresh_wide[b * TOKENS : (b + 1) * TOKENS, pl.ds(at, HD)] = key
            at = pl.multiple_of(at + HD, HD)
            fresh_wide[b * TOKENS : (b + 1) * TOKENS, pl.ds(at, HD)] = new_kv[b, :, pl.ds(at, HD)].astype(jnp.float32)
        q[head] = q_wide[head].astype(jnp.bfloat16)

    loop(0, KVH, turn)
    fresh[...] = fresh_wide[...].astype(jnp.bfloat16)
    for copy in own:
        copy.start()
    loop(1, KVH, lambda i: f_copy(i).start())
    loop(1, SHARDS, lambda i: q_copy(i).start())
    for i in range(EARLY, KVH):
        push_own(i)
    own_kv.wait()

    def wanted(dest, source):
        def look(n, carry):
            count, picks = carry
            found = retrieval[lax.rem(n, R), dest * REQ + n // R]
            hit = (found >> 4) == source
            picks = tuple(
                jnp.where(hit & (count == at), found & (HELD - 1), pick) for at, pick in enumerate(picks)
            )
            return jnp.where(hit, count + 1, count), picks

        zero = jnp.int32(0)
        return lax.fori_loop(0, REQ * R, look, (zero, (zero,) * CAP))[1]

    picks = [wanted(ahead(z, 1, STORES), ahead(z, 6, STORES)), wanted(ahead(z, 7, STORES), ahead(z, 2, STORES))]
    far_picks = [wanted(ahead(z, 2, STORES), ahead(z, 6, STORES)), wanted(ahead(z, 6, STORES), ahead(z, 2, STORES))]

    halves = (range(CHUNKS // 2), range(CHUNKS // 2, CHUNKS))
    for c in range(CHUNKS):
        for way in range(2):
            for i in range(2 * c, 2 * c + 2):
                z_own(way, i).wait_recv()
            push(way, z_copy(way, 1, c))

    def keep(way, c):
        return pltpu.make_async_copy(
            near[way * CHUNKS + c], held(HELD * (3 + way), HELD, c), near_sem.at[way, c]
        )

    for c in range(CHUNKS):
        for way in range(2):
            z_copy(way, 1, c).wait_recv()
            source = near[way * CHUNKS + c]
            for at in range(CAP):
                packed[way, c, at] = source[picks[way][at]]
            push(way, z_copy(way, 2, c))
            if c in halves[way]:
                for at in range(CAP):
                    packed_far[way, c % 2, at] = source[far_picks[way][at]]
                push(way, z_copy(way, 3, c))
            keep(way, c).start()
    for n in range(CHUNKS // 2):
        for way in range(2):
            z_copy(way, 3, halves[way][n]).wait_recv()
            push(way, z_copy(way, 4, halves[way][n]))
    for c in range(CHUNKS):
        for way in range(2):
            keep(way, c).wait()
            z_copy(way, 2, c).wait_recv()
            if c in halves[way]:
                z_copy(way, 4, c).wait_recv()

    for copy in own:
        copy.wait()
    loop(1, RING, lambda i: w_arrival(i).wait_recv())
    loop(1, KVH, lambda i: f_arrival(i).wait_recv())
    loop(1, SHARDS, lambda i: q_arrival(i).wait_recv())
    loop(1, RING, lambda i: w_copy(i).wait_send())
    loop(1, KVH, lambda i: f_copy(i).wait_send())
    loop(1, SHARDS, lambda i: q_copy(i).wait_send())
    for i in range(1, KVH):
        kv_copy(i).wait_send()
    for copies in sent:
        for copy in copies[-WINDOW:]:
            copy.wait_send()


def spread(retrieval, kv, queries, new_kv, cosines, sines, w):
    bf, f32 = jnp.bfloat16, jnp.float32
    dma = pltpu.SemaphoreType.DMA
    return pl.pallas_call(
        spread_kernel,
        out_shape=(
            jax.ShapeDtypeStruct((PLACES, CTOK // QUARTERS, 2 * HD), bf),
            jax.ShapeDtypeStruct((REQ, SHARDS, QMAX // SHARDS * GROUP, HD), bf),
            jax.ShapeDtypeStruct((KVH, 16, 2 * HD), bf),
            jax.ShapeDtypeStruct((RING, D // SHARDS, WIDTH), bf),
        ),
        in_specs=[SMEM, HBM] + [VMEM] * 4 + [HBM],
        out_specs=(HBM,) * 4,
        scratch_shapes=[
            pltpu.VMEM((KVH, REQ, TOKENS * GROUP, HD), f32),
            pltpu.VMEM((KVH, REQ, TOKENS * GROUP, HD), bf),
            pltpu.VMEM((OWNED, KVH * 2 * HD), f32),
            pltpu.VMEM((OWNED, KVH * 2 * HD), bf),
            [pltpu.VMEM((HELD, PART, 2 * HD), bf)] * (2 * CHUNKS),
            pltpu.VMEM((2, CHUNKS, CAP, PART, 2 * HD), bf),
            pltpu.VMEM((2, CHUNKS // 2, CAP, PART, 2 * HD), bf),
            pltpu.VMEM((2, CHUNKS // 2, CAP, PART, 2 * HD), bf),
            dma((2, CHUNKS)),
            dma((3,)),
            dma((KVH,)), dma((KVH,)),
            dma((SHARDS,)), dma((SHARDS,)),
            dma((KVH,)), dma((KVH,)),
            dma((RING,)), dma((RING,)),
            dma((2, KVH)), dma((2, KVH)),
            dma((2, 5, CHUNKS)), dma((2, 5, CHUNKS)),
        ],
        compiler_params=pltpu.CompilerParams(
            collective_id=0, has_side_effects=True, vmem_limit_bytes=60 << 20
        ),
        name="spread",
    )(retrieval, kv, queries, new_kv, cosines, sines, w)


def attend_kernel(
    retrieval, places, lengths, cosines, sines, q_all, fresh_all, kv_all, out, lse,
    slots, keys, q, fresh, counts, sem, q_sem, fresh_sem,
):
    quarter = CTOK // QUARTERS
    held = R * quarter
    j = lax.rem(lax.axis_index("mp"), QUARTERS)
    z = lax.axis_index("store")

    def fetch(b, r, place=0):
        return pltpu.make_async_copy(
            kv_all.at[place], slots.at[b, pl.ds(r * quarter, quarter)], sem.at[b, r]
        )

    for s in range(STORES):
        counts[s] = 0

    def locate(b, r):
        found = retrieval[r, z * REQ + b]
        apart = ((found >> 4) - z) & (STORES - 1)
        rank = counts[apart]
        counts[apart] = rank + 1
        near = HELD * jnp.where(apart <= 2, 2 * apart, 2 * (STORES - apart) - 1) + (found & (HELD - 1))
        far = 5 * HELD + CAP * jnp.where(apart == 5, 0, jnp.where(apart == 3, 1, 2)) + rank
        return jnp.where((apart <= 2) | (apart >= 6), near, far)

    def fetch_q(b):
        return pltpu.make_async_copy(q_all.at[b], q.at[b], q_sem.at[b])

    fetch_fresh = pltpu.make_async_copy(fresh_all, fresh, fresh_sem)
    for b in range(REQ):
        for r in range(R):
            fetch(b, r, locate(b, r)).start()
        fetch_q(b).start()
        if b == 0:
            fetch_fresh.start()
    fetch_fresh.wait()
    for b in range(REQ):
        slots[b, held:, :] = fresh[...]
    keys[held:, :] = fresh[:, :HD]
    col = lax.broadcasted_iota(jnp.int32, (SUB, quarter), 1)
    fresh_token = TOKENS * (QUARTERS * (col >> 4) + j) + (col & 3)
    fresh_request = (col >> 2) & 3
    row = lax.broadcasted_iota(jnp.int32, (SUB, quarter), 0)
    for b in range(REQ):
        for r in range(R):
            fetch(b, r).wait()
        for r in range(R):
            at = places[b, r]
            key = slots[b, r * quarter : (r + 1) * quarter, :HD].astype(jnp.float32)
            key = rotate(key, cosines[pl.ds(at, 1), :], sines[pl.ds(at, 1), :])
            keys[r * quarter : (r + 1) * quarter, :] = key.astype(jnp.bfloat16)
        fetch_q(b).wait()
        length = lengths[b]

        def block(i, carry):
            spans = [pl.ds(pl.multiple_of(i * BLOCK + n * SUB, SUB), SUB) for n in range(BLOCK // SUB)]
            every = [
                lax.dot_general(
                    q[b, span, :], keys[...], (((1,), (1,)), ((), ())), preferred_element_type=jnp.float32
                )
                for span in spans
            ]
            for n, (span, scores) in enumerate(zip(spans, every)):
                at = i * BLOCK + n * SUB + row
                allowed = (fresh_request == b) & (fresh_token <= (at >> 3))
                scores = jnp.concatenate(
                    [scores[:, :held], jnp.where(allowed, scores[:, held:], -1e30)], axis=1
                )
                top = jnp.max(scores, axis=1, keepdims=True)
                expo = jnp.exp2(scores - top)
                total = jnp.sum(expo, axis=1, keepdims=True)
                sums = jnp.dot(
                    expo.astype(jnp.bfloat16), slots[b, :, HD:], preferred_element_type=jnp.float32
                )
                out[b, span, :] = jnp.where(at < length * GROUP, sums / total, 0.0).astype(jnp.bfloat16)
                logs = top + jnp.log(total) * LOG2E
                lse[b, :, span] = jnp.broadcast_to(logs, (SUB, HD)).T[:8]
            return carry

        def blank(i, carry):
            span = pl.ds(pl.multiple_of(i * BLOCK, BLOCK), BLOCK)
            out[b, span, :] = jnp.zeros((BLOCK, HD), jnp.bfloat16)
            lse[b, :, span] = jnp.zeros((8, BLOCK), jnp.float32)
            return carry

        used = (length * GROUP + BLOCK - 1) // BLOCK
        lax.fori_loop(0, used, block, 0)
        lax.fori_loop(used, ROWS // BLOCK, blank, 0)


def attend(retrieval, places, lengths, cosines, sines, q_all, fresh_all, kv_all):
    quarter = CTOK // QUARTERS
    bf = jnp.bfloat16
    dma = pltpu.SemaphoreType.DMA
    return pl.pallas_call(
        attend_kernel,
        out_shape=(
            jax.ShapeDtypeStruct((REQ, ROWS, HD), bf),
            jax.ShapeDtypeStruct((REQ, 8, ROWS), jnp.float32),
        ),
        in_specs=[SMEM] * 3 + [VMEM] * 2 + [HBM] * 3,
        out_specs=(VMEM, VMEM),
        scratch_shapes=[
            pltpu.VMEM((REQ, (R + 1) * quarter, 2 * HD), bf),
            pltpu.VMEM(((R + 1) * quarter, HD), bf),
            pltpu.VMEM((REQ, ROWS, HD), bf),
            pltpu.VMEM((quarter, 2 * HD), bf),
            pltpu.SMEM((STORES,), jnp.int32),
            dma((REQ, R)), dma((REQ,)), dma,
        ],
        compiler_params=pltpu.CompilerParams(vmem_limit_bytes=60 << 20),
        name="attend",
    )(retrieval, places, lengths, cosines, sines, q_all, fresh_all, kv_all)


def merge_kernel(
    part, lse, w_own, w_all, hidden, mixed,
    w, from_mate, from_mate_lse, pair, pair_lse, from_chip, from_chip_lse, rows, attended, sent, got,
    w_sem, own_sem, c_send, c_recv, l_send, l_recv, g_send, g_recv, p_send, p_recv,
):
    m = lax.axis_index("mp")
    k = m // QUARTERS
    j = lax.rem(m, QUARTERS)
    core, half = lax.rem(j, 2), j // 2
    mate, chip = m + 1 - 2 * core, QUARTERS * k + ahead(j, 2, QUARTERS)
    ring = RING * (m // RING)
    place = lax.rem(m, RING)
    w_loads = [
        pltpu.make_async_copy(
            w_own.at[:, pl.ds(pl.multiple_of(WIDTH * place, WIDTH), WIDTH)], w.at[place], w_sem.at[0]
        )
    ]
    for i in range(1, RING):
        come = ahead(place, i, RING)
        w_loads.append(pltpu.make_async_copy(w_all.at[come], w.at[come], w_sem.at[i]))
    for load in w_loads:
        load.start()

    barrier = pltpu.get_barrier_semaphore()

    def loop(low, high, act):
        def body(i, carry):
            act(i)
            return carry

        lax.fori_loop(low, high, body, 0)

    loop(
        1,
        SHARDS,
        lambda i: pl.semaphore_signal(
            barrier, 1, device_id={"mp": ahead(m, i, SHARDS)}, device_id_type=MESH
        ),
    )
    pl.semaphore_wait(barrier, SHARDS - 1)

    def remote(src, dst, send, recv, to):
        return pltpu.make_async_remote_copy(
            src_ref=src, dst_ref=dst, send_sem=send, recv_sem=recv, device_id={"mp": to}, device_id_type=MESH
        )

    def mate_copies(at, n):
        give = 1 - core + 2 * at
        return (
            remote(lse.at[give], from_mate_lse.at[at], l_send.at[n], l_recv.at[n], mate),
            remote(part.at[give], from_mate.at[at], c_send.at[n], c_recv.at[n], mate),
        )

    def combine(one, one_log, two, two_log):
        top = jnp.maximum(one_log, two_log)
        one_share, two_share = jnp.exp2(one_log - top), jnp.exp2(two_log - top)
        total = one_share + two_share
        share = jnp.broadcast_to(one_share / total, (HD, ROWS)).T
        return two + (one - two) * share, top + jnp.log(total) * LOG2E

    def wide(ref, at):
        return ref[at].astype(jnp.float32)

    pair_copies = (
        remote(pair_lse, from_chip_lse, l_send.at[2], l_recv.at[2], chip),
        remote(pair, from_chip, c_send.at[2], c_recv.at[2], chip),
    )
    other = 1 - half
    order = ((other, 0), (half, 1))
    for at, n in order:
        for copy in mate_copies(at, n):
            copy.start()
    for copy in mate_copies(other, 0):
        copy.wait_recv()
    give = core + 2 * other
    value, logs = combine(
        wide(part, give), lse[give, :1, :], wide(from_mate, other), from_mate_lse[other, :1, :]
    )
    pair[...] = value.astype(jnp.bfloat16)
    pair_lse[...] = jnp.broadcast_to(logs, (8, ROWS))
    for copy in pair_copies:
        copy.start()
    for copy in mate_copies(half, 1):
        copy.wait_recv()
    value, logs = combine(
        wide(part, j), lse[j, :1, :], wide(from_mate, half), from_mate_lse[half, :1, :]
    )
    rows[...] = value
    for copy in pair_copies:
        copy.wait_recv()
    value, logs = combine(rows[...], logs, from_chip[...].astype(jnp.float32), from_chip_lse[:1, :])
    rows[...] = value
    for h in range(GROUP):
        attended[place, :, h * HD : (h + 1) * HD] = rows[pl.ds(h, QMAX, stride=GROUP), :].astype(jnp.bfloat16)

    def g_copy(at, n, to):
        return remote(attended.at[at], attended.at[at], g_send.at[n], g_recv.at[n], to)

    hops = (2, 6, 4)
    mate_place = place + 1 - 2 * core
    g_copy(place, 0, mate).start()
    for n, hop in enumerate(hops):
        g_copy(place, 1 + n, ring + ahead(place, hop, RING)).start()
    for load in w_loads:
        load.wait()
    for n, hop in enumerate(hops):
        come = ahead(place, RING - hop, RING)
        g_copy(come, 1 + n, mate).wait_recv()
        g_copy(come, 4 + n, mate).start()
    g_copy(mate_place, 0, mate).wait_recv()
    for n, hop in enumerate(hops):
        g_copy(ahead(mate_place, RING - hop, RING), 4 + n, mate).wait_recv()

    owned = OWNED
    span = REQ * QMAX // 4
    per = span // owned

    def p_copy(to):
        return remote(
            sent.at[pl.ds(pl.multiple_of(owned * to, owned), owned), :], got.at[m], p_send.at[to], p_recv.at[m], to
        )

    def p_own():
        return pltpu.make_async_copy(
            sent.at[pl.ds(pl.multiple_of(owned * m, owned), owned), :], got.at[m], own_sem
        )

    def p_arrival(come):
        return remote(
            sent.at[pl.ds(pl.multiple_of(owned * come, owned), owned), :], got.at[come], p_send.at[come], p_recv.at[come], come
        )

    def project(i):
        block = ahead(m // per, i, 4)
        at = block * span + lax.broadcasted_iota(jnp.int32, (span, REQ * QMAX), 0)
        source = QMAX * ((at >> 2) & 3) + 4 * (at >> 4) + (at & 3)
        pick = (source == lax.broadcasted_iota(jnp.int32, (span, REQ * QMAX), 1)).astype(jnp.bfloat16)
        total = None
        for g in range(RING // REQ):
            chosen = jnp.dot(
                pick,
                attended[REQ * g : REQ * (g + 1)].reshape(REQ * QMAX, GROUP * HD),
                preferred_element_type=jnp.float32,
            ).astype(jnp.bfloat16)
            term = jnp.dot(
                chosen,
                w[REQ * g : REQ * (g + 1)].reshape(GROUP * HD, WIDTH),
                preferred_element_type=jnp.float32,
            )
            total = term if total is None else total + term
        sent[pl.ds(pl.multiple_of(block * span, span), span), :] = total.astype(jnp.bfloat16)

        def ship(t):
            to = block * per + ahead(m, t, per)

            @pl.when(to != m)
            def _():
                p_copy(to).start()

            @pl.when(to == m)
            def _():
                p_own().start()

        loop(0, per, ship)

    loop(0, 4, project)
    p_own().wait()
    loop(1, SHARDS, lambda i: p_arrival(ahead(m, i, SHARDS)).wait_recv())

    for c in range(RING):
        cols = slice(c * WIDTH, (c + 1) * WIDTH)
        value = got[c].astype(jnp.float32)
        for group in range(1, SHARDS // RING):
            value = value + got[RING * group + c].astype(jnp.float32)
        for b in range(REQ):
            mixed[b, :, cols] = value[b * TOKENS : (b + 1) * TOKENS] + hidden[b, :, cols].astype(jnp.float32)

    for at, n in order:
        for copy in mate_copies(at, n):
            copy.wait_send()
    for copy in pair_copies:
        copy.wait_send()
    g_copy(place, 0, mate).wait_send()
    for n, hop in enumerate(hops):
        g_copy(place, 1 + n, mate).wait_send()
        g_copy(ahead(place, RING - hop, RING), 4 + n, mate).wait_send()
    loop(1, SHARDS, lambda i: p_copy(ahead(m, i, SHARDS)).wait_send())


def merge(part, lse, w_own, w_all, hidden):
    bf, f32 = jnp.bfloat16, jnp.float32
    dma = pltpu.SemaphoreType.DMA
    owned = OWNED
    return pl.pallas_call(
        merge_kernel,
        out_shape=jax.ShapeDtypeStruct((REQ, TOKENS, D), f32),
        in_specs=[VMEM, VMEM, HBM, HBM, VMEM],
        out_specs=VMEM,
        scratch_shapes=[
            pltpu.VMEM((RING, D // SHARDS, WIDTH), bf),
            pltpu.VMEM((2, ROWS, HD), bf),
            pltpu.VMEM((2, 8, ROWS), f32),
            pltpu.VMEM((ROWS, HD), bf),
            pltpu.VMEM((8, ROWS), f32),
            pltpu.VMEM((ROWS, HD), bf),
            pltpu.VMEM((8, ROWS), f32),
            pltpu.VMEM((ROWS, HD), f32),
            pltpu.VMEM((RING, QMAX, GROUP * HD), bf),
            pltpu.VMEM((REQ * QMAX, WIDTH), bf),
            pltpu.VMEM((SHARDS, owned, WIDTH), bf),
            dma((RING,)), dma,
            dma((3,)), dma((3,)),
            dma((3,)), dma((3,)),
            dma((7,)), dma((7,)),
            dma((SHARDS,)), dma((SHARDS,)),
        ],
        compiler_params=pltpu.CompilerParams(
            collective_id=1, has_side_effects=True, vmem_limit_bytes=52 << 20
        ),
        name="merge",
    )(part, lse, w_own, w_all, hidden)


def on_device(
    kv_store, retrieval, positions, lengths, queries, new_kv, hidden, out_weight, norm_gain
):
    context = R * CTOK
    cos_own, sin_own = turns(np.arange(context, context + QMAX))
    shape = (SHARDS, TOKENS, HD)
    wanted = jnp.transpose(retrieval)
    kv_all, q_all, fresh_all, w_all = spread(
        wanted, kv_store, queries, new_kv, cos_own.reshape(shape), sin_own.reshape(shape), out_weight
    )
    cos_at, sin_at = turns(np.arange(R) * CTOK)
    part, lse = attend(
        wanted, positions, lengths, cos_at, sin_at, q_all.reshape(REQ, ROWS, HD),
        fresh_all.reshape(KVH * 16, 2 * HD),
        kv_all,
    )
    mixed = merge(part, lse, out_weight, w_all, hidden)
    square = jnp.mean(mixed * mixed, axis=-1, keepdims=True)
    normed = mixed * lax.rsqrt(square + eps_norm) * norm_gain.astype(jnp.float32)
    return mixed.astype(jnp.bfloat16), normed.astype(jnp.bfloat16)


def solution(mesh):
    return jax.shard_map(
        on_device,
        mesh=mesh,
        in_specs=(
            P("store", "mp", None),
            P(),
            P("store", None),
            P("store"),
            P("store", "mp", None),
            P("store", "mp", None),
            P("store", "mp", None),
            P("mp", None),
            P(),
        ),
        out_specs=(P("store", "mp", None), P("store", "mp", None)),
        check_vma=False,
    )
```

```python
import jax
import jax.numpy as jnp
import numpy as np
from jax import lax
from jax.experimental import pallas as pl
from jax.experimental.pallas import tpu as pltpu
from jax.sharding import PartitionSpec as P

MESH = pl.DeviceIdType.MESH
HBM = pl.BlockSpec(memory_space=pltpu.HBM)
VMEM = pl.BlockSpec(memory_space=pltpu.VMEM)
SMEM = pl.BlockSpec(memory_space=pltpu.SMEM)

STORES = 8
SHARDS = 32
HEADS = 64
KVH = 8
GROUP = 8
HD = 128
D = 8192
QUARTERS = 4
CTOK = 512
R = 8
REQ = 4
QMAX = 128
HELD = 16
CHUNKS = 4
PART = CTOK // 4 // CHUNKS
CAP = 8
WINDOW = 4
EARLY = 3
PLACES = 5 * HELD + 3 * CAP
RING = 8
WIDTH = D // RING
ROWS = QMAX * GROUP
HALF = ROWS // 2
BLOCK = 512
SUB = 256
TOKENS = QMAX // SHARDS
OWNED = REQ * TOKENS
LOG2E = 1.4426950408889634

theta_base = 1000000.0
eps_norm = 1e-06


def turns(places):
    inv_freq = np.float32(theta_base) ** (-(np.arange(HD // 2, dtype=np.float32) * np.float32(2.0)) / np.float32(HD))
    angles = np.asarray(places, np.float32)[..., None] * inv_freq
    cosines, sines = np.cos(angles), np.sin(angles)
    return (
        jnp.asarray(np.concatenate([cosines, cosines], axis=-1)),
        jnp.asarray(np.concatenate([-sines, sines], axis=-1)),
    )


def rotate(field_in, cosines, sines):
    return field_in * cosines + pltpu.roll(field_in, HD // 2, 1) * sines


def ahead(a, b, n):
    return lax.rem(a + b, n)


def spread_kernel(
    retrieval, kv, queries, new_kv, cosines, sines, w, kv_all, q_all, fresh_all, w_all,
    q_wide, q, fresh_wide, fresh, near, packed, packed_far, relay, near_sem, own_sem, kv_send, kv_recv, q_send, q_recv, f_send, f_recv, w_send, w_recv, o_send, o_recv, z_send, z_recv,
):
    m = lax.axis_index("mp")
    z = lax.axis_index("store")
    k = m // QUARTERS
    j = lax.rem(m, QUARTERS)
    right, left = ahead(z, 1, STORES), ahead(z, STORES - 1, STORES)

    barrier = pltpu.get_barrier_semaphore()

    def greet(i, carry):
        pl.semaphore_signal(barrier, 1, device_id={"mp": ahead(m, i, SHARDS)}, device_id_type=MESH)
        return carry

    lax.fori_loop(1, SHARDS, greet, 0)
    for beside in (left, right):
        pl.semaphore_signal(barrier, 1, device_id={"store": beside}, device_id_type=MESH)
    pl.semaphore_wait(barrier, SHARDS + 1)

    def remote(src, dst, send, recv, **where):
        return pltpu.make_async_remote_copy(
            src_ref=src, dst_ref=dst, send_sem=send, recv_sem=recv, device_id=where, device_id_type=MESH
        )

    def kv_rows(i):
        return kv_all.at[pl.ds(0, HELD), pl.ds(16 * i, 16), :]

    def kv_part(head):
        return kv.at[:, :, pl.ds(pl.multiple_of(2 * HD * head, 2 * HD), 2 * HD)]

    def kv_copy(i):
        to = ahead(k, KVH - i, KVH)
        return remote(kv_part(to), kv_rows(i), kv_send.at[i], kv_recv.at[i], mp=QUARTERS * to + j)

    own_kv = pltpu.make_async_copy(kv_part(k), kv_rows(0), own_sem.at[2])
    for i in range(1, KVH):
        kv_copy(i).start()
    own_kv.start()

    target = (right, left)

    def rows_of(c):
        return pl.ds(PART * c, PART)

    def held(base, count, c):
        return kv_all.at[pl.ds(base, count), rows_of(c)]

    def z_own(way, i):
        src = kv_part(k) if i == 0 else kv_rows(i)
        dst = kv_all.at[pl.ds(HELD * (1 + way), HELD), pl.ds(16 * i, 16), :]
        return remote(src, dst, o_send.at[way, i], o_recv.at[way, i], store=target[way])

    def z_copy(way, s, c):
        if s == 1:
            src, dst = held(HELD * (1 + way), HELD, c), near[way * CHUNKS + c]
        elif s == 2:
            src, dst = packed.at[way, c], held(5 * HELD + CAP * way, CAP, c)
        elif s == 3:
            src, dst = packed_far.at[way, c % 2], relay.at[way, c % 2]
        else:
            src, dst = relay.at[way, c % 2], held(5 * HELD + 2 * CAP, CAP, c)
        return remote(src, dst, z_send.at[way, s, c], z_recv.at[way, s, c], store=target[way])

    def fresh_part(head):
        return fresh.at[:, pl.ds(pl.multiple_of(2 * HD * head, 2 * HD), 2 * HD)]

    def f_copy(i):
        to = ahead(k, i, KVH)
        return remote(fresh_part(to), fresh_all.at[k], f_send.at[i], f_recv.at[k], mp=QUARTERS * to + j)

    def f_arrival(i):
        come = ahead(k, i, KVH)
        return remote(fresh_part(come), fresh_all.at[come], f_send.at[i], f_recv.at[come], mp=QUARTERS * come + j)

    def q_copy(i):
        to = ahead(m, i, SHARDS)
        return remote(q.at[to // QUARTERS], q_all.at[:, m], q_send.at[i], q_recv.at[m], mp=to)

    def q_arrival(i):
        come = ahead(m, i, SHARDS)
        return remote(q.at[k], q_all.at[:, come], q_send.at[i], q_recv.at[come], mp=come)

    ring = RING * (m // RING)
    place = lax.rem(m, RING)

    def w_part(block):
        return w.at[:, pl.ds(pl.multiple_of(WIDTH * block, WIDTH), WIDTH)]

    def w_copy(i):
        to = ahead(place, i, RING)
        return remote(w_part(to), w_all.at[place], w_send.at[i], w_recv.at[place], mp=ring + to)

    def w_arrival(i):
        come = ahead(place, i, RING)
        return remote(w_part(come), w_all.at[come], w_send.at[i], w_recv.at[come], mp=ring + come)

    own = [
        pltpu.make_async_copy(fresh_part(k), fresh_all.at[k], own_sem.at[0]),
        pltpu.make_async_copy(q.at[k], q_all.at[:, m], own_sem.at[1]),
    ]

    def loop(low, high, act):
        def body(i, carry):
            act(i)
            return carry

        lax.fori_loop(low, high, body, 0)

    sent = ([], [])

    def push(way, copy):
        if len(sent[way]) >= WINDOW:
            sent[way][-WINDOW].wait_send()
        copy.start()
        sent[way].append(copy)

    def push_own(i):
        if i > 0:
            kv_copy(i).wait_recv()
        for way in range(2):
            push(way, z_own(way, i))

    for i in range(EARLY):
        push_own(i)
    loop(1, RING, lambda i: w_copy(i).start())

    cos, sin = cosines[m], sines[m]

    def turn(head):
        for b in range(REQ):
            for g in range(GROUP):
                at = pl.ds(pl.multiple_of((head * GROUP + g) * HD, HD), HD)
                value = rotate(queries[b, :, at].astype(jnp.float32), cos, sin)
                q_wide[head, b, pl.ds(g, TOKENS, stride=GROUP), :] = value * (HD**-0.5 * LOG2E)
            at = pl.multiple_of(2 * HD * head, 2 * HD)
            key = rotate(new_kv[b, :, pl.ds(at, HD)].astype(jnp.float32), cos, sin)
            fresh_wide[b * TOKENS : (b + 1) * TOKENS, pl.ds(at, HD)] = key
            at = pl.multiple_of(at + HD, HD)
            fresh_wide[b * TOKENS : (b + 1) * TOKENS, pl.ds(at, HD)] = new_kv[b, :, pl.ds(at, HD)].astype(jnp.float32)
        q[head] = q_wide[head].astype(jnp.bfloat16)

    loop(0, KVH, turn)
    fresh[...] = fresh_wide[...].astype(jnp.bfloat16)
    for copy in own:
        copy.start()
    loop(1, KVH, lambda i: f_copy(i).start())
    loop(1, SHARDS, lambda i: q_copy(i).start())
    for i in range(EARLY, KVH):
        push_own(i)
    own_kv.wait()

    def wanted(dest, source):
        def look(n, carry):
            count, picks = carry
            found = retrieval[lax.rem(n, R), dest * REQ + n // R]
            hit = (found >> 4) == source
            picks = tuple(
                jnp.where(hit & (count == at), found & (HELD - 1), pick) for at, pick in enumerate(picks)
            )
            return jnp.where(hit, count + 1, count), picks

        zero = jnp.int32(0)
        return lax.fori_loop(0, REQ * R, look, (zero, (zero,) * CAP))[1]

    picks = [wanted(ahead(z, 1, STORES), ahead(z, 6, STORES)), wanted(ahead(z, 7, STORES), ahead(z, 2, STORES))]
    far_picks = [wanted(ahead(z, 2, STORES), ahead(z, 6, STORES)), wanted(ahead(z, 6, STORES), ahead(z, 2, STORES))]

    halves = (range(CHUNKS // 2), range(CHUNKS // 2, CHUNKS))
    for c in range(CHUNKS):
        for way in range(2):
            for i in range(2 * c, 2 * c + 2):
                z_own(way, i).wait_recv()
            push(way, z_copy(way, 1, c))

    def keep(way, c):
        return pltpu.make_async_copy(
            near[way * CHUNKS + c], held(HELD * (3 + way), HELD, c), near_sem.at[way, c]
        )

    for c in range(CHUNKS):
        for way in range(2):
            z_copy(way, 1, c).wait_recv()
            source = near[way * CHUNKS + c]
            for at in range(CAP):
                packed[way, c, at] = source[picks[way][at]]
            push(way, z_copy(way, 2, c))
            if c in halves[way]:
                for at in range(CAP):
                    packed_far[way, c % 2, at] = source[far_picks[way][at]]
                push(way, z_copy(way, 3, c))
            keep(way, c).start()
    for n in range(CHUNKS // 2):
        for way in range(2):
            z_copy(way, 3, halves[way][n]).wait_recv()
            push(way, z_copy(way, 4, halves[way][n]))
    for c in range(CHUNKS):
        for way in range(2):
            keep(way, c).wait()
            z_copy(way, 2, c).wait_recv()
            if c in halves[way]:
                z_copy(way, 4, c).wait_recv()

    for copy in own:
        copy.wait()
    loop(1, RING, lambda i: w_arrival(i).wait_recv())
    loop(1, KVH, lambda i: f_arrival(i).wait_recv())
    loop(1, SHARDS, lambda i: q_arrival(i).wait_recv())
    loop(1, RING, lambda i: w_copy(i).wait_send())
    loop(1, KVH, lambda i: f_copy(i).wait_send())
    loop(1, SHARDS, lambda i: q_copy(i).wait_send())
    for i in range(1, KVH):
        kv_copy(i).wait_send()
    for copies in sent:
        for copy in copies[-WINDOW:]:
            copy.wait_send()


def spread(retrieval, kv, queries, new_kv, cosines, sines, w):
    bf, f32 = jnp.bfloat16, jnp.float32
    dma = pltpu.SemaphoreType.DMA
    return pl.pallas_call(
        spread_kernel,
        out_shape=(
            jax.ShapeDtypeStruct((PLACES, CTOK // QUARTERS, 2 * HD), bf),
            jax.ShapeDtypeStruct((REQ, SHARDS, QMAX // SHARDS * GROUP, HD), bf),
            jax.ShapeDtypeStruct((KVH, 16, 2 * HD), bf),
            jax.ShapeDtypeStruct((RING, D // SHARDS, WIDTH), bf),
        ),
        in_specs=[SMEM, HBM] + [VMEM] * 4 + [HBM],
        out_specs=(HBM,) * 4,
        scratch_shapes=[
            pltpu.VMEM((KVH, REQ, TOKENS * GROUP, HD), f32),
            pltpu.VMEM((KVH, REQ, TOKENS * GROUP, HD), bf),
            pltpu.VMEM((OWNED, KVH * 2 * HD), f32),
            pltpu.VMEM((OWNED, KVH * 2 * HD), bf),
            [pltpu.VMEM((HELD, PART, 2 * HD), bf)] * (2 * CHUNKS),
            pltpu.VMEM((2, CHUNKS, CAP, PART, 2 * HD), bf),
            pltpu.VMEM((2, CHUNKS // 2, CAP, PART, 2 * HD), bf),
            pltpu.VMEM((2, CHUNKS // 2, CAP, PART, 2 * HD), bf),
            dma((2, CHUNKS)),
            dma((3,)),
            dma((KVH,)), dma((KVH,)),
            dma((SHARDS,)), dma((SHARDS,)),
            dma((KVH,)), dma((KVH,)),
            dma((RING,)), dma((RING,)),
            dma((2, KVH)), dma((2, KVH)),
            dma((2, 5, CHUNKS)), dma((2, 5, CHUNKS)),
        ],
        compiler_params=pltpu.CompilerParams(
            collective_id=0, has_side_effects=True, vmem_limit_bytes=60 << 20
        ),
        name="spread",
    )(retrieval, kv, queries, new_kv, cosines, sines, w)


def attend_kernel(
    retrieval, places, lengths, cosines, sines, q_all, fresh_all, kv_all, out, lse,
    slots, keys, q, fresh, counts, sem, q_sem, fresh_sem,
):
    quarter = CTOK // QUARTERS
    held = R * quarter
    j = lax.rem(lax.axis_index("mp"), QUARTERS)
    z = lax.axis_index("store")

    def fetch(b, r, place=0):
        return pltpu.make_async_copy(
            kv_all.at[place], slots.at[b, pl.ds(r * quarter, quarter)], sem.at[b, r]
        )

    for s in range(STORES):
        counts[s] = 0

    def locate(b, r):
        found = retrieval[r, z * REQ + b]
        apart = ((found >> 4) - z) & (STORES - 1)
        rank = counts[apart]
        counts[apart] = rank + 1
        near = HELD * jnp.where(apart <= 2, 2 * apart, 2 * (STORES - apart) - 1) + (found & (HELD - 1))
        far = 5 * HELD + CAP * jnp.where(apart == 5, 0, jnp.where(apart == 3, 1, 2)) + rank
        return jnp.where((apart <= 2) | (apart >= 6), near, far)

    def fetch_q(b):
        return pltpu.make_async_copy(q_all.at[b], q.at[b], q_sem.at[b])

    fetch_fresh = pltpu.make_async_copy(fresh_all, fresh, fresh_sem)
    for b in range(REQ):
        for r in range(R):
            fetch(b, r, locate(b, r)).start()
        fetch_q(b).start()
        if b == 0:
            fetch_fresh.start()
    fetch_fresh.wait()
    for b in range(REQ):
        slots[b, held:, :] = fresh[...]
    keys[held:, :] = fresh[:, :HD]
    col = lax.broadcasted_iota(jnp.int32, (SUB, quarter), 1)
    fresh_token = TOKENS * (QUARTERS * (col >> 4) + j) + (col & 3)
    fresh_request = (col >> 2) & 3
    row = lax.broadcasted_iota(jnp.int32, (SUB, quarter), 0)
    for b in range(REQ):
        for r in range(R):
            fetch(b, r).wait()
        for r in range(R):
            at = places[b, r]
            key = slots[b, r * quarter : (r + 1) * quarter, :HD].astype(jnp.float32)
            key = rotate(key, cosines[pl.ds(at, 1), :], sines[pl.ds(at, 1), :])
            keys[r * quarter : (r + 1) * quarter, :] = key.astype(jnp.bfloat16)
        fetch_q(b).wait()
        length = lengths[b]

        def block(i, carry):
            spans = [pl.ds(pl.multiple_of(i * BLOCK + n * SUB, SUB), SUB) for n in range(BLOCK // SUB)]
            every = [
                lax.dot_general(
                    q[b, span, :], keys[...], (((1,), (1,)), ((), ())), preferred_element_type=jnp.float32
                )
                for span in spans
            ]
            for n, (span, scores) in enumerate(zip(spans, every)):
                at = i * BLOCK + n * SUB + row
                allowed = (fresh_request == b) & (fresh_token <= (at >> 3))
                scores = jnp.concatenate(
                    [scores[:, :held], jnp.where(allowed, scores[:, held:], -1e30)], axis=1
                )
                top = jnp.max(scores, axis=1, keepdims=True)
                expo = jnp.exp2(scores - top)
                total = jnp.sum(expo, axis=1, keepdims=True)
                sums = jnp.dot(
                    expo.astype(jnp.bfloat16), slots[b, :, HD:], preferred_element_type=jnp.float32
                )
                out[b, span, :] = jnp.where(at < length * GROUP, sums / total, 0.0).astype(jnp.bfloat16)
                logs = top + jnp.log(total) * LOG2E
                lse[b, :, span] = jnp.broadcast_to(logs, (SUB, HD)).T[:8]
            return carry

        def blank(i, carry):
            span = pl.ds(pl.multiple_of(i * BLOCK, BLOCK), BLOCK)
            out[b, span, :] = jnp.zeros((BLOCK, HD), jnp.bfloat16)
            lse[b, :, span] = jnp.zeros((8, BLOCK), jnp.float32)
            return carry

        used = (length * GROUP + BLOCK - 1) // BLOCK
        lax.fori_loop(0, used, block, 0)
        lax.fori_loop(used, ROWS // BLOCK, blank, 0)


def attend(retrieval, places, lengths, cosines, sines, q_all, fresh_all, kv_all):
    quarter = CTOK // QUARTERS
    bf = jnp.bfloat16
    dma = pltpu.SemaphoreType.DMA
    return pl.pallas_call(
        attend_kernel,
        out_shape=(
            jax.ShapeDtypeStruct((REQ, ROWS, HD), bf),
            jax.ShapeDtypeStruct((REQ, 8, ROWS), jnp.float32),
        ),
        in_specs=[SMEM] * 3 + [VMEM] * 2 + [HBM] * 3,
        out_specs=(VMEM, VMEM),
        scratch_shapes=[
            pltpu.VMEM((REQ, (R + 1) * quarter, 2 * HD), bf),
            pltpu.VMEM(((R + 1) * quarter, HD), bf),
            pltpu.VMEM((REQ, ROWS, HD), bf),
            pltpu.VMEM((quarter, 2 * HD), bf),
            pltpu.SMEM((STORES,), jnp.int32),
            dma((REQ, R)), dma((REQ,)), dma,
        ],
        compiler_params=pltpu.CompilerParams(vmem_limit_bytes=60 << 20),
        name="attend",
    )(retrieval, places, lengths, cosines, sines, q_all, fresh_all, kv_all)


def merge_kernel(
    part, lse, w_own, w_all, hidden, mixed,
    w, from_mate, from_mate_lse, pair, pair_lse, from_chip, from_chip_lse, rows, attended, sent, got,
    w_sem, own_sem, c_send, c_recv, l_send, l_recv, g_send, g_recv, p_send, p_recv,
):
    m = lax.axis_index("mp")
    k = m // QUARTERS
    j = lax.rem(m, QUARTERS)
    core, half = lax.rem(j, 2), j // 2
    mate, chip = m + 1 - 2 * core, QUARTERS * k + ahead(j, 2, QUARTERS)
    ring = RING * (m // RING)
    place = lax.rem(m, RING)
    w_loads = [
        pltpu.make_async_copy(
            w_own.at[:, pl.ds(pl.multiple_of(WIDTH * place, WIDTH), WIDTH)], w.at[place], w_sem.at[0]
        )
    ]
    for i in range(1, RING):
        come = ahead(place, i, RING)
        w_loads.append(pltpu.make_async_copy(w_all.at[come], w.at[come], w_sem.at[i]))
    for load in w_loads:
        load.start()

    barrier = pltpu.get_barrier_semaphore()

    def loop(low, high, act):
        def body(i, carry):
            act(i)
            return carry

        lax.fori_loop(low, high, body, 0)

    loop(
        1,
        SHARDS,
        lambda i: pl.semaphore_signal(
            barrier, 1, device_id={"mp": ahead(m, i, SHARDS)}, device_id_type=MESH
        ),
    )
    pl.semaphore_wait(barrier, SHARDS - 1)

    def remote(src, dst, send, recv, to):
        return pltpu.make_async_remote_copy(
            src_ref=src, dst_ref=dst, send_sem=send, recv_sem=recv, device_id={"mp": to}, device_id_type=MESH
        )

    def mate_copies(at, n):
        give = 1 - core + 2 * at
        span = pl.ds(n // 2 * HALF, HALF)
        return (
            remote(lse.at[give, :, span], from_mate_lse.at[at, :, span], l_send.at[n], l_recv.at[n], mate),
            remote(part.at[give, span], from_mate.at[at, span], c_send.at[n], c_recv.at[n], mate),
        )

    def chip_copies(n):
        span = pl.ds(n * HALF, HALF)
        return (
            remote(pair_lse.at[:, span], from_chip_lse.at[:, span], l_send.at[4 + n], l_recv.at[4 + n], chip),
            remote(pair.at[span], from_chip.at[span], c_send.at[4 + n], c_recv.at[4 + n], chip),
        )

    def combine(one, one_log, two, two_log):
        top = jnp.maximum(one_log, two_log)
        one_share, two_share = jnp.exp2(one_log - top), jnp.exp2(two_log - top)
        total = one_share + two_share
        share = jnp.broadcast_to(one_share / total, (HD, HALF)).T
        return two + (one - two) * share, top + jnp.log(total) * LOG2E

    def with_mate(at, n):
        span = slice(n * HALF, (n + 1) * HALF)
        keep = core + 2 * at
        return combine(
            part[keep, span].astype(jnp.float32), lse[keep, :1, span],
            from_mate[at, span].astype(jnp.float32), from_mate_lse[at, :1, span],
        )

    def g_copy(at, n, hf, to):
        block = attended.at[at, pl.ds(hf * (QMAX // 2), QMAX // 2)]
        return remote(block, block, g_send.at[hf, n], g_recv.at[hf, n], to)

    other = 1 - half
    order = ((other, 0), (half, 1))
    hops = (2, 6, 4)
    mate_place = place + 1 - 2 * core
    for hf in range(2):
        for at, n in order:
            for copy in mate_copies(at, 2 * hf + n):
                copy.start()
    for hf in range(2):
        for copy in mate_copies(other, 2 * hf):
            copy.wait_recv()
        value, logs = with_mate(other, hf)
        pair[hf * HALF : (hf + 1) * HALF, :] = value.astype(jnp.bfloat16)
        pair_lse[:, hf * HALF : (hf + 1) * HALF] = jnp.broadcast_to(logs, (8, HALF))
        for copy in chip_copies(hf):
            copy.start()
    kept = []
    for hf in range(2):
        for copy in mate_copies(half, 2 * hf + 1):
            copy.wait_recv()
        value, logs = with_mate(half, hf)
        rows[hf * HALF : (hf + 1) * HALF, :] = value
        kept.append(logs)
    for hf in range(2):
        span = slice(hf * HALF, (hf + 1) * HALF)
        for copy in chip_copies(hf):
            copy.wait_recv()
        rows[span, :] = combine(
            rows[span, :], kept[hf], from_chip[span].astype(jnp.float32), from_chip_lse[:1, span]
        )[0]
        for h in range(GROUP):
            attended[place, hf * (QMAX // 2) : (hf + 1) * (QMAX // 2), h * HD : (h + 1) * HD] = rows[
                pl.ds(hf * HALF + h, QMAX // 2, stride=GROUP), :
            ].astype(jnp.bfloat16)
        for n, hop in enumerate(hops):
            g_copy(place, 1 + n, hf, ring + ahead(place, hop, RING)).start()
        g_copy(place, 0, hf, mate).start()
    for load in w_loads:
        load.wait()
    for hf in range(2):
        for n, hop in enumerate(hops):
            come = ahead(place, RING - hop, RING)
            g_copy(come, 1 + n, hf, mate).wait_recv()
            g_copy(come, 4 + n, hf, mate).start()
    for hf in range(2):
        g_copy(mate_place, 0, hf, mate).wait_recv()
        for n, hop in enumerate(hops):
            g_copy(ahead(mate_place, RING - hop, RING), 4 + n, hf, mate).wait_recv()

    owned = OWNED
    span = REQ * QMAX // 4
    per = span // owned

    def p_copy(to):
        return remote(
            sent.at[pl.ds(pl.multiple_of(owned * to, owned), owned), :], got.at[m], p_send.at[to], p_recv.at[m], to
        )

    def p_own():
        return pltpu.make_async_copy(
            sent.at[pl.ds(pl.multiple_of(owned * m, owned), owned), :], got.at[m], own_sem
        )

    def p_arrival(come):
        return remote(
            sent.at[pl.ds(pl.multiple_of(owned * come, owned), owned), :], got.at[come], p_send.at[come], p_recv.at[come], come
        )

    def project(i):
        block = ahead(m // per, i, 4)
        at = block * span + lax.broadcasted_iota(jnp.int32, (span, REQ * QMAX), 0)
        source = QMAX * ((at >> 2) & 3) + 4 * (at >> 4) + (at & 3)
        pick = (source == lax.broadcasted_iota(jnp.int32, (span, REQ * QMAX), 1)).astype(jnp.bfloat16)
        total = None
        for g in range(RING // REQ):
            chosen = jnp.dot(
                pick,
                attended[REQ * g : REQ * (g + 1)].reshape(REQ * QMAX, GROUP * HD),
                preferred_element_type=jnp.float32,
            ).astype(jnp.bfloat16)
            term = jnp.dot(
                chosen,
                w[REQ * g : REQ * (g + 1)].reshape(GROUP * HD, WIDTH),
                preferred_element_type=jnp.float32,
            )
            total = term if total is None else total + term
        sent[pl.ds(pl.multiple_of(block * span, span), span), :] = total.astype(jnp.bfloat16)

        def ship(t):
            to = block * per + ahead(m, t, per)

            @pl.when(to != m)
            def _():
                p_copy(to).start()

            @pl.when(to == m)
            def _():
                p_own().start()

        loop(0, per, ship)

    loop(0, 4, project)
    p_own().wait()
    loop(1, SHARDS, lambda i: p_arrival(ahead(m, i, SHARDS)).wait_recv())

    for c in range(RING):
        cols = slice(c * WIDTH, (c + 1) * WIDTH)
        value = got[c].astype(jnp.float32)
        for group in range(1, SHARDS // RING):
            value = value + got[RING * group + c].astype(jnp.float32)
        for b in range(REQ):
            mixed[b, :, cols] = value[b * TOKENS : (b + 1) * TOKENS] + hidden[b, :, cols].astype(jnp.float32)

    for hf in range(2):
        for at, n in order:
            for copy in mate_copies(at, 2 * hf + n):
                copy.wait_send()
        for copy in chip_copies(hf):
            copy.wait_send()
        g_copy(place, 0, hf, mate).wait_send()
        for n, hop in enumerate(hops):
            g_copy(place, 1 + n, hf, mate).wait_send()
            g_copy(ahead(place, RING - hop, RING), 4 + n, hf, mate).wait_send()
    loop(1, SHARDS, lambda i: p_copy(ahead(m, i, SHARDS)).wait_send())


def merge(part, lse, w_own, w_all, hidden):
    bf, f32 = jnp.bfloat16, jnp.float32
    dma = pltpu.SemaphoreType.DMA
    owned = OWNED
    return pl.pallas_call(
        merge_kernel,
        out_shape=jax.ShapeDtypeStruct((REQ, TOKENS, D), f32),
        in_specs=[VMEM, VMEM, HBM, HBM, VMEM],
        out_specs=VMEM,
        scratch_shapes=[
            pltpu.VMEM((RING, D // SHARDS, WIDTH), bf),
            pltpu.VMEM((2, ROWS, HD), bf),
            pltpu.VMEM((2, 8, ROWS), f32),
            pltpu.VMEM((ROWS, HD), bf),
            pltpu.VMEM((8, ROWS), f32),
            pltpu.VMEM((ROWS, HD), bf),
            pltpu.VMEM((8, ROWS), f32),
            pltpu.VMEM((ROWS, HD), f32),
            pltpu.VMEM((RING, QMAX, GROUP * HD), bf),
            pltpu.VMEM((REQ * QMAX, WIDTH), bf),
            pltpu.VMEM((SHARDS, owned, WIDTH), bf),
            dma((RING,)), dma,
            dma((6,)), dma((6,)),
            dma((6,)), dma((6,)),
            dma((2, 7)), dma((2, 7)),
            dma((SHARDS,)), dma((SHARDS,)),
        ],
        compiler_params=pltpu.CompilerParams(
            collective_id=1, has_side_effects=True, vmem_limit_bytes=52 << 20
        ),
        name="merge",
    )(part, lse, w_own, w_all, hidden)


def on_device(
    kv_store, retrieval, positions, lengths, queries, new_kv, hidden, out_weight, norm_gain
):
    context = R * CTOK
    cos_own, sin_own = turns(np.arange(context, context + QMAX))
    shape = (SHARDS, TOKENS, HD)
    wanted = jnp.transpose(retrieval)
    kv_all, q_all, fresh_all, w_all = spread(
        wanted, kv_store, queries, new_kv, cos_own.reshape(shape), sin_own.reshape(shape), out_weight
    )
    cos_at, sin_at = turns(np.arange(R) * CTOK)
    part, lse = attend(
        wanted, positions, lengths, cos_at, sin_at, q_all.reshape(REQ, ROWS, HD),
        fresh_all.reshape(KVH * 16, 2 * HD),
        kv_all,
    )
    mixed = merge(part, lse, out_weight, w_all, hidden)
    square = jnp.mean(mixed * mixed, axis=-1, keepdims=True)
    normed = mixed * lax.rsqrt(square + eps_norm) * norm_gain.astype(jnp.float32)
    return mixed.astype(jnp.bfloat16), normed.astype(jnp.bfloat16)


def solution(mesh):
    return jax.shard_map(
        on_device,
        mesh=mesh,
        in_specs=(
            P("store", "mp", None),
            P(),
            P("store", None),
            P("store"),
            P("store", "mp", None),
            P("store", "mp", None),
            P("store", "mp", None),
            P("mp", None),
            P(),
        ),
        out_specs=(P("store", "mp", None), P("store", "mp", None)),
        check_vma=False,
    )
```

```python
import jax
import jax.numpy as jnp
import numpy as np
from jax import lax
from jax.experimental import pallas as pl
from jax.experimental.pallas import tpu as pltpu
from jax.sharding import PartitionSpec as P

MESH = pl.DeviceIdType.MESH
HBM = pl.BlockSpec(memory_space=pltpu.HBM)
VMEM = pl.BlockSpec(memory_space=pltpu.VMEM)
SMEM = pl.BlockSpec(memory_space=pltpu.SMEM)

STORES = 8
SHARDS = 32
HEADS = 64
KVH = 8
GROUP = 8
HD = 128
D = 8192
QUARTERS = 4
CTOK = 512
R = 8
REQ = 4
QMAX = 128
HELD = 16
CHUNKS = 4
PART = CTOK // 4 // CHUNKS
CAP = 8
WINDOW = 6
STEPS = 2
STEP = HELD // STEPS
EARLY = 3
PLACES = 5 * HELD + 3 * CAP
RING = 8
WIDTH = D // RING
ROWS = QMAX * GROUP
HALF = ROWS // 2
BLOCK = 512
SUB = 256
TOKENS = QMAX // SHARDS
OWNED = REQ * TOKENS
LOG2E = 1.4426950408889634

theta_base = 1000000.0
eps_norm = 1e-06


def turns(places):
    inv_freq = np.float32(theta_base) ** (-(np.arange(HD // 2, dtype=np.float32) * np.float32(2.0)) / np.float32(HD))
    angles = np.asarray(places, np.float32)[..., None] * inv_freq
    cosines, sines = np.cos(angles), np.sin(angles)
    return (
        jnp.asarray(np.concatenate([cosines, cosines], axis=-1)),
        jnp.asarray(np.concatenate([-sines, sines], axis=-1)),
    )


def rotate(field_in, cosines, sines):
    return field_in * cosines + pltpu.roll(field_in, HD // 2, 1) * sines


def ahead(a, b, n):
    return lax.rem(a + b, n)


def spread_kernel(
    retrieval, kv, queries, new_kv, cosines, sines, w, kv_all, q_all, fresh_all, w_all,
    q_wide, q, fresh_wide, fresh, near, packed, packed_far, relay, near_sem, own_sem, kv_send, kv_recv, q_send, q_recv, f_send, f_recv, w_send, w_recv, o_send, o_recv, z_send, z_recv,
):
    m = lax.axis_index("mp")
    z = lax.axis_index("store")
    k = m // QUARTERS
    j = lax.rem(m, QUARTERS)
    right, left = ahead(z, 1, STORES), ahead(z, STORES - 1, STORES)

    barrier = pltpu.get_barrier_semaphore()

    def greet(i, carry):
        pl.semaphore_signal(barrier, 1, device_id={"mp": ahead(m, i, SHARDS)}, device_id_type=MESH)
        return carry

    lax.fori_loop(1, SHARDS, greet, 0)
    for beside in (left, right):
        pl.semaphore_signal(barrier, 1, device_id={"store": beside}, device_id_type=MESH)
    pl.semaphore_wait(barrier, SHARDS + 1)

    def remote(src, dst, send, recv, **where):
        return pltpu.make_async_remote_copy(
            src_ref=src, dst_ref=dst, send_sem=send, recv_sem=recv, device_id=where, device_id_type=MESH
        )

    def kv_rows(base, n, i):
        return kv_all.at[pl.ds(base + STEP * n, STEP), pl.ds(16 * i, 16), :]

    def kv_part(n, head):
        return kv.at[pl.ds(STEP * n, STEP), :, pl.ds(pl.multiple_of(2 * HD * head, 2 * HD), 2 * HD)]

    def kv_copy(n, i):
        to = ahead(k, KVH - i, KVH)
        return remote(
            kv_part(n, to), kv_rows(0, n, i), kv_send.at[n, i], kv_recv.at[n, i], mp=QUARTERS * to + j
        )

    def own_kv(n):
        return pltpu.make_async_copy(kv_part(n, k), kv_rows(0, n, 0), own_sem.at[2 + n])

    for n in range(STEPS):
        for i in range(1, KVH):
            kv_copy(n, i).start()

    target = (right, left)

    def rows_of(c):
        return pl.ds(PART * c, PART)

    def held(base, count, c):
        return kv_all.at[pl.ds(base, count), rows_of(c)]

    def z_own(way, n, i):
        src = kv_part(n, k) if i == 0 else kv_rows(0, n, i)
        dst = kv_rows(HELD * (1 + way), n, i)
        return remote(src, dst, o_send.at[way, n, i], o_recv.at[way, n, i], store=target[way])

    def z_copy(way, s, c):
        if s == 1:
            src, dst = held(HELD * (1 + way), HELD, c), near[way * CHUNKS + c]
        elif s == 2:
            src, dst = packed.at[way, c], held(5 * HELD + CAP * way, CAP, c)
        elif s == 3:
            src, dst = packed_far.at[way, c % 2], relay.at[way, c % 2]
        else:
            src, dst = relay.at[way, c % 2], held(5 * HELD + 2 * CAP, CAP, c)
        return remote(src, dst, z_send.at[way, s, c], z_recv.at[way, s, c], store=target[way])

    def fresh_part(head):
        return fresh.at[:, pl.ds(pl.multiple_of(2 * HD * head, 2 * HD), 2 * HD)]

    def f_copy(i):
        to = ahead(k, i, KVH)
        return remote(fresh_part(to), fresh_all.at[k], f_send.at[i], f_recv.at[k], mp=QUARTERS * to + j)

    def f_arrival(i):
        come = ahead(k, i, KVH)
        return remote(fresh_part(come), fresh_all.at[come], f_send.at[i], f_recv.at[come], mp=QUARTERS * come + j)

    def q_copy(i):
        to = ahead(m, i, SHARDS)
        return remote(q.at[to // QUARTERS], q_all.at[:, m], q_send.at[i], q_recv.at[m], mp=to)

    def q_arrival(i):
        come = ahead(m, i, SHARDS)
        return remote(q.at[k], q_all.at[:, come], q_send.at[i], q_recv.at[come], mp=come)

    ring = RING * (m // RING)
    place = lax.rem(m, RING)

    def w_part(block):
        return w.at[:, pl.ds(pl.multiple_of(WIDTH * block, WIDTH), WIDTH)]

    def w_copy(i):
        to = ahead(place, i, RING)
        return remote(w_part(to), w_all.at[place], w_send.at[i], w_recv.at[place], mp=ring + to)

    def w_arrival(i):
        come = ahead(place, i, RING)
        return remote(w_part(come), w_all.at[come], w_send.at[i], w_recv.at[come], mp=ring + come)

    own = [
        pltpu.make_async_copy(fresh_part(k), fresh_all.at[k], own_sem.at[0]),
        pltpu.make_async_copy(q.at[k], q_all.at[:, m], own_sem.at[1]),
    ]

    def loop(low, high, act):
        def body(i, carry):
            act(i)
            return carry

        lax.fori_loop(low, high, body, 0)

    sent = ([], [])

    def push(way, copy):
        if len(sent[way]) >= WINDOW:
            sent[way][-WINDOW].wait_send()
        copy.start()
        sent[way].append(copy)

    def push_own(n, i):
        if i > 0:
            kv_copy(n, i).wait_recv()
        for way in range(2):
            push(way, z_own(way, n, i))

    for n in range(STEPS):
        push_own(n, 0)
    for n in range(STEPS):
        own_kv(n).start()
    for i in range(1, EARLY):
        push_own(0, i)
    loop(1, RING, lambda i: w_copy(i).start())

    cos, sin = cosines[m], sines[m]

    def turn(head):
        for b in range(REQ):
            for g in range(GROUP):
                at = pl.ds(pl.multiple_of((head * GROUP + g) * HD, HD), HD)
                value = rotate(queries[b, :, at].astype(jnp.float32), cos, sin)
                q_wide[head, b, pl.ds(g, TOKENS, stride=GROUP), :] = value * (HD**-0.5 * LOG2E)
            at = pl.multiple_of(2 * HD * head, 2 * HD)
            key = rotate(new_kv[b, :, pl.ds(at, HD)].astype(jnp.float32), cos, sin)
            fresh_wide[b * TOKENS : (b + 1) * TOKENS, pl.ds(at, HD)] = key
            at = pl.multiple_of(at + HD, HD)
            fresh_wide[b * TOKENS : (b + 1) * TOKENS, pl.ds(at, HD)] = new_kv[b, :, pl.ds(at, HD)].astype(jnp.float32)
        q[head] = q_wide[head].astype(jnp.bfloat16)

    loop(0, KVH, turn)
    fresh[...] = fresh_wide[...].astype(jnp.bfloat16)
    for copy in own:
        copy.start()
    loop(1, KVH, lambda i: f_copy(i).start())
    loop(1, SHARDS, lambda i: q_copy(i).start())
    for i in range(EARLY, KVH):
        push_own(0, i)
    for n in range(1, STEPS):
        for i in range(1, KVH):
            push_own(n, i)
    for n in range(STEPS):
        own_kv(n).wait()

    def wanted(dest, source):
        def look(n, carry):
            count, picks = carry
            found = retrieval[lax.rem(n, R), dest * REQ + n // R]
            hit = (found >> 4) == source
            picks = tuple(
                jnp.where(hit & (count == at), found & (HELD - 1), pick) for at, pick in enumerate(picks)
            )
            return jnp.where(hit, count + 1, count), picks

        zero = jnp.int32(0)
        return lax.fori_loop(0, REQ * R, look, (zero, (zero,) * CAP))[1]

    picks = [wanted(ahead(z, 1, STORES), ahead(z, 6, STORES)), wanted(ahead(z, 7, STORES), ahead(z, 2, STORES))]
    far_picks = [wanted(ahead(z, 2, STORES), ahead(z, 6, STORES)), wanted(ahead(z, 6, STORES), ahead(z, 2, STORES))]

    halves = (range(CHUNKS // 2), range(CHUNKS // 2, CHUNKS))
    for c in range(CHUNKS):
        for way in range(2):
            for i in range(2 * c, 2 * c + 2):
                for n in range(STEPS):
                    z_own(way, n, i).wait_recv()
            push(way, z_copy(way, 1, c))

    def keep(way, c):
        return pltpu.make_async_copy(
            near[way * CHUNKS + c], held(HELD * (3 + way), HELD, c), near_sem.at[way, c]
        )

    for c in range(CHUNKS):
        for way in range(2):
            z_copy(way, 1, c).wait_recv()
            source = near[way * CHUNKS + c]
            for at in range(CAP):
                packed[way, c, at] = source[picks[way][at]]
            push(way, z_copy(way, 2, c))
            if c in halves[way]:
                for at in range(CAP):
                    packed_far[way, c % 2, at] = source[far_picks[way][at]]
                push(way, z_copy(way, 3, c))
            keep(way, c).start()
    for n in range(CHUNKS // 2):
        for way in range(2):
            z_copy(way, 3, halves[way][n]).wait_recv()
            push(way, z_copy(way, 4, halves[way][n]))
    for c in range(CHUNKS):
        for way in range(2):
            keep(way, c).wait()
            z_copy(way, 2, c).wait_recv()
            if c in halves[way]:
                z_copy(way, 4, c).wait_recv()

    for copy in own:
        copy.wait()
    loop(1, RING, lambda i: w_arrival(i).wait_recv())
    loop(1, KVH, lambda i: f_arrival(i).wait_recv())
    loop(1, SHARDS, lambda i: q_arrival(i).wait_recv())
    loop(1, RING, lambda i: w_copy(i).wait_send())
    loop(1, KVH, lambda i: f_copy(i).wait_send())
    loop(1, SHARDS, lambda i: q_copy(i).wait_send())
    for n in range(STEPS):
        for i in range(1, KVH):
            kv_copy(n, i).wait_send()
    for copies in sent:
        for copy in copies[-WINDOW:]:
            copy.wait_send()


def spread(retrieval, kv, queries, new_kv, cosines, sines, w):
    bf, f32 = jnp.bfloat16, jnp.float32
    dma = pltpu.SemaphoreType.DMA
    return pl.pallas_call(
        spread_kernel,
        out_shape=(
            jax.ShapeDtypeStruct((PLACES, CTOK // QUARTERS, 2 * HD), bf),
            jax.ShapeDtypeStruct((REQ, SHARDS, QMAX // SHARDS * GROUP, HD), bf),
            jax.ShapeDtypeStruct((KVH, 16, 2 * HD), bf),
            jax.ShapeDtypeStruct((RING, D // SHARDS, WIDTH), bf),
        ),
        in_specs=[SMEM, HBM] + [VMEM] * 4 + [HBM],
        out_specs=(HBM,) * 4,
        scratch_shapes=[
            pltpu.VMEM((KVH, REQ, TOKENS * GROUP, HD), f32),
            pltpu.VMEM((KVH, REQ, TOKENS * GROUP, HD), bf),
            pltpu.VMEM((OWNED, KVH * 2 * HD), f32),
            pltpu.VMEM((OWNED, KVH * 2 * HD), bf),
            [pltpu.VMEM((HELD, PART, 2 * HD), bf)] * (2 * CHUNKS),
            pltpu.VMEM((2, CHUNKS, CAP, PART, 2 * HD), bf),
            pltpu.VMEM((2, CHUNKS // 2, CAP, PART, 2 * HD), bf),
            pltpu.VMEM((2, CHUNKS // 2, CAP, PART, 2 * HD), bf),
            dma((2, CHUNKS)),
            dma((2 + STEPS,)),
            dma((STEPS, KVH)), dma((STEPS, KVH)),
            dma((SHARDS,)), dma((SHARDS,)),
            dma((KVH,)), dma((KVH,)),
            dma((RING,)), dma((RING,)),
            dma((2, STEPS, KVH)), dma((2, STEPS, KVH)),
            dma((2, 5, CHUNKS)), dma((2, 5, CHUNKS)),
        ],
        compiler_params=pltpu.CompilerParams(
            collective_id=0, has_side_effects=True, vmem_limit_bytes=60 << 20
        ),
        name="spread",
    )(retrieval, kv, queries, new_kv, cosines, sines, w)


def attend_kernel(
    retrieval, places, lengths, cosines, sines, q_all, fresh_all, kv_all, out, lse,
    slots, keys, q, fresh, counts, sem, q_sem, fresh_sem,
):
    quarter = CTOK // QUARTERS
    held = R * quarter
    j = lax.rem(lax.axis_index("mp"), QUARTERS)
    z = lax.axis_index("store")

    def fetch(b, r, place=0):
        return pltpu.make_async_copy(
            kv_all.at[place], slots.at[b, pl.ds(r * quarter, quarter)], sem.at[b, r]
        )

    for s in range(STORES):
        counts[s] = 0

    def locate(b, r):
        found = retrieval[r, z * REQ + b]
        apart = ((found >> 4) - z) & (STORES - 1)
        rank = counts[apart]
        counts[apart] = rank + 1
        near = HELD * jnp.where(apart <= 2, 2 * apart, 2 * (STORES - apart) - 1) + (found & (HELD - 1))
        far = 5 * HELD + CAP * jnp.where(apart == 5, 0, jnp.where(apart == 3, 1, 2)) + rank
        return jnp.where((apart <= 2) | (apart >= 6), near, far)

    def fetch_q(b):
        return pltpu.make_async_copy(q_all.at[b], q.at[b], q_sem.at[b])

    fetch_fresh = pltpu.make_async_copy(fresh_all, fresh, fresh_sem)
    for b in range(REQ):
        for r in range(R):
            fetch(b, r, locate(b, r)).start()
        fetch_q(b).start()
        if b == 0:
            fetch_fresh.start()
    fetch_fresh.wait()
    for b in range(REQ):
        slots[b, held:, :] = fresh[...]
    keys[held:, :] = fresh[:, :HD]
    col = lax.broadcasted_iota(jnp.int32, (SUB, quarter), 1)
    fresh_token = TOKENS * (QUARTERS * (col >> 4) + j) + (col & 3)
    fresh_request = (col >> 2) & 3
    row = lax.broadcasted_iota(jnp.int32, (SUB, quarter), 0)
    for b in range(REQ):
        for r in range(R):
            fetch(b, r).wait()
        for r in range(R):
            at = places[b, r]
            key = slots[b, r * quarter : (r + 1) * quarter, :HD].astype(jnp.float32)
            key = rotate(key, cosines[pl.ds(at, 1), :], sines[pl.ds(at, 1), :])
            keys[r * quarter : (r + 1) * quarter, :] = key.astype(jnp.bfloat16)
        fetch_q(b).wait()
        length = lengths[b]

        def block(i, carry):
            spans = [pl.ds(pl.multiple_of(i * BLOCK + n * SUB, SUB), SUB) for n in range(BLOCK // SUB)]
            every = [
                lax.dot_general(
                    q[b, span, :], keys[...], (((1,), (1,)), ((), ())), preferred_element_type=jnp.float32
                )
                for span in spans
            ]
            for n, (span, scores) in enumerate(zip(spans, every)):
                at = i * BLOCK + n * SUB + row
                allowed = (fresh_request == b) & (fresh_token <= (at >> 3))
                scores = jnp.concatenate(
                    [scores[:, :held], jnp.where(allowed, scores[:, held:], -1e30)], axis=1
                )
                top = jnp.max(scores, axis=1, keepdims=True)
                expo = jnp.exp2(scores - top)
                total = jnp.sum(expo, axis=1, keepdims=True)
                sums = jnp.dot(
                    expo.astype(jnp.bfloat16), slots[b, :, HD:], preferred_element_type=jnp.float32
                )
                out[b, span, :] = jnp.where(at < length * GROUP, sums / total, 0.0).astype(jnp.bfloat16)
                logs = top + jnp.log(total) * LOG2E
                lse[b, :, span] = jnp.broadcast_to(logs, (SUB, HD)).T[:8]
            return carry

        def blank(i, carry):
            span = pl.ds(pl.multiple_of(i * BLOCK, BLOCK), BLOCK)
            out[b, span, :] = jnp.zeros((BLOCK, HD), jnp.bfloat16)
            lse[b, :, span] = jnp.zeros((8, BLOCK), jnp.float32)
            return carry

        used = (length * GROUP + BLOCK - 1) // BLOCK
        lax.fori_loop(0, used, block, 0)
        lax.fori_loop(used, ROWS // BLOCK, blank, 0)


def attend(retrieval, places, lengths, cosines, sines, q_all, fresh_all, kv_all):
    quarter = CTOK // QUARTERS
    bf = jnp.bfloat16
    dma = pltpu.SemaphoreType.DMA
    return pl.pallas_call(
        attend_kernel,
        out_shape=(
            jax.ShapeDtypeStruct((REQ, ROWS, HD), bf),
            jax.ShapeDtypeStruct((REQ, 8, ROWS), jnp.float32),
        ),
        in_specs=[SMEM] * 3 + [VMEM] * 2 + [HBM] * 3,
        out_specs=(VMEM, VMEM),
        scratch_shapes=[
            pltpu.VMEM((REQ, (R + 1) * quarter, 2 * HD), bf),
            pltpu.VMEM(((R + 1) * quarter, HD), bf),
            pltpu.VMEM((REQ, ROWS, HD), bf),
            pltpu.VMEM((quarter, 2 * HD), bf),
            pltpu.SMEM((STORES,), jnp.int32),
            dma((REQ, R)), dma((REQ,)), dma,
        ],
        compiler_params=pltpu.CompilerParams(vmem_limit_bytes=60 << 20),
        name="attend",
    )(retrieval, places, lengths, cosines, sines, q_all, fresh_all, kv_all)


def merge_kernel(
    part, lse, w_own, w_all, hidden, mixed,
    w, from_mate, from_mate_lse, pair, pair_lse, from_chip, from_chip_lse, rows, attended, sent, got,
    w_sem, own_sem, c_send, c_recv, l_send, l_recv, g_send, g_recv, p_send, p_recv,
):
    m = lax.axis_index("mp")
    k = m // QUARTERS
    j = lax.rem(m, QUARTERS)
    core, half = lax.rem(j, 2), j // 2
    mate, chip = m + 1 - 2 * core, QUARTERS * k + ahead(j, 2, QUARTERS)
    ring = RING * (m // RING)
    place = lax.rem(m, RING)
    w_loads = [
        pltpu.make_async_copy(
            w_own.at[:, pl.ds(pl.multiple_of(WIDTH * place, WIDTH), WIDTH)], w.at[place], w_sem.at[0]
        )
    ]
    for i in range(1, RING):
        come = ahead(place, i, RING)
        w_loads.append(pltpu.make_async_copy(w_all.at[come], w.at[come], w_sem.at[i]))
    for load in w_loads:
        load.start()

    barrier = pltpu.get_barrier_semaphore()

    def loop(low, high, act):
        def body(i, carry):
            act(i)
            return carry

        lax.fori_loop(low, high, body, 0)

    loop(
        1,
        SHARDS,
        lambda i: pl.semaphore_signal(
            barrier, 1, device_id={"mp": ahead(m, i, SHARDS)}, device_id_type=MESH
        ),
    )
    pl.semaphore_wait(barrier, SHARDS - 1)

    def remote(src, dst, send, recv, to):
        return pltpu.make_async_remote_copy(
            src_ref=src, dst_ref=dst, send_sem=send, recv_sem=recv, device_id={"mp": to}, device_id_type=MESH
        )

    def mate_copies(at, n):
        give = 1 - core + 2 * at
        span = pl.ds(n // 2 * HALF, HALF)
        return (
            remote(lse.at[give, :, span], from_mate_lse.at[at, :, span], l_send.at[n], l_recv.at[n], mate),
            remote(part.at[give, span], from_mate.at[at, span], c_send.at[n], c_recv.at[n], mate),
        )

    def chip_copies(n):
        span = pl.ds(n * HALF, HALF)
        return (
            remote(pair_lse.at[:, span], from_chip_lse.at[:, span], l_send.at[4 + n], l_recv.at[4 + n], chip),
            remote(pair.at[span], from_chip.at[span], c_send.at[4 + n], c_recv.at[4 + n], chip),
        )

    def combine(one, one_log, two, two_log):
        top = jnp.maximum(one_log, two_log)
        one_share, two_share = jnp.exp2(one_log - top), jnp.exp2(two_log - top)
        total = one_share + two_share
        share = jnp.broadcast_to(one_share / total, (HD, HALF)).T
        return two + (one - two) * share, top + jnp.log(total) * LOG2E

    def with_mate(at, n):
        span = slice(n * HALF, (n + 1) * HALF)
        keep = core + 2 * at
        return combine(
            part[keep, span].astype(jnp.float32), lse[keep, :1, span],
            from_mate[at, span].astype(jnp.float32), from_mate_lse[at, :1, span],
        )

    def g_copy(at, n, hf, to):
        block = attended.at[at, pl.ds(hf * (QMAX // 2), QMAX // 2)]
        return remote(block, block, g_send.at[hf, n], g_recv.at[hf, n], to)

    other = 1 - half
    order = ((other, 0), (half, 1))
    hops = (2, 6, 4)
    mate_place = place + 1 - 2 * core
    for hf in range(2):
        for at, n in order:
            for copy in mate_copies(at, 2 * hf + n):
                copy.start()
    for hf in range(2):
        for copy in mate_copies(other, 2 * hf):
            copy.wait_recv()
        value, logs = with_mate(other, hf)
        pair[hf * HALF : (hf + 1) * HALF, :] = value.astype(jnp.bfloat16)
        pair_lse[:, hf * HALF : (hf + 1) * HALF] = jnp.broadcast_to(logs, (8, HALF))
        for copy in chip_copies(hf):
            copy.start()
    kept = []
    for hf in range(2):
        for copy in mate_copies(half, 2 * hf + 1):
            copy.wait_recv()
        value, logs = with_mate(half, hf)
        rows[hf * HALF : (hf + 1) * HALF, :] = value
        kept.append(logs)
    for hf in range(2):
        span = slice(hf * HALF, (hf + 1) * HALF)
        for copy in chip_copies(hf):
            copy.wait_recv()
        rows[span, :] = combine(
            rows[span, :], kept[hf], from_chip[span].astype(jnp.float32), from_chip_lse[:1, span]
        )[0]
        for h in range(GROUP):
            attended[place, hf * (QMAX // 2) : (hf + 1) * (QMAX // 2), h * HD : (h + 1) * HD] = rows[
                pl.ds(hf * HALF + h, QMAX // 2, stride=GROUP), :
            ].astype(jnp.bfloat16)
        for n, hop in enumerate(hops):
            g_copy(place, 1 + n, hf, ring + ahead(place, hop, RING)).start()
        g_copy(place, 0, hf, mate).start()
    for load in w_loads:
        load.wait()
    for hf in range(2):
        for n, hop in enumerate(hops):
            come = ahead(place, RING - hop, RING)
            g_copy(come, 1 + n, hf, mate).wait_recv()
            g_copy(come, 4 + n, hf, mate).start()
    for hf in range(2):
        g_copy(mate_place, 0, hf, mate).wait_recv()
        for n, hop in enumerate(hops):
            g_copy(ahead(mate_place, RING - hop, RING), 4 + n, hf, mate).wait_recv()

    owned = OWNED
    span = REQ * QMAX // 4
    per = span // owned

    def p_copy(to):
        return remote(
            sent.at[pl.ds(pl.multiple_of(owned * to, owned), owned), :], got.at[m], p_send.at[to], p_recv.at[m], to
        )

    def p_own():
        return pltpu.make_async_copy(
            sent.at[pl.ds(pl.multiple_of(owned * m, owned), owned), :], got.at[m], own_sem
        )

    def p_arrival(come):
        return remote(
            sent.at[pl.ds(pl.multiple_of(owned * come, owned), owned), :], got.at[come], p_send.at[come], p_recv.at[come], come
        )

    def project(i):
        block = ahead(m // per, i + 2, 4)
        at = block * span + lax.broadcasted_iota(jnp.int32, (span, REQ * QMAX), 0)
        source = QMAX * ((at >> 2) & 3) + 4 * (at >> 4) + (at & 3)
        pick = (source == lax.broadcasted_iota(jnp.int32, (span, REQ * QMAX), 1)).astype(jnp.bfloat16)
        total = None
        for g in range(RING // REQ):
            chosen = jnp.dot(
                pick,
                attended[REQ * g : REQ * (g + 1)].reshape(REQ * QMAX, GROUP * HD),
                preferred_element_type=jnp.float32,
            ).astype(jnp.bfloat16)
            term = jnp.dot(
                chosen,
                w[REQ * g : REQ * (g + 1)].reshape(GROUP * HD, WIDTH),
                preferred_element_type=jnp.float32,
            )
            total = term if total is None else total + term
        sent[pl.ds(pl.multiple_of(block * span, span), span), :] = total.astype(jnp.bfloat16)

        def ship(t):
            to = block * per + ahead(m, t, per)

            @pl.when(to != m)
            def _():
                p_copy(to).start()

            @pl.when(to == m)
            def _():
                p_own().start()

        loop(0, per, ship)

    loop(0, 4, project)
    p_own().wait()
    loop(1, SHARDS, lambda i: p_arrival(ahead(m, i, SHARDS)).wait_recv())

    for c in range(RING):
        cols = slice(c * WIDTH, (c + 1) * WIDTH)
        value = got[c].astype(jnp.float32)
        for group in range(1, SHARDS // RING):
            value = value + got[RING * group + c].astype(jnp.float32)
        for b in range(REQ):
            mixed[b, :, cols] = value[b * TOKENS : (b + 1) * TOKENS] + hidden[b, :, cols].astype(jnp.float32)

    for hf in range(2):
        for at, n in order:
            for copy in mate_copies(at, 2 * hf + n):
                copy.wait_send()
        for copy in chip_copies(hf):
            copy.wait_send()
        g_copy(place, 0, hf, mate).wait_send()
        for n, hop in enumerate(hops):
            g_copy(place, 1 + n, hf, mate).wait_send()
            g_copy(ahead(place, RING - hop, RING), 4 + n, hf, mate).wait_send()
    loop(1, SHARDS, lambda i: p_copy(ahead(m, i, SHARDS)).wait_send())


def merge(part, lse, w_own, w_all, hidden):
    bf, f32 = jnp.bfloat16, jnp.float32
    dma = pltpu.SemaphoreType.DMA
    owned = OWNED
    return pl.pallas_call(
        merge_kernel,
        out_shape=jax.ShapeDtypeStruct((REQ, TOKENS, D), f32),
        in_specs=[VMEM, VMEM, HBM, HBM, VMEM],
        out_specs=VMEM,
        scratch_shapes=[
            pltpu.VMEM((RING, D // SHARDS, WIDTH), bf),
            pltpu.VMEM((2, ROWS, HD), bf),
            pltpu.VMEM((2, 8, ROWS), f32),
            pltpu.VMEM((ROWS, HD), bf),
            pltpu.VMEM((8, ROWS), f32),
            pltpu.VMEM((ROWS, HD), bf),
            pltpu.VMEM((8, ROWS), f32),
            pltpu.VMEM((ROWS, HD), f32),
            pltpu.VMEM((RING, QMAX, GROUP * HD), bf),
            pltpu.VMEM((REQ * QMAX, WIDTH), bf),
            pltpu.VMEM((SHARDS, owned, WIDTH), bf),
            dma((RING,)), dma,
            dma((6,)), dma((6,)),
            dma((6,)), dma((6,)),
            dma((2, 7)), dma((2, 7)),
            dma((SHARDS,)), dma((SHARDS,)),
        ],
        compiler_params=pltpu.CompilerParams(
            collective_id=1, has_side_effects=True, vmem_limit_bytes=52 << 20
        ),
        name="merge",
    )(part, lse, w_own, w_all, hidden)


def on_device(
    kv_store, retrieval, positions, lengths, queries, new_kv, hidden, out_weight, norm_gain
):
    context = R * CTOK
    cos_own, sin_own = turns(np.arange(context, context + QMAX))
    shape = (SHARDS, TOKENS, HD)
    wanted = jnp.transpose(retrieval)
    kv_all, q_all, fresh_all, w_all = spread(
        wanted, kv_store, queries, new_kv, cos_own.reshape(shape), sin_own.reshape(shape), out_weight
    )
    cos_at, sin_at = turns(np.arange(R) * CTOK)
    part, lse = attend(
        wanted, positions, lengths, cos_at, sin_at, q_all.reshape(REQ, ROWS, HD),
        fresh_all.reshape(KVH * 16, 2 * HD),
        kv_all,
    )
    mixed = merge(part, lse, out_weight, w_all, hidden)
    square = jnp.mean(mixed * mixed, axis=-1, keepdims=True)
    normed = mixed * lax.rsqrt(square + eps_norm) * norm_gain.astype(jnp.float32)
    return mixed.astype(jnp.bfloat16), normed.astype(jnp.bfloat16)


def solution(mesh):
    return jax.shard_map(
        on_device,
        mesh=mesh,
        in_specs=(
            P("store", "mp", None),
            P(),
            P("store", None),
            P("store"),
            P("store", "mp", None),
            P("store", "mp", None),
            P("store", "mp", None),
            P("mp", None),
            P(),
        ),
        out_specs=(P("store", "mp", None), P("store", "mp", None)),
        check_vma=False,
    )
```

```python
import jax
import jax.numpy as jnp
import numpy as np
from jax import lax
from jax.experimental import pallas as pl
from jax.experimental.pallas import tpu as pltpu
from jax.sharding import PartitionSpec as P

MESH = pl.DeviceIdType.MESH
HBM = pl.BlockSpec(memory_space=pltpu.HBM)
VMEM = pl.BlockSpec(memory_space=pltpu.VMEM)
SMEM = pl.BlockSpec(memory_space=pltpu.SMEM)

STORES = 8
SHARDS = 32
HEADS = 64
KVH = 8
GROUP = 8
HD = 128
D = 8192
QUARTERS = 4
CTOK = 512
R = 8
REQ = 4
QMAX = 128
HELD = 16
CHUNKS = 4
PART = CTOK // 4 // CHUNKS
CAP = 8
WINDOW = 6
STEPS = 2
STEP = HELD // STEPS
EARLY = 3
PLACES = 5 * HELD + 3 * CAP
RING = 8
WIDTH = D // RING
ROWS = QMAX * GROUP
HALF = ROWS // 2
BLOCK = 512
SUB = 256
TOKENS = QMAX // SHARDS
OWNED = REQ * TOKENS
LOG2E = 1.4426950408889634

theta_base = 1000000.0
eps_norm = 1e-06


def turns(places):
    inv_freq = np.float32(theta_base) ** (-(np.arange(HD // 2, dtype=np.float32) * np.float32(2.0)) / np.float32(HD))
    angles = np.asarray(places, np.float32)[..., None] * inv_freq
    cosines, sines = np.cos(angles), np.sin(angles)
    return (
        jnp.asarray(np.concatenate([cosines, cosines], axis=-1)),
        jnp.asarray(np.concatenate([-sines, sines], axis=-1)),
    )


def rotate(field_in, cosines, sines):
    return field_in * cosines + pltpu.roll(field_in, HD // 2, 1) * sines


def ahead(a, b, n):
    return lax.rem(a + b, n)


def spread_kernel(
    retrieval, kv, queries, new_kv, cosines, sines, w, kv_all, q_all, fresh_all, w_all,
    q_wide, q, fresh_wide, fresh, near, packed, packed_far, relay, near_sem, own_sem, kv_send, kv_recv, q_send, q_recv, f_send, f_recv, w_send, w_recv, o_send, o_recv, z_send, z_recv,
):
    m = lax.axis_index("mp")
    z = lax.axis_index("store")
    k = m // QUARTERS
    j = lax.rem(m, QUARTERS)
    right, left = ahead(z, 1, STORES), ahead(z, STORES - 1, STORES)

    barrier = pltpu.get_barrier_semaphore()

    def greet(i, carry):
        pl.semaphore_signal(barrier, 1, device_id={"mp": ahead(m, i, SHARDS)}, device_id_type=MESH)
        return carry

    lax.fori_loop(1, SHARDS, greet, 0)
    for beside in (left, right):
        pl.semaphore_signal(barrier, 1, device_id={"store": beside}, device_id_type=MESH)
    pl.semaphore_wait(barrier, SHARDS + 1)

    def remote(src, dst, send, recv, **where):
        return pltpu.make_async_remote_copy(
            src_ref=src, dst_ref=dst, send_sem=send, recv_sem=recv, device_id=where, device_id_type=MESH
        )

    def kv_rows(base, n, i):
        return kv_all.at[pl.ds(base + STEP * n, STEP), pl.ds(16 * i, 16), :]

    def kv_part(n, head):
        return kv.at[pl.ds(STEP * n, STEP), :, pl.ds(pl.multiple_of(2 * HD * head, 2 * HD), 2 * HD)]

    def kv_copy(n, i):
        to = ahead(k, KVH - i, KVH)
        return remote(
            kv_part(n, to), kv_rows(0, n, i), kv_send.at[n, i], kv_recv.at[n, i], mp=QUARTERS * to + j
        )

    def own_kv(n):
        return pltpu.make_async_copy(kv_part(n, k), kv_rows(0, n, 0), own_sem.at[2 + n])

    for n in range(STEPS):
        for i in range(1, KVH):
            kv_copy(n, i).start()

    target = (right, left)

    def rows_of(c):
        return pl.ds(PART * c, PART)

    def held(base, count, c):
        return kv_all.at[pl.ds(base, count), rows_of(c)]

    def z_own(way, n, i):
        src = kv_part(n, k) if i == 0 else kv_rows(0, n, i)
        dst = kv_rows(HELD * (1 + way), n, i)
        return remote(src, dst, o_send.at[way, n, i], o_recv.at[way, n, i], store=target[way])

    def z_copy(way, s, c):
        if s == 1:
            src, dst = held(HELD * (1 + way), HELD, c), near[way * CHUNKS + c]
        elif s == 2:
            src, dst = packed.at[way, c], held(5 * HELD + CAP * way, CAP, c)
        elif s == 3:
            src, dst = packed_far.at[way, c % 2], relay.at[way, c % 2]
        else:
            src, dst = relay.at[way, c % 2], held(5 * HELD + 2 * CAP, CAP, c)
        return remote(src, dst, z_send.at[way, s, c], z_recv.at[way, s, c], store=target[way])

    def fresh_part(head):
        return fresh.at[:, pl.ds(pl.multiple_of(2 * HD * head, 2 * HD), 2 * HD)]

    def f_copy(i):
        to = ahead(k, i, KVH)
        return remote(fresh_part(to), fresh_all.at[k], f_send.at[i], f_recv.at[k], mp=QUARTERS * to + j)

    def f_arrival(i):
        come = ahead(k, i, KVH)
        return remote(fresh_part(come), fresh_all.at[come], f_send.at[i], f_recv.at[come], mp=QUARTERS * come + j)

    def q_copy(i):
        to = ahead(m, i, SHARDS)
        return remote(q.at[to // QUARTERS], q_all.at[:, m], q_send.at[i], q_recv.at[m], mp=to)

    def q_arrival(i):
        come = ahead(m, i, SHARDS)
        return remote(q.at[k], q_all.at[:, come], q_send.at[i], q_recv.at[come], mp=come)

    ring = RING * (m // RING)
    place = lax.rem(m, RING)

    def w_part(block):
        return w.at[:, pl.ds(pl.multiple_of(WIDTH * block, WIDTH), WIDTH)]

    def w_copy(i):
        to = ahead(place, i, RING)
        return remote(w_part(to), w_all.at[place], w_send.at[i], w_recv.at[place], mp=ring + to)

    def w_arrival(i):
        come = ahead(place, i, RING)
        return remote(w_part(come), w_all.at[come], w_send.at[i], w_recv.at[come], mp=ring + come)

    own = [
        pltpu.make_async_copy(fresh_part(k), fresh_all.at[k], own_sem.at[0]),
        pltpu.make_async_copy(q.at[k], q_all.at[:, m], own_sem.at[1]),
    ]

    def loop(low, high, act):
        def body(i, carry):
            act(i)
            return carry

        lax.fori_loop(low, high, body, 0)

    sent = ([], [])

    def push(way, copy):
        if len(sent[way]) >= WINDOW:
            sent[way][-WINDOW].wait_send()
        copy.start()
        sent[way].append(copy)

    def push_own(n, i):
        if i > 0:
            kv_copy(n, i).wait_recv()
        for way in range(2):
            push(way, z_own(way, n, i))

    for n in range(STEPS):
        push_own(n, 0)
    for n in range(STEPS):
        own_kv(n).start()
    for i in range(1, EARLY):
        push_own(0, i)
    loop(1, RING, lambda i: w_copy(i).start())

    cos, sin = cosines[m], sines[m]

    def turn(head):
        for b in range(REQ):
            for g in range(GROUP):
                at = pl.ds(pl.multiple_of((head * GROUP + g) * HD, HD), HD)
                value = rotate(queries[b, :, at].astype(jnp.float32), cos, sin)
                q_wide[head, b, pl.ds(g, TOKENS, stride=GROUP), :] = value * (HD**-0.5 * LOG2E)
            at = pl.multiple_of(2 * HD * head, 2 * HD)
            key = rotate(new_kv[b, :, pl.ds(at, HD)].astype(jnp.float32), cos, sin)
            fresh_wide[b * TOKENS : (b + 1) * TOKENS, pl.ds(at, HD)] = key
            at = pl.multiple_of(at + HD, HD)
            fresh_wide[b * TOKENS : (b + 1) * TOKENS, pl.ds(at, HD)] = new_kv[b, :, pl.ds(at, HD)].astype(jnp.float32)
        q[head] = q_wide[head].astype(jnp.bfloat16)

    loop(0, KVH, turn)
    fresh[...] = fresh_wide[...].astype(jnp.bfloat16)
    for copy in own:
        copy.start()
    loop(1, KVH, lambda i: f_copy(i).start())
    loop(1, SHARDS, lambda i: q_copy(i).start())
    for i in range(EARLY, KVH):
        push_own(0, i)
    for n in range(1, STEPS):
        for i in range(1, KVH):
            push_own(n, i)
    for n in range(STEPS):
        own_kv(n).wait()

    def wanted(dest, source):
        def look(n, carry):
            count, picks = carry
            found = retrieval[lax.rem(n, R), dest * REQ + n // R]
            hit = (found >> 4) == source
            picks = tuple(
                jnp.where(hit & (count == at), found & (HELD - 1), pick) for at, pick in enumerate(picks)
            )
            return jnp.where(hit, count + 1, count), picks

        zero = jnp.int32(0)
        return lax.fori_loop(0, REQ * R, look, (zero, (zero,) * CAP))[1]

    picks = [wanted(ahead(z, 1, STORES), ahead(z, 6, STORES)), wanted(ahead(z, 7, STORES), ahead(z, 2, STORES))]
    far_picks = [wanted(ahead(z, 2, STORES), ahead(z, 6, STORES)), wanted(ahead(z, 6, STORES), ahead(z, 2, STORES))]

    halves = (range(CHUNKS // 2), range(CHUNKS // 2, CHUNKS))
    for c in range(CHUNKS):
        for way in range(2):
            for i in range(2 * c, 2 * c + 2):
                for n in range(STEPS):
                    z_own(way, n, i).wait_recv()
            push(way, z_copy(way, 1, c))

    def keep(way, c):
        return pltpu.make_async_copy(
            near[way * CHUNKS + c], held(HELD * (3 + way), HELD, c), near_sem.at[way, c]
        )

    for c in range(CHUNKS):
        for way in range(2):
            z_copy(way, 1, c).wait_recv()
            source = near[way * CHUNKS + c]
            for at in range(CAP):
                packed[way, c, at] = source[picks[way][at]]
            push(way, z_copy(way, 2, c))
            if c in halves[way]:
                for at in range(CAP):
                    packed_far[way, c % 2, at] = source[far_picks[way][at]]
                push(way, z_copy(way, 3, c))
            keep(way, c).start()
    for n in range(CHUNKS // 2):
        for way in range(2):
            z_copy(way, 3, halves[way][n]).wait_recv()
            push(way, z_copy(way, 4, halves[way][n]))
    for c in range(CHUNKS):
        for way in range(2):
            keep(way, c).wait()
            z_copy(way, 2, c).wait_recv()
            if c in halves[way]:
                z_copy(way, 4, c).wait_recv()

    for copy in own:
        copy.wait()
    loop(1, RING, lambda i: w_arrival(i).wait_recv())
    loop(1, KVH, lambda i: f_arrival(i).wait_recv())
    loop(1, SHARDS, lambda i: q_arrival(i).wait_recv())
    loop(1, RING, lambda i: w_copy(i).wait_send())
    loop(1, KVH, lambda i: f_copy(i).wait_send())
    loop(1, SHARDS, lambda i: q_copy(i).wait_send())
    for n in range(STEPS):
        for i in range(1, KVH):
            kv_copy(n, i).wait_send()
    for copies in sent:
        for copy in copies[-WINDOW:]:
            copy.wait_send()


def spread(retrieval, kv, queries, new_kv, cosines, sines, w):
    bf, f32 = jnp.bfloat16, jnp.float32
    dma = pltpu.SemaphoreType.DMA
    return pl.pallas_call(
        spread_kernel,
        out_shape=(
            jax.ShapeDtypeStruct((PLACES, CTOK // QUARTERS, 2 * HD), bf),
            jax.ShapeDtypeStruct((REQ, SHARDS, QMAX // SHARDS * GROUP, HD), bf),
            jax.ShapeDtypeStruct((KVH, 16, 2 * HD), bf),
            jax.ShapeDtypeStruct((RING, D // SHARDS, WIDTH), bf),
        ),
        in_specs=[SMEM, HBM] + [VMEM] * 4 + [HBM],
        out_specs=(HBM,) * 4,
        scratch_shapes=[
            pltpu.VMEM((KVH, REQ, TOKENS * GROUP, HD), f32),
            pltpu.VMEM((KVH, REQ, TOKENS * GROUP, HD), bf),
            pltpu.VMEM((OWNED, KVH * 2 * HD), f32),
            pltpu.VMEM((OWNED, KVH * 2 * HD), bf),
            [pltpu.VMEM((HELD, PART, 2 * HD), bf)] * (2 * CHUNKS),
            pltpu.VMEM((2, CHUNKS, CAP, PART, 2 * HD), bf),
            pltpu.VMEM((2, CHUNKS // 2, CAP, PART, 2 * HD), bf),
            pltpu.VMEM((2, CHUNKS // 2, CAP, PART, 2 * HD), bf),
            dma((2, CHUNKS)),
            dma((2 + STEPS,)),
            dma((STEPS, KVH)), dma((STEPS, KVH)),
            dma((SHARDS,)), dma((SHARDS,)),
            dma((KVH,)), dma((KVH,)),
            dma((RING,)), dma((RING,)),
            dma((2, STEPS, KVH)), dma((2, STEPS, KVH)),
            dma((2, 5, CHUNKS)), dma((2, 5, CHUNKS)),
        ],
        compiler_params=pltpu.CompilerParams(
            collective_id=0, has_side_effects=True, vmem_limit_bytes=60 << 20
        ),
        name="spread",
    )(retrieval, kv, queries, new_kv, cosines, sines, w)


def attend_kernel(
    retrieval, places, lengths, cosines, sines, q_all, fresh_all, kv_all, out, lse,
    slots, keys, q, fresh, counts, sem, q_sem, fresh_sem,
):
    quarter = CTOK // QUARTERS
    held = R * quarter
    j = lax.rem(lax.axis_index("mp"), QUARTERS)
    z = lax.axis_index("store")

    def fetch(b, r, place=0):
        return pltpu.make_async_copy(
            kv_all.at[place], slots.at[b, pl.ds(r * quarter, quarter)], sem.at[b, r]
        )

    for s in range(STORES):
        counts[s] = 0

    def locate(b, r):
        found = retrieval[r, z * REQ + b]
        apart = ((found >> 4) - z) & (STORES - 1)
        rank = counts[apart]
        counts[apart] = rank + 1
        near = HELD * jnp.where(apart <= 2, 2 * apart, 2 * (STORES - apart) - 1) + (found & (HELD - 1))
        far = 5 * HELD + CAP * jnp.where(apart == 5, 0, jnp.where(apart == 3, 1, 2)) + rank
        return jnp.where((apart <= 2) | (apart >= 6), near, far)

    def fetch_q(b):
        return pltpu.make_async_copy(q_all.at[b], q.at[b], q_sem.at[b])

    fetch_fresh = pltpu.make_async_copy(fresh_all, fresh, fresh_sem)
    for b in range(REQ):
        for r in range(R):
            fetch(b, r, locate(b, r)).start()
        fetch_q(b).start()
        if b == 0:
            fetch_fresh.start()
    fetch_fresh.wait()
    for b in range(REQ):
        slots[b, held:, :] = fresh[...]
    keys[held:, :] = fresh[:, :HD]
    col = lax.broadcasted_iota(jnp.int32, (SUB, quarter), 1)
    fresh_token = TOKENS * (QUARTERS * (col >> 4) + j) + (col & 3)
    fresh_request = (col >> 2) & 3
    row = lax.broadcasted_iota(jnp.int32, (SUB, quarter), 0)
    for b in range(REQ):
        for r in range(R):
            fetch(b, r).wait()
        for r in range(R):
            at = places[b, r]
            key = slots[b, r * quarter : (r + 1) * quarter, :HD].astype(jnp.float32)
            key = rotate(key, cosines[pl.ds(at, 1), :], sines[pl.ds(at, 1), :])
            keys[r * quarter : (r + 1) * quarter, :] = key.astype(jnp.bfloat16)
        fetch_q(b).wait()
        length = lengths[b]

        def block(i, carry):
            spans = [pl.ds(pl.multiple_of(i * BLOCK + n * SUB, SUB), SUB) for n in range(BLOCK // SUB)]
            every = [
                lax.dot_general(
                    q[b, span, :], keys[...], (((1,), (1,)), ((), ())), preferred_element_type=jnp.float32
                )
                for span in spans
            ]
            for n, (span, scores) in enumerate(zip(spans, every)):
                at = i * BLOCK + n * SUB + row
                allowed = (fresh_request == b) & (fresh_token <= (at >> 3))
                scores = jnp.concatenate(
                    [scores[:, :held], jnp.where(allowed, scores[:, held:], -1e30)], axis=1
                )
                top = jnp.max(scores, axis=1, keepdims=True)
                expo = jnp.exp2(scores - top)
                total = jnp.sum(expo, axis=1, keepdims=True)
                sums = jnp.dot(
                    expo.astype(jnp.bfloat16), slots[b, :, HD:], preferred_element_type=jnp.float32
                )
                out[b, span, :] = jnp.where(at < length * GROUP, sums / total, 0.0).astype(jnp.bfloat16)
                logs = top + jnp.log(total) * LOG2E
                lse[b, :, span] = jnp.broadcast_to(logs, (SUB, HD)).T[:8]
            return carry

        def blank(i, carry):
            span = pl.ds(pl.multiple_of(i * BLOCK, BLOCK), BLOCK)
            out[b, span, :] = jnp.zeros((BLOCK, HD), jnp.bfloat16)
            lse[b, :, span] = jnp.zeros((8, BLOCK), jnp.float32)
            return carry

        used = (length * GROUP + BLOCK - 1) // BLOCK
        lax.fori_loop(0, used, block, 0)
        lax.fori_loop(used, ROWS // BLOCK, blank, 0)


def attend(retrieval, places, lengths, cosines, sines, q_all, fresh_all, kv_all):
    quarter = CTOK // QUARTERS
    bf = jnp.bfloat16
    dma = pltpu.SemaphoreType.DMA
    return pl.pallas_call(
        attend_kernel,
        out_shape=(
            jax.ShapeDtypeStruct((REQ, ROWS, HD), bf),
            jax.ShapeDtypeStruct((REQ, 8, ROWS), jnp.float32),
        ),
        in_specs=[SMEM] * 3 + [VMEM] * 2 + [HBM] * 3,
        out_specs=(VMEM, VMEM),
        scratch_shapes=[
            pltpu.VMEM((REQ, (R + 1) * quarter, 2 * HD), bf),
            pltpu.VMEM(((R + 1) * quarter, HD), bf),
            pltpu.VMEM((REQ, ROWS, HD), bf),
            pltpu.VMEM((quarter, 2 * HD), bf),
            pltpu.SMEM((STORES,), jnp.int32),
            dma((REQ, R)), dma((REQ,)), dma,
        ],
        compiler_params=pltpu.CompilerParams(vmem_limit_bytes=60 << 20),
        name="attend",
    )(retrieval, places, lengths, cosines, sines, q_all, fresh_all, kv_all)


def merge_kernel(
    part, lse, w_own, w_all, hidden, mixed,
    w, from_mate, from_mate_lse, pair, pair_lse, from_chip, from_chip_lse, rows, attended, sent, got,
    w_sem, own_sem, c_send, c_recv, l_send, l_recv, g_send, g_recv, p_send, p_recv,
):
    m = lax.axis_index("mp")
    k = m // QUARTERS
    j = lax.rem(m, QUARTERS)
    core, half = lax.rem(j, 2), j // 2
    mate, chip = m + 1 - 2 * core, QUARTERS * k + ahead(j, 2, QUARTERS)
    ring = RING * (m // RING)
    place = lax.rem(m, RING)
    w_loads = [
        pltpu.make_async_copy(
            w_own.at[:, pl.ds(pl.multiple_of(WIDTH * place, WIDTH), WIDTH)], w.at[place], w_sem.at[0]
        )
    ]
    for i in range(1, RING):
        come = ahead(place, i, RING)
        w_loads.append(pltpu.make_async_copy(w_all.at[come], w.at[come], w_sem.at[i]))
    for load in w_loads:
        load.start()

    barrier = pltpu.get_barrier_semaphore()

    def loop(low, high, act):
        def body(i, carry):
            act(i)
            return carry

        lax.fori_loop(low, high, body, 0)

    loop(
        1,
        SHARDS,
        lambda i: pl.semaphore_signal(
            barrier, 1, device_id={"mp": ahead(m, i, SHARDS)}, device_id_type=MESH
        ),
    )
    pl.semaphore_wait(barrier, SHARDS - 1)

    def remote(src, dst, send, recv, to):
        return pltpu.make_async_remote_copy(
            src_ref=src, dst_ref=dst, send_sem=send, recv_sem=recv, device_id={"mp": to}, device_id_type=MESH
        )

    def mate_copies(at, n):
        give = 1 - core + 2 * at
        span = pl.ds(n // 2 * HALF, HALF)
        return (
            remote(lse.at[give, :, span], from_mate_lse.at[at, :, span], l_send.at[n], l_recv.at[n], mate),
            remote(part.at[give, span], from_mate.at[at, span], c_send.at[n], c_recv.at[n], mate),
        )

    def chip_copies(n):
        span = pl.ds(n * HALF, HALF)
        return (
            remote(pair_lse.at[:, span], from_chip_lse.at[:, span], l_send.at[4 + n], l_recv.at[4 + n], chip),
            remote(pair.at[span], from_chip.at[span], c_send.at[4 + n], c_recv.at[4 + n], chip),
        )

    def combine(one, one_log, two, two_log):
        top = jnp.maximum(one_log, two_log)
        one_share, two_share = jnp.exp2(one_log - top), jnp.exp2(two_log - top)
        total = one_share + two_share
        share = jnp.broadcast_to(one_share / total, (HD, HALF)).T
        return two + (one - two) * share, top + jnp.log(total) * LOG2E

    def with_mate(at, n):
        span = slice(n * HALF, (n + 1) * HALF)
        keep = core + 2 * at
        return combine(
            part[keep, span].astype(jnp.float32), lse[keep, :1, span],
            from_mate[at, span].astype(jnp.float32), from_mate_lse[at, :1, span],
        )

    def g_copy(at, n, hf, to):
        block = attended.at[at, pl.ds(hf * (QMAX // 2), QMAX // 2)]
        return remote(block, block, g_send.at[hf, n], g_recv.at[hf, n], to)

    other = 1 - half
    order = ((other, 0), (half, 1))
    hops = (4, 2, 6)
    mate_place = place + 1 - 2 * core
    for hf in range(2):
        for at, n in order:
            for copy in mate_copies(at, 2 * hf + n):
                copy.start()
    for hf in range(2):
        for copy in mate_copies(other, 2 * hf):
            copy.wait_recv()
        value, logs = with_mate(other, hf)
        pair[hf * HALF : (hf + 1) * HALF, :] = value.astype(jnp.bfloat16)
        pair_lse[:, hf * HALF : (hf + 1) * HALF] = jnp.broadcast_to(logs, (8, HALF))
        for copy in chip_copies(hf):
            copy.start()
    kept = []
    for hf in range(2):
        for copy in mate_copies(half, 2 * hf + 1):
            copy.wait_recv()
        value, logs = with_mate(half, hf)
        rows[hf * HALF : (hf + 1) * HALF, :] = value
        kept.append(logs)
    for hf in range(2):
        span = slice(hf * HALF, (hf + 1) * HALF)
        for copy in chip_copies(hf):
            copy.wait_recv()
        rows[span, :] = combine(
            rows[span, :], kept[hf], from_chip[span].astype(jnp.float32), from_chip_lse[:1, span]
        )[0]
        for h in range(GROUP):
            attended[place, hf * (QMAX // 2) : (hf + 1) * (QMAX // 2), h * HD : (h + 1) * HD] = rows[
                pl.ds(hf * HALF + h, QMAX // 2, stride=GROUP), :
            ].astype(jnp.bfloat16)
        for n, hop in enumerate(hops):
            g_copy(place, 1 + n, hf, ring + ahead(place, hop, RING)).start()
        g_copy(place, 0, hf, mate).start()
    for load in w_loads:
        load.wait()
    for hf in range(2):
        for n, hop in enumerate(hops):
            come = ahead(place, RING - hop, RING)
            g_copy(come, 1 + n, hf, mate).wait_recv()
            g_copy(come, 4 + n, hf, mate).start()
    for hf in range(2):
        g_copy(mate_place, 0, hf, mate).wait_recv()
        for n, hop in enumerate(hops):
            g_copy(ahead(mate_place, RING - hop, RING), 4 + n, hf, mate).wait_recv()

    owned = OWNED
    span = REQ * QMAX // 4
    per = span // owned

    def p_copy(to):
        return remote(
            sent.at[pl.ds(pl.multiple_of(owned * to, owned), owned), :], got.at[m], p_send.at[to], p_recv.at[m], to
        )

    def p_own():
        return pltpu.make_async_copy(
            sent.at[pl.ds(pl.multiple_of(owned * m, owned), owned), :], got.at[m], own_sem
        )

    def p_arrival(come):
        return remote(
            sent.at[pl.ds(pl.multiple_of(owned * come, owned), owned), :], got.at[come], p_send.at[come], p_recv.at[come], come
        )

    def project(i):
        block = ahead(m // per, i + 2, 4)
        at = block * span + lax.broadcasted_iota(jnp.int32, (span, REQ * QMAX), 0)
        source = QMAX * ((at >> 2) & 3) + 4 * (at >> 4) + (at & 3)
        pick = (source == lax.broadcasted_iota(jnp.int32, (span, REQ * QMAX), 1)).astype(jnp.bfloat16)
        total = None
        for g in range(RING // REQ):
            chosen = jnp.dot(
                pick,
                attended[REQ * g : REQ * (g + 1)].reshape(REQ * QMAX, GROUP * HD),
                preferred_element_type=jnp.float32,
            ).astype(jnp.bfloat16)
            term = jnp.dot(
                chosen,
                w[REQ * g : REQ * (g + 1)].reshape(GROUP * HD, WIDTH),
                preferred_element_type=jnp.float32,
            )
            total = term if total is None else total + term
        sent[pl.ds(pl.multiple_of(block * span, span), span), :] = total.astype(jnp.bfloat16)

        def ship(t):
            to = block * per + ahead(m, t, per)

            @pl.when(to != m)
            def _():
                p_copy(to).start()

            @pl.when(to == m)
            def _():
                p_own().start()

        loop(0, per, ship)

    loop(0, 4, project)
    p_own().wait()
    loop(1, SHARDS, lambda i: p_arrival(ahead(m, i, SHARDS)).wait_recv())

    for c in range(RING):
        cols = slice(c * WIDTH, (c + 1) * WIDTH)
        value = got[c].astype(jnp.float32)
        for group in range(1, SHARDS // RING):
            value = value + got[RING * group + c].astype(jnp.float32)
        for b in range(REQ):
            mixed[b, :, cols] = value[b * TOKENS : (b + 1) * TOKENS] + hidden[b, :, cols].astype(jnp.float32)

    for hf in range(2):
        for at, n in order:
            for copy in mate_copies(at, 2 * hf + n):
                copy.wait_send()
        for copy in chip_copies(hf):
            copy.wait_send()
        g_copy(place, 0, hf, mate).wait_send()
        for n, hop in enumerate(hops):
            g_copy(place, 1 + n, hf, mate).wait_send()
            g_copy(ahead(place, RING - hop, RING), 4 + n, hf, mate).wait_send()
    loop(1, SHARDS, lambda i: p_copy(ahead(m, i, SHARDS)).wait_send())


def merge(part, lse, w_own, w_all, hidden):
    bf, f32 = jnp.bfloat16, jnp.float32
    dma = pltpu.SemaphoreType.DMA
    owned = OWNED
    return pl.pallas_call(
        merge_kernel,
        out_shape=jax.ShapeDtypeStruct((REQ, TOKENS, D), f32),
        in_specs=[VMEM, VMEM, HBM, HBM, VMEM],
        out_specs=VMEM,
        scratch_shapes=[
            pltpu.VMEM((RING, D // SHARDS, WIDTH), bf),
            pltpu.VMEM((2, ROWS, HD), bf),
            pltpu.VMEM((2, 8, ROWS), f32),
            pltpu.VMEM((ROWS, HD), bf),
            pltpu.VMEM((8, ROWS), f32),
            pltpu.VMEM((ROWS, HD), bf),
            pltpu.VMEM((8, ROWS), f32),
            pltpu.VMEM((ROWS, HD), f32),
            pltpu.VMEM((RING, QMAX, GROUP * HD), bf),
            pltpu.VMEM((REQ * QMAX, WIDTH), bf),
            pltpu.VMEM((SHARDS, owned, WIDTH), bf),
            dma((RING,)), dma,
            dma((6,)), dma((6,)),
            dma((6,)), dma((6,)),
            dma((2, 7)), dma((2, 7)),
            dma((SHARDS,)), dma((SHARDS,)),
        ],
        compiler_params=pltpu.CompilerParams(
            collective_id=1, has_side_effects=True, vmem_limit_bytes=52 << 20
        ),
        name="merge",
    )(part, lse, w_own, w_all, hidden)


def on_device(
    kv_store, retrieval, positions, lengths, queries, new_kv, hidden, out_weight, norm_gain
):
    context = R * CTOK
    cos_own, sin_own = turns(np.arange(context, context + QMAX))
    shape = (SHARDS, TOKENS, HD)
    wanted = jnp.transpose(retrieval)
    kv_all, q_all, fresh_all, w_all = spread(
        wanted, kv_store, queries, new_kv, cos_own.reshape(shape), sin_own.reshape(shape), out_weight
    )
    cos_at, sin_at = turns(np.arange(R) * CTOK)
    part, lse = attend(
        wanted, positions, lengths, cos_at, sin_at, q_all.reshape(REQ, ROWS, HD),
        fresh_all.reshape(KVH * 16, 2 * HD),
        kv_all,
    )
    mixed = merge(part, lse, out_weight, w_all, hidden)
    square = jnp.mean(mixed * mixed, axis=-1, keepdims=True)
    normed = mixed * lax.rsqrt(square + eps_norm) * norm_gain.astype(jnp.float32)
    return mixed.astype(jnp.bfloat16), normed.astype(jnp.bfloat16)


def solution(mesh):
    return jax.shard_map(
        on_device,
        mesh=mesh,
        in_specs=(
            P("store", "mp", None),
            P(),
            P("store", None),
            P("store"),
            P("store", "mp", None),
            P("store", "mp", None),
            P("store", "mp", None),
            P("mp", None),
            P(),
        ),
        out_specs=(P("store", "mp", None), P("store", "mp", None)),
        check_vma=False,
    )
```
